512 devices in a mesh: dp: 16 (over y, core), section: 8 (over z), tensor: 4 (over x).
Axes of the slice: x: 4, y: 8, z: 8, core: 2. Of those that a mesh axis runs over, the one named last changes fastest.
Arguments:
- sent_queries: bfloat16 [8, 32, 128, 2048], P('section', 'dp', None, 'tensor'), may hold values from -96 to 96
- mem_keys: bfloat16 [8, 128, 64, 2048], P('section', 'dp', None, 'tensor'), may hold values from -4 to 4
- mem_values: bfloat16 [8, 128, 64, 2048], P('section', 'dp', None, 'tensor'), may hold values from -24 to 24
- out_weight: bfloat16 [8, 2048, 4096], P('section', 'tensor', 'dp'), may hold values from -0.5 to 0.5
- sent_grads: bfloat16 [8, 32, 128, 4096], P('section', 'dp', None, 'tensor'), may hold values from -24 to 24
- counts: int32 [32], P('dp'), may hold values from 1 to 4, 80 in all
- neg_ids: int32 [32, 4], P('dp'), may hold values from 0 to 127, as said below
Outputs:
- mixed: bfloat16 [8, 32, 128, 4096], P('section', 'dp', None, 'tensor')
- query_grads: bfloat16 [8, 32, 128, 2048], P('section', 'dp', None, 'tensor')
- key_grads: bfloat16 [8, 128, 64, 2048], P('section', 'dp', None, 'tensor')
- value_grads: bfloat16 [8, 128, 64, 2048], P('section', 'dp', None, 'tensor')
The draws below stay inside these ranges and needn't reach their ends.
Inputs may be any that keep to these rules, and one draw needn't show every extreme that they name: `neg_ids`: an id names a memory block, blocks numbered replica by replica with 8 to a replica (replica r holds documents r * 2 .. (r + 1) * 2 - 1); every entry names a block of another replica than its document's; the entries of one replica's documents name at most 1 entries held by any one other replica, and exactly 1 for some other replica; two entries may name the same block.
All inputs are finite; a program needn't handle non-finite values. No bound on the sum of `counts` on one device may be relied on, other than what follows from the above.
Results may differ from the reference program's by a relative error of at most 0.04.
Values may be sent and summed in bfloat16 or wider, within the bound.
No kernel may reach another device: no remote copies, remote signals or barrier semaphores. Data moves between devices by JAX's collectives and lax.ppermute only.
A program may use at most 64 MiB of HBM per device.

```python
import math
import jax
import jax.numpy as jnp
import numpy as np
from jax import lax

D = 4096
HEADS = 16
HD = 128
QROWS = 128
DOCS_DEV = 2
BLOCK = 64
OWN = 4
NEG = 4
LAYERS = 8
DOCS = 32
MEM_DEV = 8
BLOCKS = 128
KEYS = 512
CAP = 1
N_DP = 16
N_TENSOR = 4


def draw_mem_keys(key, part):
    key = jax.random.fold_in(key, 3)
    draw_shape = (LAYERS, BLOCKS, BLOCK, HEADS * HD)
    base_draw = jnp.clip(jax.random.normal(key, draw_shape, jnp.float32), -4.0, 4.0)
    return base_draw.astype(jnp.bfloat16)


def draw_sent_queries(key, part):
    key = jax.random.fold_in(key, 5)
    draw_shape = (LAYERS, DOCS, QROWS, HEADS * HD)
    base_draw = jnp.clip(jax.random.normal(key, draw_shape, jnp.float32), -4.0, 4.0)
    return base_draw.astype(jnp.bfloat16)


def draw_neg_ids(key, part):
    key = jax.random.fold_in(key, 11)
    slot_total = (N_DP - 1) * CAP
    entries = DOCS_DEV * NEG

    def per_replica(replica):
        replica_key = jax.random.fold_in(key, replica)
        key_order, key_spot = jax.random.split(replica_key)
        chosen = jax.random.permutation(key_order, slot_total)[:entries]
        holder = (replica + 1 + chosen // CAP) % N_DP
        block_spot = jax.random.randint(key_spot, (entries,), 0, MEM_DEV)
        return (holder * MEM_DEV + block_spot).reshape(DOCS_DEV, NEG)
    replicas = jnp.arange(N_DP, dtype=jnp.int32)
    return jax.vmap(per_replica)(replicas).reshape(DOCS, NEG).astype(jnp.int32)


def block_levels(own_key, dims, cuts, smallest, high):
    gain = 1.0
    for dim, parts in cuts:
        steps = jax.random.uniform(jax.random.fold_in(jax.random.fold_in(own_key, 6), dim), (parts,), jnp.float32, smallest / len(cuts), high / len(cuts))
        gain = gain * jnp.repeat(jnp.exp(steps), dims[dim] // parts).reshape((-1,) + (1,) * (len(dims) - 1 - dim))
    return gain


def length_profile(amount, total, reach, skew):
    portions = [(1 << 20) // math.isqrt(rank ** skew) + 1 for rank in range(2, amount + 1)]
    surplus, holding = total - reach - (amount - 1), [1] * (amount - 1)
    while surplus > 0:
        movable = [i for i in range(amount - 1) if holding[i] < reach]
        pool, left = sum([portions[i] for i in movable]), surplus
        for i in movable:
            extra = min(reach - holding[i], max(1, left * portions[i] // pool), surplus)
            holding[i] = holding[i] + extra
            surplus = surplus - extra
    return np.array([reach] + holding)


def uneven_parts(own_key, amount, total, most, lean):
    if amount == 2:
        one = jax.random.randint(own_key, (), max(1, total - most), min(most, total - 1) + 1)
        return jnp.stack([one, total - one])
    sizes = jnp.asarray(length_profile(amount, total, most, lean), jnp.int32)
    twos = (amount - 1) // 2
    source_of, taker = sizes[1:1 + 2 * twos:2], sizes[2:2 + 2 * twos:2]
    slack = jnp.minimum(source_of - 1, most - taker)
    moved = jax.random.randint(jax.random.fold_in(own_key, 1), (twos,), 0, 1 << 20) % (slack + 1)
    sizes = sizes.at[1:1 + 2 * twos:2].set(source_of - moved).at[2:2 + 2 * twos:2].set(taker + moved)
    return sizes[jax.random.permutation(jax.random.fold_in(own_key, 2), amount)]


def noise(key, shape, scale, bound, cuts=(), held_as=jnp.bfloat16):
    values = scale * jax.random.normal(key, shape, jnp.float32)
    if cuts:
        values = values * block_levels(key, shape, cuts, -0.22, 0.18)
    return jnp.clip(values, -bound, bound).astype(held_as)


def setup_inputs(seed: int = 0) -> dict:
    arg_keys = jax.random.split(jax.random.key(seed), 8)
    return {
        "sent_queries": draw_sent_queries(jax.random.fold_in(arg_keys[7], 71), 0),
        "mem_keys": draw_mem_keys(jax.random.fold_in(arg_keys[7], 71), 0),
        "mem_values": noise(arg_keys[2], (LAYERS, BLOCKS, BLOCK, HEADS * HD), 4.0, 24.0, ((0, 8), (1, 16), (3, 4))),
        "out_weight": noise(arg_keys[3], (LAYERS, HEADS * HD, D), (HEADS * HD // 16) ** -0.5, 0.5, ((0, 8), (1, 4), (2, 16))),
        "sent_grads": noise(arg_keys[4], (LAYERS, DOCS, QROWS, D), 4.0, 24.0, ((0, 8), (1, 16), (3, 4))),
        "counts": uneven_parts(arg_keys[5], DOCS, DOCS * (OWN + 1) // 2, OWN, 0).astype(jnp.int32),
        "neg_ids": draw_neg_ids(jax.random.fold_in(arg_keys[7], 71), 0),
    }


def rounded(values):
    return lax.optimization_barrier(values.astype(jnp.bfloat16)).astype(jnp.float32)


def attend_document(query_rows, key_rows, value_rows, valid_keys, grad_rows, weight):
    scale_value = HD ** -0.5
    query_heads = query_rows.astype(jnp.float32).reshape(QROWS, HEADS, HD)
    key_heads = key_rows.astype(jnp.float32).reshape(KEYS, HEADS, HD)
    value_heads = value_rows.astype(jnp.float32).reshape(KEYS, HEADS, HD)
    scores = jnp.einsum("qhe,khe->hqk", query_heads, key_heads) * scale_value
    scores = jnp.where(valid_keys[None, None, :], scores, -jnp.inf)
    row_max = jnp.max(scores, axis=-1, keepdims=True)
    expo_terms = jnp.exp(scores - row_max)
    probabilities = expo_terms / jnp.sum(expo_terms, axis=-1, keepdims=True)
    prob_round = rounded(probabilities)
    attended = rounded(jnp.einsum("hqk,khe->qhe", prob_round, value_heads))
    group_width = HEADS * HD // N_TENSOR
    weight_full = weight.astype(jnp.float32).reshape(N_TENSOR, group_width, D)
    group_terms = jnp.einsum("qgf,gfd->gqd", attended.reshape(QROWS, N_TENSOR, group_width), weight_full)
    mixed = jnp.sum(rounded(group_terms), axis=0).astype(jnp.bfloat16)
    grad_attended = rounded(jnp.dot(grad_rows, weight.T, preferred_element_type=jnp.float32)).reshape(QROWS, HEADS, HD)
    row_delta = jnp.einsum("qhe,qhe->hq", grad_attended, attended)
    grad_values = jnp.einsum("hqk,qhe->khe", prob_round, grad_attended)
    grad_probs = jnp.einsum("qhe,khe->hqk", grad_attended, value_heads)
    grad_scores = rounded(probabilities * (grad_probs - row_delta[:, :, None]))
    grad_query = (jnp.einsum("hqk,khe->qhe", grad_scores, key_heads) * scale_value).reshape(QROWS, HEADS * HD).astype(jnp.bfloat16)
    grad_keys = (jnp.einsum("hqk,qhe->khe", grad_scores, query_heads) * scale_value).reshape(KEYS, HEADS * HD)
    return mixed, grad_query, grad_keys, grad_values.reshape(KEYS, HEADS * HD)


def collect_blocks(grad_rows, neg_ids):
    blocked = grad_rows.reshape(DOCS, OWN + NEG, BLOCK, HEADS * HD)
    own_part = blocked[:, :OWN].reshape(BLOCKS, BLOCK, HEADS * HD)
    neg_part = rounded(blocked[:, OWN:]).reshape(DOCS * NEG, BLOCK, HEADS * HD)
    return own_part.at[neg_ids.reshape(-1)].add(neg_part).astype(jnp.bfloat16)


def reference(sent_queries, mem_keys, mem_values, out_weight, sent_grads, counts, neg_ids):
    queries = jnp.roll(sent_queries, 1, axis=0)
    grads = jnp.roll(sent_grads, -1, axis=0)
    own_ids = jnp.arange(DOCS, dtype=jnp.int32)[:, None] * OWN + jnp.arange(OWN, dtype=jnp.int32)[None, :]
    list_ids = jnp.concatenate([own_ids, neg_ids.astype(jnp.int32)], axis=1)
    position = jnp.arange(KEYS, dtype=jnp.int32)
    valid = (position[None, :] < counts[:, None] * BLOCK) | (position[None, :] >= OWN * BLOCK)
    mixed_list, query_list, key_list, value_list = [], [], [], []
    for layer_index in range(LAYERS):
        layer_keys = mem_keys[layer_index]
        layer_values = mem_values[layer_index]
        layer_queries = queries[layer_index]
        layer_grads = grads[layer_index]
        weight = out_weight[layer_index]

        def per_document(document):
            chosen = list_ids[document]
            key_rows = jnp.take(layer_keys, chosen, axis=0).reshape(KEYS, HEADS * HD)
            value_rows = jnp.take(layer_values, chosen, axis=0).reshape(KEYS, HEADS * HD)
            return attend_document(layer_queries[document], key_rows, value_rows, valid[document], layer_grads[document], weight)

        mixed, grad_query, grad_keys, grad_values = lax.map(per_document, jnp.arange(DOCS, dtype=jnp.int32))
        mixed_list.append(mixed)
        query_list.append(grad_query)
        key_list.append(collect_blocks(grad_keys, neg_ids))
        value_list.append(collect_blocks(grad_values, neg_ids))
    return (jnp.stack(mixed_list), jnp.stack(query_list), jnp.stack(key_list), jnp.stack(value_list))
```

```python
import functools

import jax
import jax.numpy as jnp
from jax import lax
from jax.experimental import pallas as pl
from jax.experimental.pallas import tpu as pltpu
from jax.sharding import PartitionSpec as P

HD = 128
PARTS = 2
F32 = jnp.float32
BF16 = jnp.bfloat16
NT = (((1,), (1,)), ((), ()))
TN = (((0,), (0,)), ((), ()))
VMEM = pl.BlockSpec(memory_space=pltpu.VMEM)
SMEM = pl.BlockSpec(memory_space=pltpu.SMEM)
PARAMS = pltpu.CompilerParams(vmem_limit_bytes=40 * 1024 * 1024)


def passed_along(block, axis, distance):
    count = lax.axis_size(axis)
    return lax.ppermute(block, axis, [(i, (i + distance) % count) for i in range(count)])


def exchanged(slots):
    return lax.all_to_all(slots, "dp", split_axis=0, concat_axis=0, tiled=True)


def cost(flops, nbytes):
    return pl.CostEstimate(flops=int(flops), bytes_accessed=int(nbytes), transcendentals=0)


def pick_kernel(asked, keys, values, *slots):
    rows = keys.shape[1]
    wide = slots[0].shape[2]
    for slot in range(slots[0].shape[0]):
        spot = jnp.maximum(asked[slot], 0)
        for part, out in enumerate(slots):
            lanes = slice(part * wide, (part + 1) * wide)
            out[slot, :rows, :] = keys[spot, :, lanes]
            out[slot, rows:, :] = values[spot, :, lanes]


def picked_slots(asked, keys, values):
    slot_count = asked.shape[0]
    _, rows, features = keys.shape
    shape = jax.ShapeDtypeStruct((slot_count, 2 * rows, features // PARTS), BF16)
    return pl.pallas_call(
        pick_kernel,
        out_shape=[shape] * PARTS,
        in_specs=[SMEM, VMEM, VMEM],
        out_specs=[VMEM] * PARTS,
        compiler_params=PARAMS,
        cost_estimate=cost(0, 3 * 2**20),
        name="pick_blocks",
    )(asked, keys, values)


def attend_kernel(part, counts, holder, queries, keys, values, recv, grads, attended, grad_query, own_keys, own_values, slots):
    docs, _, _ = queries.shape
    mem_count, rows, _ = keys.shape
    own = mem_count // docs
    neg = holder.shape[0] // docs
    wide = recv.shape[2]
    scale = HD**-0.5
    total = (own + neg) * rows
    position = lax.broadcasted_iota(jnp.int32, (total, 1), 0)
    for doc in range(docs):
        valid = (position < counts[doc] * rows) | (position >= own * rows)
        for head in range(wide // HD):
            at = slice(head * HD, (head + 1) * HD)
            lanes = slice(part * wide + head * HD, part * wide + (head + 1) * HD)
            query = queries[doc, :, lanes]
            grad = grads[doc, :, lanes]
            key_rows = [keys[doc * own + m, :, lanes] for m in range(own)]
            value_rows = [values[doc * own + m, :, lanes] for m in range(own)]
            for m in range(neg):
                slot = holder[doc * neg + m]
                key_rows.append(recv[slot, :rows, at])
                value_rows.append(recv[slot, rows:, at])
            key = jnp.concatenate(key_rows, axis=0)
            value = jnp.concatenate(value_rows, axis=0)
            scores = lax.dot_general(key, query, NT, preferred_element_type=F32) * scale
            scores = jnp.where(valid, scores, -jnp.inf)
            expo = jnp.exp(scores - jnp.max(scores, axis=0, keepdims=True))
            prob = expo / jnp.sum(expo, axis=0, keepdims=True)
            prob_round = prob.astype(BF16)
            attended[doc, :, at] = lax.dot_general(prob_round, value, TN, preferred_element_type=F32).astype(BF16)
            grad_prob = lax.dot_general(value, grad, NT, preferred_element_type=F32)
            delta = jnp.sum(prob * grad_prob, axis=0, keepdims=True)
            grad_score = (prob * (grad_prob - delta)).astype(BF16)
            grad_query[doc, :, at] = (
                lax.dot_general(grad_score, key, TN, preferred_element_type=F32) * scale
            ).astype(BF16)
            grad_key = jnp.dot(grad_score, query, preferred_element_type=F32) * scale
            grad_value = jnp.dot(prob_round, grad, preferred_element_type=F32)
            for m in range(own):
                here = slice(m * rows, (m + 1) * rows)
                own_keys[doc * own + m, :, at] = grad_key[here]
                own_values[doc * own + m, :, at] = grad_value[here]
            for m in range(neg):
                here = slice((own + m) * rows, (own + m + 1) * rows)
                slot = holder[doc * neg + m]
                slots[slot, :rows, at] = grad_key[here].astype(BF16)
                slots[slot, rows:, at] = grad_value[here].astype(BF16)


def attend_part(part, counts, holder, queries, keys, values, recv, grads):
    docs, query_count, _ = queries.shape
    mem_count, rows, _ = keys.shape
    wide = recv.shape[2]
    query_shape = jax.ShapeDtypeStruct((docs, query_count, wide), BF16)
    own_shape = jax.ShapeDtypeStruct((mem_count, rows, wide), F32)
    return pl.pallas_call(
        functools.partial(attend_kernel, part),
        out_shape=[query_shape, query_shape, own_shape, own_shape, jax.ShapeDtypeStruct(recv.shape, BF16)],
        in_specs=[SMEM, SMEM] + [VMEM] * 5,
        out_specs=[VMEM] * 5,
        compiler_params=PARAMS,
        cost_estimate=cost(4 * 2**30, 8 * 2**20),
        name=f"attend_part{part}",
    )(counts, holder, queries, keys, values, recv, grads)


def back_kernel(spot, weight, grad0, grad1, grad2, grad3, out):
    block = weight.shape[2]
    held = (grad0, grad1, grad2, grad3)
    per = weight.shape[0] // len(held)
    total = None
    for j, grad in enumerate(held):
        first = lax.rem(spot[0] + j, len(held)) * per
        for c in range(per):
            term = lax.dot_general(
                grad[:, c * block : (c + 1) * block], weight[first + c], NT, preferred_element_type=F32
            )
            total = term if total is None else total + term
    out[...] = total.astype(BF16)


def back_projected(weight, held):
    rows = held[0].shape[0]
    return pl.pallas_call(
        back_kernel,
        out_shape=jax.ShapeDtypeStruct((rows, weight.shape[1]), BF16),
        in_specs=[SMEM] + [VMEM] * (1 + len(held)),
        out_specs=VMEM,
        compiler_params=PARAMS,
        cost_estimate=cost(2 * 2**30, 8 * 2**20),
        name="back_projection",
    )(lax.axis_index("tensor").astype(jnp.int32).reshape(1), weight, *held)


def project_kernel(weight, *refs):
    *parts, out = refs
    block = weight.shape[2]
    per = weight.shape[0] // out.shape[0]
    wide = parts[0].shape[1]
    for b in range(weight.shape[0]):
        total = None
        for p, part in enumerate(parts):
            term = jnp.dot(part[...], weight[b, p * wide : (p + 1) * wide, :], preferred_element_type=F32)
            total = term if total is None else total + term
        out[b // per, :, (b % per) * block : (b % per + 1) * block] = total.astype(BF16)


def projected(weight, parts, groups):
    columns = weight.shape[0] * weight.shape[2] // groups
    return pl.pallas_call(
        project_kernel,
        out_shape=jax.ShapeDtypeStruct((groups, parts[0].shape[0], columns), BF16),
        in_specs=[VMEM] * (1 + len(parts)),
        out_specs=VMEM,
        compiler_params=PARAMS,
        cost_estimate=cost(2 * 2**30, 8 * 2**20),
        name="projection",
    )(weight, *parts)


def combine_kernel(part, asked, own_keys, own_values, back, *refs):
    key_grads, value_grads, key_total, value_total = refs[-4:]
    rows = own_keys.shape[1]
    key_total[...] = own_keys[...]
    value_total[...] = own_values[...]
    for slot in range(back.shape[0]):
        spot = asked[slot]

        @pl.when(spot >= 0)
        def _(slot=slot, spot=spot):
            key_total[spot] += back[slot, :rows, :].astype(F32)
            value_total[spot] += back[slot, rows:, :].astype(F32)

    key_grads[...] = key_total[...].astype(BF16)
    value_grads[...] = value_total[...].astype(BF16)


def combined(part, asked, own_keys, own_values, back, earlier):
    mem_count, rows, wide = own_keys.shape
    shape = jax.ShapeDtypeStruct((mem_count, rows, wide * PARTS), BF16)
    block = pl.BlockSpec((mem_count, rows, wide), lambda i: (0, 0, part))
    return pl.pallas_call(
        functools.partial(combine_kernel, part),
        grid=(1,),
        out_shape=[shape, shape],
        in_specs=[SMEM, VMEM, VMEM, VMEM] + [pl.BlockSpec(memory_space=pl.ANY)] * len(earlier),
        out_specs=[block, block],
        scratch_shapes=[pltpu.VMEM(own_keys.shape, F32)] * 2,
        input_output_aliases={4 + i: i for i in range(len(earlier))},
        compiler_params=PARAMS,
        cost_estimate=cost(0, 4 * 2**20),
        name=f"combine_part{part}",
    )(asked, own_keys, own_values, back, *earlier)


def on_device(sent_queries, mem_keys, mem_values, out_weight, sent_grads, counts, neg_ids):
    keys, values = mem_keys[0], mem_values[0]
    mem_count = keys.shape[0]
    groups = lax.axis_size("dp")
    tensor = lax.axis_size("tensor")

    flat_ids = neg_ids.reshape(-1)
    holder = flat_ids // mem_count
    spot = flat_ids - holder * mem_count
    named = holder[None, :] == jnp.arange(groups, dtype=jnp.int32)[:, None]
    request = jnp.sum(jnp.where(named, spot[None, :] + 1, 0), axis=1) - 1
    asked = exchanged(request.reshape(groups, 1)).reshape(groups)

    queries = passed_along(sent_queries, "section", 1)[0]
    grads = passed_along(sent_grads, "section", -1)[0]
    docs, query_count, features = queries.shape
    weight = lax.all_gather(out_weight[0], "dp")

    recv = [exchanged(part) for part in picked_slots(asked, keys, values)]

    grad_rows = grads.reshape(docs * query_count, grads.shape[2])
    held = [grad_rows] + [passed_along(grad_rows, "tensor", -j) for j in range(1, tensor)]
    grad_attended = back_projected(weight, held).reshape(docs, query_count, features)

    attended, query_grads, own, back = [], [], [], []
    for part in range(PARTS):
        out, grad_query, own_keys, own_values, slots = attend_part(
            part, counts, holder, queries, keys, values, recv[part], grad_attended
        )
        attended.append(out.reshape(docs * query_count, -1))
        query_grads.append(grad_query)
        own.append((own_keys, own_values))
        back.append(exchanged(slots))

    mixed = lax.psum_scatter(projected(weight, attended, tensor), "tensor", scatter_dimension=0)
    mixed = mixed.reshape(1, docs, query_count, -1)

    grads_out = []
    for part in range(PARTS):
        grads_out = combined(part, asked, *own[part], back[part], grads_out)
    key_grads, value_grads = grads_out
    return mixed, jnp.concatenate(query_grads, axis=-1)[None], key_grads[None], value_grads[None]


def solution(mesh):
    rows = P("section", "dp", None, "tensor")
    return jax.shard_map(
        on_device,
        mesh=mesh,
        in_specs=(rows, rows, rows, P("section", "tensor", "dp"), rows, P("dp"), P("dp", None)),
        out_specs=(rows, rows, rows, rows),
        check_vma=False,
    )
```

```python
import functools

import jax
import jax.numpy as jnp
from jax import lax
from jax.experimental import pallas as pl
from jax.experimental.pallas import tpu as pltpu
from jax.sharding import PartitionSpec as P

HD = 128
PARTS = 1
F32 = jnp.float32
BF16 = jnp.bfloat16
NT = (((1,), (1,)), ((), ()))
TN = (((0,), (0,)), ((), ()))
VMEM = pl.BlockSpec(memory_space=pltpu.VMEM)
SMEM = pl.BlockSpec(memory_space=pltpu.SMEM)
PARAMS = pltpu.CompilerParams(vmem_limit_bytes=40 * 1024 * 1024)


def passed_along(block, axis, distance):
    count = lax.axis_size(axis)
    return lax.ppermute(block, axis, [(i, (i + distance) % count) for i in range(count)])


def exchanged(slots):
    return lax.all_to_all(slots, "dp", split_axis=0, concat_axis=0, tiled=True)


def cost(flops, nbytes):
    return pl.CostEstimate(flops=int(flops), bytes_accessed=int(nbytes), transcendentals=0)


def pick_kernel(asked, keys, values, *slots):
    rows = keys.shape[1]
    wide = slots[0].shape[2]
    for slot in range(slots[0].shape[0]):
        spot = jnp.maximum(asked[slot], 0)
        for part, out in enumerate(slots):
            lanes = slice(part * wide, (part + 1) * wide)
            out[slot, :rows, :] = keys[spot, :, lanes]
            out[slot, rows:, :] = values[spot, :, lanes]


def picked_slots(asked, keys, values):
    slot_count = asked.shape[0]
    _, rows, features = keys.shape
    shape = jax.ShapeDtypeStruct((slot_count, 2 * rows, features // PARTS), BF16)
    return pl.pallas_call(
        pick_kernel,
        out_shape=[shape] * PARTS,
        in_specs=[SMEM, VMEM, VMEM],
        out_specs=[VMEM] * PARTS,
        compiler_params=PARAMS,
        cost_estimate=cost(0, 3 * 2**20),
        name="pick_blocks",
    )(asked, keys, values)


def attend_kernel(part, counts, holder, queries, keys, values, recv, grads, attended, grad_query, own_keys, own_values, slots):
    docs, _, _ = queries.shape
    mem_count, rows, _ = keys.shape
    own = mem_count // docs
    neg = holder.shape[0] // docs
    wide = recv.shape[2]
    scale = HD**-0.5
    total = (own + neg) * rows
    position = lax.broadcasted_iota(jnp.int32, (total, 1), 0)
    for doc in range(docs):
        valid = (position < counts[doc] * rows) | (position >= own * rows)
        for head in range(wide // HD):
            at = slice(head * HD, (head + 1) * HD)
            lanes = slice(part * wide + head * HD, part * wide + (head + 1) * HD)
            query = queries[doc, :, lanes]
            grad = grads[doc, :, lanes]
            key_rows = [keys[doc * own + m, :, lanes] for m in range(own)]
            value_rows = [values[doc * own + m, :, lanes] for m in range(own)]
            for m in range(neg):
                slot = holder[doc * neg + m]
                key_rows.append(recv[slot, :rows, at])
                value_rows.append(recv[slot, rows:, at])
            key = jnp.concatenate(key_rows, axis=0)
            value = jnp.concatenate(value_rows, axis=0)
            scores = lax.dot_general(key, query, NT, preferred_element_type=F32) * scale
            scores = jnp.where(valid, scores, -jnp.inf)
            expo = jnp.exp(scores - jnp.max(scores, axis=0, keepdims=True))
            prob = expo / jnp.sum(expo, axis=0, keepdims=True)
            prob_round = prob.astype(BF16)
            attended[doc, :, at] = lax.dot_general(prob_round, value, TN, preferred_element_type=F32).astype(BF16)
            grad_prob = lax.dot_general(value, grad, NT, preferred_element_type=F32)
            delta = jnp.sum(prob * grad_prob, axis=0, keepdims=True)
            grad_score = (prob * (grad_prob - delta)).astype(BF16)
            grad_query[doc, :, at] = (
                lax.dot_general(grad_score, key, TN, preferred_element_type=F32) * scale
            ).astype(BF16)
            grad_key = jnp.dot(grad_score, query, preferred_element_type=F32) * scale
            grad_value = jnp.dot(prob_round, grad, preferred_element_type=F32)
            for m in range(own):
                here = slice(m * rows, (m + 1) * rows)
                own_keys[doc * own + m, :, at] = grad_key[here]
                own_values[doc * own + m, :, at] = grad_value[here]
            for m in range(neg):
                here = slice((own + m) * rows, (own + m + 1) * rows)
                slot = holder[doc * neg + m]
                slots[slot, :rows, at] = grad_key[here].astype(BF16)
                slots[slot, rows:, at] = grad_value[here].astype(BF16)


def attend_part(part, counts, holder, queries, keys, values, recv, grads):
    docs, query_count, _ = queries.shape
    mem_count, rows, _ = keys.shape
    wide = recv.shape[2]
    query_shape = jax.ShapeDtypeStruct((docs, query_count, wide), BF16)
    own_shape = jax.ShapeDtypeStruct((mem_count, rows, wide), F32)
    return pl.pallas_call(
        functools.partial(attend_kernel, part),
        out_shape=[query_shape, query_shape, own_shape, own_shape, jax.ShapeDtypeStruct(recv.shape, BF16)],
        in_specs=[SMEM, SMEM] + [VMEM] * 5,
        out_specs=[VMEM] * 5,
        compiler_params=PARAMS,
        cost_estimate=cost(4 * 2**30, 8 * 2**20),
        name=f"attend_part{part}",
    )(counts, holder, queries, keys, values, recv, grads)


def back_kernel(spot, weight, grad0, grad1, grad2, grad3, out):
    block = weight.shape[2]
    held = (grad0, grad1, grad2, grad3)
    per = weight.shape[0] // len(held)
    total = None
    for j, grad in enumerate(held):
        first = lax.rem(spot[0] + j, len(held)) * per
        for c in range(per):
            term = lax.dot_general(
                grad[:, c * block : (c + 1) * block], weight[first + c], NT, preferred_element_type=F32
            )
            total = term if total is None else total + term
    out[...] = total.astype(BF16)


def back_projected(weight, held):
    rows = held[0].shape[0]
    return pl.pallas_call(
        back_kernel,
        out_shape=jax.ShapeDtypeStruct((rows, weight.shape[1]), BF16),
        in_specs=[SMEM] + [VMEM] * (1 + len(held)),
        out_specs=VMEM,
        compiler_params=PARAMS,
        cost_estimate=cost(2 * 2**30, 8 * 2**20),
        name="back_projection",
    )(lax.axis_index("tensor").astype(jnp.int32).reshape(1), weight, *held)


def project_kernel(weight, *refs):
    *parts, out = refs
    block = weight.shape[2]
    per = weight.shape[0] // out.shape[0]
    wide = parts[0].shape[1]
    for b in range(weight.shape[0]):
        total = None
        for p, part in enumerate(parts):
            term = jnp.dot(part[...], weight[b, p * wide : (p + 1) * wide, :], preferred_element_type=F32)
            total = term if total is None else total + term
        out[b // per, :, (b % per) * block : (b % per + 1) * block] = total.astype(BF16)


def projected(weight, parts, groups):
    columns = weight.shape[0] * weight.shape[2] // groups
    return pl.pallas_call(
        project_kernel,
        out_shape=jax.ShapeDtypeStruct((groups, parts[0].shape[0], columns), BF16),
        in_specs=[VMEM] * (1 + len(parts)),
        out_specs=VMEM,
        compiler_params=PARAMS,
        cost_estimate=cost(2 * 2**30, 8 * 2**20),
        name="projection",
    )(weight, *parts)


def combine_kernel(part, asked, own_keys, own_values, back, *refs):
    key_grads, value_grads, key_total, value_total = refs[-4:]
    rows = own_keys.shape[1]
    key_total[...] = own_keys[...]
    value_total[...] = own_values[...]
    for slot in range(back.shape[0]):
        spot = asked[slot]

        @pl.when(spot >= 0)
        def _(slot=slot, spot=spot):
            key_total[spot] += back[slot, :rows, :].astype(F32)
            value_total[spot] += back[slot, rows:, :].astype(F32)

    key_grads[...] = key_total[...].astype(BF16)
    value_grads[...] = value_total[...].astype(BF16)


def combined(part, asked, own_keys, own_values, back, earlier):
    mem_count, rows, wide = own_keys.shape
    shape = jax.ShapeDtypeStruct((mem_count, rows, wide * PARTS), BF16)
    block = pl.BlockSpec((mem_count, rows, wide), lambda i: (0, 0, part))
    return pl.pallas_call(
        functools.partial(combine_kernel, part),
        grid=(1,),
        out_shape=[shape, shape],
        in_specs=[SMEM, VMEM, VMEM, VMEM] + [pl.BlockSpec(memory_space=pl.ANY)] * len(earlier),
        out_specs=[block, block],
        scratch_shapes=[pltpu.VMEM(own_keys.shape, F32)] * 2,
        input_output_aliases={4 + i: i for i in range(len(earlier))},
        compiler_params=PARAMS,
        cost_estimate=cost(0, 4 * 2**20),
        name=f"combine_part{part}",
    )(asked, own_keys, own_values, back, *earlier)


def on_device(sent_queries, mem_keys, mem_values, out_weight, sent_grads, counts, neg_ids):
    keys, values = mem_keys[0], mem_values[0]
    mem_count = keys.shape[0]
    groups = lax.axis_size("dp")
    tensor = lax.axis_size("tensor")

    flat_ids = neg_ids.reshape(-1)
    holder = flat_ids // mem_count
    spot = flat_ids - holder * mem_count
    named = holder[None, :] == jnp.arange(groups, dtype=jnp.int32)[:, None]
    request = jnp.sum(jnp.where(named, spot[None, :] + 1, 0), axis=1) - 1
    asked = exchanged(request.reshape(groups, 1)).reshape(groups)

    queries = passed_along(sent_queries, "section", 1)[0]
    grads = passed_along(sent_grads, "section", -1)[0]
    docs, query_count, features = queries.shape
    weight = lax.all_gather(out_weight[0], "dp")

    recv = [exchanged(part) for part in picked_slots(asked, keys, values)]

    grad_rows = grads.reshape(docs * query_count, grads.shape[2])
    held = [grad_rows] + [passed_along(grad_rows, "tensor", -j) for j in range(1, tensor)]
    grad_attended = back_projected(weight, held).reshape(docs, query_count, features)

    attended, query_grads, own, back = [], [], [], []
    for part in range(PARTS):
        out, grad_query, own_keys, own_values, slots = attend_part(
            part, counts, holder, queries, keys, values, recv[part], grad_attended
        )
        attended.append(out.reshape(docs * query_count, -1))
        query_grads.append(grad_query)
        own.append((own_keys, own_values))
        back.append(exchanged(slots))

    mixed = lax.psum_scatter(projected(weight, attended, tensor), "tensor", scatter_dimension=0)
    mixed = mixed.reshape(1, docs, query_count, -1)

    grads_out = []
    for part in range(PARTS):
        grads_out = combined(part, asked, *own[part], back[part], grads_out)
    key_grads, value_grads = grads_out
    return mixed, jnp.concatenate(query_grads, axis=-1)[None], key_grads[None], value_grads[None]


def solution(mesh):
    rows = P("section", "dp", None, "tensor")
    return jax.shard_map(
        on_device,
        mesh=mesh,
        in_specs=(rows, rows, rows, P("section", "tensor", "dp"), rows, P("dp"), P("dp", None)),
        out_specs=(rows, rows, rows, rows),
        check_vma=False,
    )
```

```python
import jax
import jax.numpy as jnp
from jax import lax
from jax.experimental import pallas as pl
from jax.experimental.pallas import tpu as pltpu
from jax.sharding import PartitionSpec as P

HD = 128
F32 = jnp.float32
BF16 = jnp.bfloat16
NT = (((1,), (1,)), ((), ()))
TN = (((0,), (0,)), ((), ()))
VMEM = pl.BlockSpec(memory_space=pltpu.VMEM)
HBM = pl.BlockSpec(memory_space=pltpu.HBM)
SMEM = pl.BlockSpec(memory_space=pltpu.SMEM)
PARAMS = pltpu.CompilerParams(vmem_limit_bytes=60 * 1024 * 1024)


def passed_along(block, axis, distance):
    count = lax.axis_size(axis)
    return lax.ppermute(block, axis, [(i, (i + distance) % count) for i in range(count)])


def exchanged(slots):
    return lax.all_to_all(slots, "dp", split_axis=0, concat_axis=0, tiled=True)


def cost(flops, nbytes):
    return pl.CostEstimate(flops=int(flops), bytes_accessed=int(nbytes), transcendentals=0)


def pick_kernel(asked, keys, values, slots, sem):
    rows = keys.shape[1]
    copies = []
    for slot in range(slots.shape[0]):
        spot = jnp.maximum(asked[slot], 0)
        copies.append(pltpu.make_async_copy(keys.at[spot], slots.at[slot, pl.ds(0, rows)], sem.at[slot, 0]))
        copies.append(pltpu.make_async_copy(values.at[spot], slots.at[slot, pl.ds(rows, rows)], sem.at[slot, 1]))
    for copy in copies:
        copy.start()
    for copy in copies:
        copy.wait()


def picked_slots(asked, keys, values):
    slot_count = asked.shape[0]
    _, rows, features = keys.shape
    return pl.pallas_call(
        pick_kernel,
        out_shape=jax.ShapeDtypeStruct((slot_count, 2 * rows, features), BF16),
        in_specs=[SMEM, HBM, HBM],
        out_specs=HBM,
        scratch_shapes=[pltpu.SemaphoreType.DMA((slot_count, 2))],
        compiler_params=PARAMS,
        cost_estimate=cost(0, 4 * 2**20),
        name="pick_blocks",
    )(asked, keys, values)


def layer_kernel(
    counts, holder, spot, queries_hbm, keys_hbm, values_hbm, recv_hbm, weight_hbm, grad0, grad1, grad2, grad3,
    terms_hbm, grad_query_hbm, own_keys_hbm, own_values_hbm, slots_hbm,
    queries, keys, values, recv, weight, held, grads, attended, terms, grad_query, own_keys, own_values, slots,
    weight_sem, held_sem, in_sem, recv_sem, own_sem, slot_sem, term_sem, query_sem,
):
    docs = queries.shape[0]
    mem_count, rows, features = keys.shape
    own = mem_count // docs
    neg = holder.shape[0] // docs
    groups, per, _, block = weight.shape
    scale = HD**-0.5
    total = (own + neg) * rows

    group_of = [lax.rem(spot[0] + j, groups) for j in range(groups)]
    in_weight = [
        pltpu.make_async_copy(weight_hbm.at[pl.ds(group_of[j] * per, per)], weight.at[j], weight_sem.at[j])
        for j in range(groups)
    ]
    in_held = [
        pltpu.make_async_copy(ref, held.at[j], held_sem.at[j]) for j, ref in enumerate((grad0, grad1, grad2, grad3))
    ]
    in_rest = [
        pltpu.make_async_copy(source, target, in_sem.at[i])
        for i, (source, target) in enumerate(((queries_hbm, queries), (keys_hbm, keys), (values_hbm, values)))
    ]
    in_recv = [
        pltpu.make_async_copy(recv_hbm.at[holder[e]], recv.at[e], recv_sem.at[e]) for e in range(docs * neg)
    ]
    for j in range(groups):
        in_weight[j].start()
        in_held[j].start()
    for copy in in_rest + in_recv:
        copy.start()

    grad_rows = None
    for j in range(groups):
        in_weight[j].wait()
        in_held[j].wait()
        for c in range(per):
            term = lax.dot_general(
                held[j, :, c * block : (c + 1) * block], weight[j, c], NT, preferred_element_type=F32
            )
            grad_rows = term if grad_rows is None else grad_rows + term
    grads[...] = grad_rows.astype(BF16)

    for copy in in_rest + in_recv:
        copy.wait()
    position = lax.broadcasted_iota(jnp.int32, (total, 1), 0)
    outgoing = []
    for doc in range(docs):
        valid = (position < counts[doc] * rows) | (position >= own * rows)
        query_rows = slice(doc * queries.shape[1], (doc + 1) * queries.shape[1])
        entries = range(doc * neg, (doc + 1) * neg)
        blocks = range(doc * own, (doc + 1) * own)
        for head in range(features // HD):
            at = slice(head * HD, (head + 1) * HD)
            query = queries[doc, :, at]
            grad = grads[query_rows, at]
            key = jnp.concatenate([keys[m, :, at] for m in blocks] + [recv[e, :rows, at] for e in entries], axis=0)
            value = jnp.concatenate([values[m, :, at] for m in blocks] + [recv[e, rows:, at] for e in entries], axis=0)
            scores = lax.dot_general(key, query, NT, preferred_element_type=F32) * scale
            scores = jnp.where(valid, scores, -jnp.inf)
            expo = jnp.exp(scores - jnp.max(scores, axis=0, keepdims=True))
            prob = expo * (1.0 / jnp.sum(expo, axis=0, keepdims=True))
            prob_round = prob.astype(BF16)
            attended[query_rows, at] = lax.dot_general(
                prob_round, value, TN, preferred_element_type=F32
            ).astype(BF16)
            grad_prob = lax.dot_general(value, grad, NT, preferred_element_type=F32)
            delta = jnp.sum(prob * grad_prob, axis=0, keepdims=True)
            grad_score = (prob * (grad_prob - delta)).astype(BF16)
            grad_query[doc, :, at] = (
                lax.dot_general(grad_score, key, TN, preferred_element_type=F32) * scale
            ).astype(BF16)
            grad_key = jnp.dot(grad_score, query, preferred_element_type=F32) * scale
            grad_value = jnp.dot(prob_round, grad, preferred_element_type=F32)
            for m, place in enumerate(blocks):
                here = slice(m * rows, (m + 1) * rows)
                own_keys[place, :, at] = grad_key[here]
                own_values[place, :, at] = grad_value[here]
            for m, entry in enumerate(entries):
                here = slice((own + m) * rows, (own + m + 1) * rows)
                slots[entry, :rows, at] = grad_key[here].astype(BF16)
                slots[entry, rows:, at] = grad_value[here].astype(BF16)
        for e in entries:
            outgoing.append(pltpu.make_async_copy(slots.at[e], slots_hbm.at[holder[e]], slot_sem.at[e]))
        span = pl.ds(doc * own, own)
        outgoing.append(pltpu.make_async_copy(own_keys.at[span], own_keys_hbm.at[span], own_sem.at[doc, 0]))
        outgoing.append(pltpu.make_async_copy(own_values.at[span], own_values_hbm.at[span], own_sem.at[doc, 1]))
        outgoing.append(pltpu.make_async_copy(grad_query.at[doc], grad_query_hbm.at[doc], query_sem.at[doc]))
        for copy in outgoing[-(neg + 3) :]:
            copy.start()

    for j in range(groups):
        for c in range(per):
            term = jnp.dot(attended[...], weight[j, c], preferred_element_type=F32)
            terms[j, :, c * block : (c + 1) * block] = term.astype(BF16)
        outgoing.append(pltpu.make_async_copy(terms.at[j], terms_hbm.at[group_of[j]], term_sem.at[j]))
        outgoing[-1].start()
    for copy in outgoing:
        copy.wait()


def layer(counts, holder, spot, queries, keys, values, recv, weight, held):
    docs, query_count, features = queries.shape
    entries, groups = holder.shape[0], len(held)
    rows, columns = held[0].shape
    dma = pltpu.SemaphoreType.DMA
    return pl.pallas_call(
        layer_kernel,
        out_shape=[
            jax.ShapeDtypeStruct((groups, rows, columns), BF16),
            jax.ShapeDtypeStruct(queries.shape, BF16),
            jax.ShapeDtypeStruct(keys.shape, F32),
            jax.ShapeDtypeStruct(values.shape, F32),
            jax.ShapeDtypeStruct(recv.shape, BF16),
        ],
        in_specs=[SMEM] * 3 + [HBM] * (5 + groups),
        out_specs=[HBM] * 5,
        scratch_shapes=[
            pltpu.VMEM(queries.shape, BF16),
            pltpu.VMEM(keys.shape, BF16),
            pltpu.VMEM(values.shape, BF16),
            pltpu.VMEM((entries, *recv.shape[1:]), BF16),
            pltpu.VMEM((groups, weight.shape[0] // groups, *weight.shape[1:]), BF16),
            pltpu.VMEM((groups, rows, columns), BF16),
            pltpu.VMEM((rows, features), BF16),
            pltpu.VMEM((rows, features), BF16),
            pltpu.VMEM((groups, rows, columns), BF16),
            pltpu.VMEM(queries.shape, BF16),
            pltpu.VMEM(keys.shape, F32),
            pltpu.VMEM(values.shape, F32),
            pltpu.VMEM((entries, *recv.shape[1:]), BF16),
            dma((groups,)),
            dma((groups,)),
            dma((3,)),
            dma((entries,)),
            dma((docs, 2)),
            dma((entries,)),
            dma((groups,)),
            dma((docs,)),
        ],
        compiler_params=PARAMS,
        cost_estimate=cost(5 * 2**30, 16 * 2**20),
        name="layer",
    )(counts, holder, spot, queries, keys, values, recv, weight, *held)


def combine_kernel(asked, own_keys, own_values, back, key_grads, value_grads, key_total, value_total):
    rows = own_keys.shape[1]
    key_total[...] = own_keys[...]
    value_total[...] = own_values[...]
    for slot in range(back.shape[0]):
        spot = asked[slot]

        @pl.when(spot >= 0)
        def _(slot=slot, spot=spot):
            key_total[spot] += back[slot, :rows, :].astype(F32)
            value_total[spot] += back[slot, rows:, :].astype(F32)

    key_grads[...] = key_total[...].astype(BF16)
    value_grads[...] = value_total[...].astype(BF16)


def combined(asked, own_keys, own_values, back):
    shape = jax.ShapeDtypeStruct(own_keys.shape, BF16)
    return pl.pallas_call(
        combine_kernel,
        out_shape=[shape, shape],
        in_specs=[SMEM, VMEM, VMEM, VMEM],
        out_specs=[VMEM, VMEM],
        scratch_shapes=[pltpu.VMEM(own_keys.shape, F32)] * 2,
        compiler_params=PARAMS,
        cost_estimate=cost(0, 4 * 2**20),
        name="combine",
    )(asked, own_keys, own_values, back)


def on_device(sent_queries, mem_keys, mem_values, out_weight, sent_grads, counts, neg_ids):
    keys, values = mem_keys[0], mem_values[0]
    mem_count = keys.shape[0]
    groups = lax.axis_size("dp")
    tensor = lax.axis_size("tensor")
    tensor_spot = lax.axis_index("tensor").astype(jnp.int32).reshape(1)

    flat_ids = neg_ids.reshape(-1)
    holder = flat_ids // mem_count
    spot = flat_ids - holder * mem_count
    named = holder[None, :] == jnp.arange(groups, dtype=jnp.int32)[:, None]
    request = jnp.sum(jnp.where(named, spot[None, :] + 1, 0), axis=1) - 1
    asked = exchanged(request.reshape(groups, 1)).reshape(groups)

    queries = passed_along(sent_queries, "section", 1)[0]
    grads = passed_along(sent_grads, "section", -1)[0]
    docs, query_count, features = queries.shape
    weight = lax.all_gather(out_weight[0], "dp")

    recv = exchanged(picked_slots(asked, keys, values))

    grad_rows = grads.reshape(docs * query_count, grads.shape[2])
    held = [grad_rows] + [passed_along(grad_rows, "tensor", -j) for j in range(1, tensor)]
    terms, query_grads, own_keys, own_values, slots = layer(
        counts, holder, tensor_spot, queries, keys, values, recv, weight, held
    )
    back = exchanged(slots)
    mixed = lax.psum_scatter(terms, "tensor", scatter_dimension=0).reshape(1, docs, query_count, -1)

    key_grads, value_grads = combined(asked, own_keys, own_values, back)
    return mixed, query_grads[None], key_grads[None], value_grads[None]


def solution(mesh):
    rows = P("section", "dp", None, "tensor")
    return jax.shard_map(
        on_device,
        mesh=mesh,
        in_specs=(rows, rows, rows, P("section", "tensor", "dp"), rows, P("dp"), P("dp", None)),
        out_specs=(rows, rows, rows, rows),
        check_vma=False,
    )
```

```python
import jax
import jax.numpy as jnp
from jax import lax
from jax.experimental import pallas as pl
from jax.experimental.pallas import tpu as pltpu
from jax.sharding import PartitionSpec as P

HD = 128
F32 = jnp.float32
BF16 = jnp.bfloat16
NT = (((1,), (1,)), ((), ()))
TN = (((0,), (0,)), ((), ()))
VMEM = pl.BlockSpec(memory_space=pltpu.VMEM)
HBM = pl.BlockSpec(memory_space=pltpu.HBM)
ANY = pl.BlockSpec(memory_space=pl.ANY)
SMEM = pl.BlockSpec(memory_space=pltpu.SMEM)
PARAMS = pltpu.CompilerParams(vmem_limit_bytes=24 * 1024 * 1024)


def passed_along(block, axis, distance):
    count = lax.axis_size(axis)
    return lax.ppermute(block, axis, [(i, (i + distance) % count) for i in range(count)])


def exchanged(slots):
    return lax.all_to_all(slots, "dp", split_axis=0, concat_axis=0, tiled=True)


def in_hbm(array):
    return pltpu.with_memory_space_constraint(array, pltpu.HBM)


def cost(flops, nbytes):
    return pl.CostEstimate(flops=int(flops), bytes_accessed=int(nbytes), transcendentals=0)


def pick_kernel(asked, keys_hbm, values_hbm, slots, keys, values, in_sem, out_sem):
    rows = keys.shape[1]
    in_key = pltpu.make_async_copy(keys_hbm, keys, in_sem.at[0])
    in_value = pltpu.make_async_copy(values_hbm, values, in_sem.at[1])
    in_key.start()
    in_value.start()
    outgoing = []
    for which, (arriving, source) in enumerate(((in_key, keys), (in_value, values))):
        arriving.wait()
        for slot in range(slots.shape[0]):
            spot = jnp.maximum(asked[slot, 0], 0)
            target = slots.at[slot, pl.ds(which * rows, rows)]
            outgoing.append(pltpu.make_async_copy(source.at[spot], target, out_sem.at[slot, which]))
            outgoing[-1].start()
    for copy in outgoing:
        copy.wait()


def picked_slots(asked, keys, values):
    slot_count = asked.shape[0]
    _, rows, features = keys.shape
    return pl.pallas_call(
        pick_kernel,
        out_shape=pltpu.HBM((slot_count, 2 * rows, features), BF16),
        in_specs=[SMEM, HBM, HBM],
        out_specs=HBM,
        scratch_shapes=[
            pltpu.VMEM(keys.shape, BF16),
            pltpu.VMEM(values.shape, BF16),
            pltpu.SemaphoreType.DMA((2,)),
            pltpu.SemaphoreType.DMA((slot_count, 2)),
        ],
        compiler_params=PARAMS,
        cost_estimate=cost(0, 4 * 2**20),
        name="pick_blocks",
    )(asked, in_hbm(keys), in_hbm(values))


def layer_kernel(
    counts, holder, spot, queries_hbm, keys_hbm, values_hbm, recv_hbm, weight_hbm, grad0, grad1, grad2, grad3,
    attended, grad_query_hbm, own_rows_hbm, slots_hbm,
    queries, keys, values, recv, weight, held, grads, grad_query, own_rows, slots,
    weight_sem, held_sem, in_sem, recv_sem, own_sem, slot_sem, query_sem,
):
    docs = queries.shape[0]
    mem_count, rows, features = keys.shape
    own = mem_count // docs
    neg = holder.shape[1]
    groups, per, _, block = weight.shape
    scale = HD**-0.5
    total = (own + neg) * rows

    group_of = [lax.rem(spot[0] + j, groups) for j in range(groups)]
    in_weight = [
        pltpu.make_async_copy(weight_hbm.at[pl.ds(group_of[j] * per, per)], weight.at[j], weight_sem.at[j])
        for j in range(groups)
    ]
    in_held = [
        pltpu.make_async_copy(ref, held.at[j], held_sem.at[j]) for j, ref in enumerate((grad0, grad1, grad2, grad3))
    ]
    in_rest = [
        pltpu.make_async_copy(source, target, in_sem.at[i])
        for i, (source, target) in enumerate(((queries_hbm, queries), (keys_hbm, keys), (values_hbm, values)))
    ]
    in_recv = [
        pltpu.make_async_copy(recv_hbm.at[holder[e // neg, e % neg]], recv.at[e], recv_sem.at[e])
        for e in range(docs * neg)
    ]
    for j in range(groups):
        in_weight[j].start()
        in_held[j].start()
    for copy in in_rest + in_recv:
        copy.start()

    grad_rows = None
    for j in range(groups):
        in_weight[j].wait()
        in_held[j].wait()
        for c in range(per):
            term = lax.dot_general(
                held[j, :, c * block : (c + 1) * block], weight[j, c], NT, preferred_element_type=F32
            )
            grad_rows = term if grad_rows is None else grad_rows + term
    grads[...] = grad_rows.astype(BF16)

    for copy in in_rest + in_recv:
        copy.wait()
    position = lax.broadcasted_iota(jnp.int32, (total, 1), 0)
    outgoing = []
    for doc in range(docs):
        valid = (position < counts[doc] * rows) | (position >= own * rows)
        query_rows = slice(doc * queries.shape[1], (doc + 1) * queries.shape[1])
        entries = range(doc * neg, (doc + 1) * neg)
        blocks = range(doc * own, (doc + 1) * own)
        for head in range(features // HD):
            at = slice(head * HD, (head + 1) * HD)
            query = queries[doc, :, at]
            grad = grads[query_rows, at]
            key = jnp.concatenate([keys[m, :, at] for m in blocks] + [recv[e, :rows, at] for e in entries], axis=0)
            value = jnp.concatenate([values[m, :, at] for m in blocks] + [recv[e, rows:, at] for e in entries], axis=0)
            scores = lax.dot_general(key, query, NT, preferred_element_type=F32) * scale
            scores = jnp.where(valid, scores, -jnp.inf)
            expo = jnp.exp(scores - jnp.max(scores, axis=0, keepdims=True))
            prob = expo * (1.0 / jnp.sum(expo, axis=0, keepdims=True))
            prob_round = prob.astype(BF16)
            attended[query_rows, at] = lax.dot_general(
                prob_round, value, TN, preferred_element_type=F32
            ).astype(BF16)
            grad_prob = lax.dot_general(value, grad, NT, preferred_element_type=F32)
            delta = jnp.sum(prob * grad_prob, axis=0, keepdims=True)
            grad_score = (prob * (grad_prob - delta)).astype(BF16)
            grad_query[doc, :, at] = (
                lax.dot_general(grad_score, key, TN, preferred_element_type=F32) * scale
            ).astype(BF16)
            grad_key = jnp.dot(grad_score, query, preferred_element_type=F32) * scale
            grad_value = jnp.dot(prob_round, grad, preferred_element_type=F32)
            for m, place in enumerate(blocks):
                here = slice(m * rows, (m + 1) * rows)
                own_rows[0, place, :, at] = grad_key[here]
                own_rows[1, place, :, at] = grad_value[here]
            for m in range(neg):
                here = slice((own + m) * rows, (own + m + 1) * rows)
                slots[doc * neg + m, :rows, at] = grad_key[here].astype(BF16)
                slots[doc * neg + m, rows:, at] = grad_value[here].astype(BF16)
        for m in range(neg):
            entry = doc * neg + m
            outgoing.append(pltpu.make_async_copy(slots.at[entry], slots_hbm.at[holder[doc, m]], slot_sem.at[entry]))
        span = pl.ds(doc * own, own)
        outgoing.append(pltpu.make_async_copy(own_rows.at[:, span], own_rows_hbm.at[:, span], own_sem.at[doc]))
        outgoing.append(pltpu.make_async_copy(grad_query.at[doc], grad_query_hbm.at[doc], query_sem.at[doc]))
        for copy in outgoing[-(neg + 2) :]:
            copy.start()

    for copy in outgoing:
        copy.wait()


def layer(counts, holder, spot, queries, keys, values, recv, weight, held):
    docs, query_count, features = queries.shape
    entries, groups = holder.shape[0] * holder.shape[1], len(held)
    rows, columns = held[0].shape
    dma = pltpu.SemaphoreType.DMA
    return pl.pallas_call(
        layer_kernel,
        out_shape=[
            jax.ShapeDtypeStruct((rows, features), BF16),
            pltpu.HBM(queries.shape, BF16),
            pltpu.HBM((2, *keys.shape), F32),
            pltpu.HBM(recv.shape, BF16),
        ],
        in_specs=[SMEM] * 3 + [HBM, HBM, HBM, ANY, HBM] + [HBM] * groups,
        out_specs=[VMEM] + [HBM] * 3,
        scratch_shapes=[
            pltpu.VMEM(queries.shape, BF16),
            pltpu.VMEM(keys.shape, BF16),
            pltpu.VMEM(values.shape, BF16),
            pltpu.VMEM((entries, *recv.shape[1:]), BF16),
            pltpu.VMEM((groups, weight.shape[0] // groups, *weight.shape[1:]), BF16),
            pltpu.VMEM((groups, rows, columns), BF16),
            pltpu.VMEM((rows, features), BF16),
            pltpu.VMEM(queries.shape, BF16),
            pltpu.VMEM((2, *keys.shape), F32),
            pltpu.VMEM((entries, *recv.shape[1:]), BF16),
            dma((groups,)),
            dma((groups,)),
            dma((3,)),
            dma((entries,)),
            dma((docs,)),
            dma((entries,)),
            dma((docs,)),
        ],
        compiler_params=PARAMS,
        cost_estimate=cost(5 * 2**30, 16 * 2**20),
        name="layer",
    )(counts, holder, spot, in_hbm(queries), in_hbm(keys), in_hbm(values), recv, in_hbm(weight), *map(in_hbm, held))


def project_kernel(spot, weight_hbm, attended, out0, out1, out2, out3, weight, sem):
    groups, per, _, block = weight.shape
    outs = (out0, out1, out2, out3)
    copies = []
    for j in range(groups):
        first = lax.rem(spot[0] + j, groups) * per
        copies.append(pltpu.make_async_copy(weight_hbm.at[pl.ds(first, per)], weight.at[j], sem.at[j]))
        copies[j].start()
    for j, out in enumerate(outs):
        copies[j].wait()
        for c in range(per):
            term = jnp.dot(attended[...], weight[j, c], preferred_element_type=F32)
            out[:, c * block : (c + 1) * block] = term.astype(BF16)


def projected(spot, weight, attended, groups):
    per = weight.shape[0] // groups
    shape = jax.ShapeDtypeStruct((attended.shape[0], per * weight.shape[2]), BF16)
    return pl.pallas_call(
        project_kernel,
        out_shape=[shape] * groups,
        in_specs=[SMEM, HBM, VMEM],
        out_specs=[VMEM] * groups,
        scratch_shapes=[
            pltpu.VMEM((groups, per, *weight.shape[1:]), BF16),
            pltpu.SemaphoreType.DMA((groups,)),
        ],
        compiler_params=PARAMS,
        cost_estimate=cost(2 * 2**30, 8 * 2**20),
        name="projection",
    )(spot, in_hbm(weight), attended)


def combine_kernel(asked, own_rows, back, key_grads, value_grads, total):
    rows = own_rows.shape[2]
    total[...] = own_rows[...]
    for slot in range(back.shape[0]):
        spot = asked[slot, 0]

        @pl.when(spot >= 0)
        def _(slot=slot, spot=spot):
            total[0, spot] += back[slot, :rows, :].astype(F32)
            total[1, spot] += back[slot, rows:, :].astype(F32)

    key_grads[...] = total[0].astype(BF16)
    value_grads[...] = total[1].astype(BF16)


def combined(asked, own_rows, back):
    shape = jax.ShapeDtypeStruct(own_rows.shape[1:], BF16)
    return pl.pallas_call(
        combine_kernel,
        out_shape=[shape, shape],
        in_specs=[SMEM, VMEM, VMEM],
        out_specs=[VMEM, VMEM],
        scratch_shapes=[pltpu.VMEM(own_rows.shape, F32)],
        compiler_params=PARAMS,
        cost_estimate=cost(0, 4 * 2**20),
        name="combine",
    )(asked, own_rows, back)


def on_device(sent_queries, mem_keys, mem_values, out_weight, sent_grads, counts, neg_ids):
    keys, values = mem_keys[0], mem_values[0]
    mem_count = keys.shape[0]
    groups = lax.axis_size("dp")
    tensor = lax.axis_size("tensor")
    tensor_spot = lax.axis_index("tensor").astype(jnp.int32).reshape(1)

    holder = neg_ids // mem_count
    spot = neg_ids - holder * mem_count
    named = holder[None] == jnp.arange(groups, dtype=jnp.int32)[:, None, None]
    request = jnp.sum(jnp.where(named, spot[None] + 1, 0), axis=(1, 2)) - 1
    asked = exchanged(request.reshape(groups, 1))

    queries = passed_along(sent_queries, "section", 1)[0]
    grads = passed_along(sent_grads, "section", -1)[0]
    docs, query_count, features = queries.shape
    weight = lax.all_gather(out_weight[0], "dp")

    recv = exchanged(picked_slots(asked, keys, values))

    grad_rows = grads.reshape(docs * query_count, grads.shape[2])
    held = [grad_rows] + [passed_along(grad_rows, "tensor", -j) for j in range(1, tensor)]
    attended, query_grads, own_rows, slots = layer(
        counts, holder, tensor_spot, queries, keys, values, recv, weight, held
    )
    back = exchanged(slots)
    terms = projected(tensor_spot, weight, attended, tensor)
    arrived = [terms[0]] + [passed_along(terms[j], "tensor", j) for j in range(1, tensor)]
    mixed = sum(term.astype(F32) for term in arrived).astype(BF16).reshape(1, docs, query_count, -1)

    key_grads, value_grads = combined(asked, own_rows, back)
    return mixed, query_grads[None], key_grads[None], value_grads[None]


def solution(mesh):
    rows = P("section", "dp", None, "tensor")
    return jax.shard_map(
        on_device,
        mesh=mesh,
        in_specs=(rows, rows, rows, P("section", "tensor", "dp"), rows, P("dp"), P("dp", None)),
        out_specs=(rows, rows, rows, rows),
        check_vma=False,
    )
```

```python
import jax
import jax.numpy as jnp
from jax import lax
from jax.experimental import pallas as pl
from jax.experimental.pallas import tpu as pltpu
from jax.sharding import PartitionSpec as P

HD = 128
F32 = jnp.float32
BF16 = jnp.bfloat16
NT = (((1,), (1,)), ((), ()))
TN = (((0,), (0,)), ((), ()))
VMEM = pl.BlockSpec(memory_space=pltpu.VMEM)
HBM = pl.BlockSpec(memory_space=pltpu.HBM)
ANY = pl.BlockSpec(memory_space=pl.ANY)
SMEM = pl.BlockSpec(memory_space=pltpu.SMEM)
PARAMS = pltpu.CompilerParams(vmem_limit_bytes=16 * 1024 * 1024)


def passed_along(block, axis, distance):
    count = lax.axis_size(axis)
    return lax.ppermute(block, axis, [(i, (i + distance) % count) for i in range(count)])


def exchanged(slots):
    return lax.all_to_all(slots, "dp", split_axis=0, concat_axis=0, tiled=True)


def in_hbm(array):
    return pltpu.with_memory_space_constraint(array, pltpu.HBM)


def cost(flops, nbytes):
    return pl.CostEstimate(flops=int(flops), bytes_accessed=int(nbytes), transcendentals=0)


def pick_kernel(asked, keys_hbm, values_hbm, slots, keys, values, in_sem, out_sem):
    rows = keys.shape[1]
    in_key = pltpu.make_async_copy(keys_hbm, keys, in_sem.at[0])
    in_value = pltpu.make_async_copy(values_hbm, values, in_sem.at[1])
    in_key.start()
    in_value.start()
    outgoing = []
    for which, (arriving, source) in enumerate(((in_key, keys), (in_value, values))):
        arriving.wait()
        for slot in range(slots.shape[0]):
            spot = asked[slot, 0]
            target = slots.at[slot, pl.ds(which * rows, rows)]
            copy = pltpu.make_async_copy(source.at[jnp.maximum(spot, 0)], target, out_sem.at[slot, which])
            pl.when(spot >= 0)(copy.start)
            outgoing.append((spot, copy))
    for spot, copy in outgoing:
        pl.when(spot >= 0)(copy.wait)


def picked_slots(asked, keys, values):
    slot_count = asked.shape[0]
    _, rows, features = keys.shape
    return pl.pallas_call(
        pick_kernel,
        out_shape=pltpu.HBM((slot_count, 2 * rows, features), BF16),
        in_specs=[SMEM, HBM, HBM],
        out_specs=HBM,
        scratch_shapes=[
            pltpu.VMEM(keys.shape, BF16),
            pltpu.VMEM(values.shape, BF16),
            pltpu.SemaphoreType.DMA((2,)),
            pltpu.SemaphoreType.DMA((slot_count, 2)),
        ],
        compiler_params=PARAMS,
        cost_estimate=cost(0, 4 * 2**20),
        name="pick_blocks",
    )(asked, in_hbm(keys), in_hbm(values))


def layer_kernel(
    counts, holder, spot, queries, keys, values, recv, weight_hbm, grad0, grad1, grad2, grad3,
    attended_hbm, grad_query, own_rows_hbm, slots_hbm,
    weight, held, grads, probs, attended, own_rows, slots, weight_sem, held_sem, out_sem, own_sem, slot_sem,
):
    docs, query_count, _ = queries.shape
    mem_count, rows, features = keys.shape
    own = mem_count // docs
    neg = holder.shape[1]
    groups, per, _, block = weight.shape
    heads = features // HD
    scale = HD**-0.5
    total = (own + neg) * rows

    arriving = []
    for j, grad in enumerate((grad0, grad1, grad2, grad3)):
        first = lax.rem(spot[0] + j, groups) * per
        in_weight = pltpu.make_async_copy(weight_hbm.at[pl.ds(first, per)], weight.at[j], weight_sem.at[j])
        in_held = pltpu.make_async_copy(grad, held.at[j], held_sem.at[j])
        in_held.start()
        in_weight.start()
        arriving.append((in_held, in_weight))

    def listed(doc, head):
        at = slice(head * HD, (head + 1) * HD)
        blocks = range(doc * own, (doc + 1) * own)
        senders = [holder[doc, m] for m in range(neg)]
        key = jnp.concatenate([keys[m, :, at] for m in blocks] + [recv[e, :rows, at] for e in senders], axis=0)
        value = jnp.concatenate([values[m, :, at] for m in blocks] + [recv[e, rows:, at] for e in senders], axis=0)
        return at, slice(doc * query_count, (doc + 1) * query_count), key, value

    position = lax.broadcasted_iota(jnp.int32, (total, 1), 0)
    for doc in range(docs):
        valid = (position < counts[doc] * rows) | (position >= own * rows)
        for head in range(heads):
            at, query_rows, key, value = listed(doc, head)
            scores = lax.dot_general(key, queries[doc, :, at], NT, preferred_element_type=F32) * scale
            scores = jnp.where(valid, scores, -jnp.inf)
            expo = jnp.exp(scores - jnp.max(scores, axis=0, keepdims=True))
            prob = expo * (1.0 / jnp.sum(expo, axis=0, keepdims=True))
            probs[doc * heads + head] = prob
            attended[query_rows, at] = lax.dot_general(
                prob.astype(BF16), value, TN, preferred_element_type=F32
            ).astype(BF16)

    outgoing = [pltpu.make_async_copy(attended, attended_hbm, out_sem)]
    outgoing[0].start()

    grad_rows = None
    for j, copies in enumerate(arriving):
        for copy in copies:
            copy.wait()
        for c in range(per):
            term = lax.dot_general(
                held[j, :, c * block : (c + 1) * block], weight[j, c], NT, preferred_element_type=F32
            )
            grad_rows = term if grad_rows is None else grad_rows + term
    grads[...] = grad_rows.astype(BF16)

    for doc in range(docs):
        for head in range(heads):
            at, query_rows, key, value = listed(doc, head)
            grad = grads[query_rows, at]
            prob = probs[doc * heads + head]
            grad_prob = lax.dot_general(value, grad, NT, preferred_element_type=F32)
            delta = jnp.sum(prob * grad_prob, axis=0, keepdims=True)
            grad_score = (prob * (grad_prob - delta)).astype(BF16)
            grad_value = jnp.dot(prob.astype(BF16), grad, preferred_element_type=F32)
            grad_key = jnp.dot(grad_score, queries[doc, :, at], preferred_element_type=F32) * scale
            grad_query[doc, :, at] = (
                lax.dot_general(grad_score, key, TN, preferred_element_type=F32) * scale
            ).astype(BF16)
            for m in range(own):
                here = slice(m * rows, (m + 1) * rows)
                own_rows[0, doc * own + m, :, at] = grad_key[here]
                own_rows[1, doc * own + m, :, at] = grad_value[here]
            for m in range(neg):
                here = slice((own + m) * rows, (own + m + 1) * rows)
                slots[doc * neg + m, :rows, at] = grad_key[here].astype(BF16)
                slots[doc * neg + m, rows:, at] = grad_value[here].astype(BF16)
        for m in range(neg):
            entry = doc * neg + m
            outgoing.append(pltpu.make_async_copy(slots.at[entry], slots_hbm.at[holder[doc, m]], slot_sem.at[entry]))
        span = pl.ds(doc * own, own)
        outgoing.append(pltpu.make_async_copy(own_rows.at[:, span], own_rows_hbm.at[:, span], own_sem.at[doc]))
        for copy in outgoing[-(neg + 1) :]:
            copy.start()
    for copy in outgoing:
        copy.wait()


def layer(counts, holder, spot, queries, keys, values, recv, weight, held):
    docs, query_count, features = queries.shape
    entries, groups = holder.shape[0] * holder.shape[1], len(held)
    rows, columns = held[0].shape
    dma = pltpu.SemaphoreType.DMA
    return pl.pallas_call(
        layer_kernel,
        out_shape=[
            pltpu.HBM((rows, features), BF16),
            jax.ShapeDtypeStruct(queries.shape, BF16),
            pltpu.HBM((2, *keys.shape), F32),
            pltpu.HBM(recv.shape, BF16),
        ],
        in_specs=[SMEM] * 3 + [VMEM] * 4 + [HBM] * (1 + groups),
        out_specs=[HBM, VMEM, HBM, HBM],
        scratch_shapes=[
            pltpu.VMEM((groups, weight.shape[0] // groups, *weight.shape[1:]), BF16),
            pltpu.VMEM((groups, rows, columns), BF16),
            pltpu.VMEM((rows, features), BF16),
            pltpu.VMEM((docs * features // HD, (keys.shape[0] // docs + holder.shape[1]) * keys.shape[1], query_count), F32),
            pltpu.VMEM((rows, features), BF16),
            pltpu.VMEM((2, *keys.shape), F32),
            pltpu.VMEM((entries, *recv.shape[1:]), BF16),
            dma((groups,)),
            dma((groups,)),
            dma,
            dma((docs,)),
            dma((entries,)),
        ],
        compiler_params=PARAMS,
        cost_estimate=cost(5 * 2**30, 16 * 2**20),
        name="layer",
    )(counts, holder, spot, queries, keys, values, recv, in_hbm(weight), *map(in_hbm, held))


def project_kernel(spot, weight_hbm, attended_hbm, out0, out1, out2, out3, weight, attended, sem, in_sem):
    groups, per, _, block = weight.shape
    outs = (out0, out1, out2, out3)
    in_attended = pltpu.make_async_copy(attended_hbm, attended, in_sem)
    in_attended.start()
    copies = []
    for j in range(groups):
        first = lax.rem(spot[0] + j, groups) * per
        copies.append(pltpu.make_async_copy(weight_hbm.at[pl.ds(first, per)], weight.at[j], sem.at[j]))
        copies[j].start()
    in_attended.wait()
    for j, out in enumerate(outs):
        copies[j].wait()
        for c in range(per):
            term = jnp.dot(attended[...], weight[j, c], preferred_element_type=F32)
            out[:, c * block : (c + 1) * block] = term.astype(BF16)


def projected(spot, weight, attended, groups):
    per = weight.shape[0] // groups
    shape = jax.ShapeDtypeStruct((attended.shape[0], per * weight.shape[2]), BF16)
    return pl.pallas_call(
        project_kernel,
        out_shape=[shape] * groups,
        in_specs=[SMEM, HBM, HBM],
        out_specs=[VMEM] * groups,
        scratch_shapes=[
            pltpu.VMEM((groups, per, *weight.shape[1:]), BF16),
            pltpu.VMEM(attended.shape, BF16),
            pltpu.SemaphoreType.DMA((groups,)),
            pltpu.SemaphoreType.DMA,
        ],
        compiler_params=PARAMS,
        cost_estimate=cost(2 * 2**30, 8 * 2**20),
        name="projection",
    )(spot, in_hbm(weight), in_hbm(attended))


def combine_kernel(asked, own_rows_hbm, back, key_grads_hbm, value_grads_hbm, own_rows, total, grads, in_sem, out_sem):
    rows = own_rows.shape[2]
    arriving = [pltpu.make_async_copy(own_rows_hbm.at[i], own_rows.at[i], in_sem.at[i]) for i in range(2)]
    for copy in arriving:
        copy.start()
    total[...] = jnp.zeros_like(total)
    for slot in range(back.shape[0]):
        spot = asked[slot, 0]

        @pl.when(spot >= 0)
        def _(slot=slot, spot=spot):
            total[0, spot] += back[slot, :rows, :].astype(F32)
            total[1, spot] += back[slot, rows:, :].astype(F32)

    outgoing = []
    for i, target in enumerate((key_grads_hbm, value_grads_hbm)):
        arriving[i].wait()
        grads[i] = (own_rows[i] + total[i]).astype(BF16)
        outgoing.append(pltpu.make_async_copy(grads.at[i], target, out_sem.at[i]))
        outgoing[i].start()
    for copy in outgoing:
        copy.wait()


def combined(asked, own_rows, back):
    shape = pltpu.HBM(own_rows.shape[1:], BF16)
    return pl.pallas_call(
        combine_kernel,
        out_shape=[shape, shape],
        in_specs=[SMEM, HBM, VMEM],
        out_specs=[HBM, HBM],
        scratch_shapes=[
            pltpu.VMEM(own_rows.shape, F32),
            pltpu.VMEM(own_rows.shape, F32),
            pltpu.VMEM(own_rows.shape, BF16),
            pltpu.SemaphoreType.DMA((2,)),
            pltpu.SemaphoreType.DMA((2,)),
        ],
        compiler_params=PARAMS,
        cost_estimate=cost(0, 4 * 2**20),
        name="combine",
    )(asked, in_hbm(own_rows), back)


def on_device(sent_queries, mem_keys, mem_values, out_weight, sent_grads, counts, neg_ids):
    keys, values = mem_keys[0], mem_values[0]
    mem_count = keys.shape[0]
    groups = lax.axis_size("dp")
    tensor = lax.axis_size("tensor")
    tensor_spot = lax.axis_index("tensor").astype(jnp.int32).reshape(1)

    holder = neg_ids // mem_count
    spot = neg_ids - holder * mem_count
    named = holder[None] == jnp.arange(groups, dtype=jnp.int32)[:, None, None]
    request = jnp.sum(jnp.where(named, spot[None] + 1, 0), axis=(1, 2)) - 1
    asked = exchanged(request.reshape(groups, 1))

    queries = passed_along(sent_queries, "section", 1)[0]
    grads = passed_along(sent_grads, "section", -1)[0]
    docs, query_count, features = queries.shape
    weight = lax.all_gather(out_weight[0], "dp")

    recv = exchanged(picked_slots(asked, keys, values))

    grad_rows = grads.reshape(docs * query_count, grads.shape[2])
    held = [grad_rows] + [passed_along(grad_rows, "tensor", -j) for j in range(1, tensor)]
    attended, query_grads, own_rows, slots = layer(
        counts, holder, tensor_spot, queries, keys, values, recv, weight, held
    )
    back = exchanged(slots)
    terms = projected(tensor_spot, weight, attended, tensor)
    arrived = [terms[0]] + [passed_along(terms[j], "tensor", j) for j in range(1, tensor)]
    mixed = sum(term.astype(F32) for term in arrived).astype(BF16).reshape(1, docs, query_count, -1)

    key_grads, value_grads = combined(asked, own_rows, back)
    return mixed, query_grads[None], key_grads[None], value_grads[None]


def solution(mesh):
    rows = P("section", "dp", None, "tensor")
    return jax.shard_map(
        on_device,
        mesh=mesh,
        in_specs=(rows, rows, rows, P("section", "tensor", "dp"), rows, P("dp"), P("dp", None)),
        out_specs=(rows, rows, rows, rows),
        check_vma=False,
    )
```

```python
import jax
import jax.numpy as jnp
from jax import lax
from jax.experimental import pallas as pl
from jax.experimental.pallas import tpu as pltpu
from jax.sharding import PartitionSpec as P

HD = 128
F32 = jnp.float32
BF16 = jnp.bfloat16
NT = (((1,), (1,)), ((), ()))
TN = (((0,), (0,)), ((), ()))
VMEM = pl.BlockSpec(memory_space=pltpu.VMEM)
HBM = pl.BlockSpec(memory_space=pltpu.HBM)
ANY = pl.BlockSpec(memory_space=pl.ANY)
SMEM = pl.BlockSpec(memory_space=pltpu.SMEM)
PARAMS = pltpu.CompilerParams(vmem_limit_bytes=16 * 1024 * 1024)


def passed_along(block, axis, distance):
    count = lax.axis_size(axis)
    return lax.ppermute(block, axis, [(i, (i + distance) % count) for i in range(count)])


def exchanged(slots):
    return lax.all_to_all(slots, "dp", split_axis=0, concat_axis=0, tiled=True)


def in_hbm(array):
    return pltpu.with_memory_space_constraint(array, pltpu.HBM)


def cost(flops, nbytes):
    return pl.CostEstimate(flops=int(flops), bytes_accessed=int(nbytes), transcendentals=0)


def pick_kernel(asked, keys_hbm, values_hbm, slots, keys, values, in_sem, out_sem):
    rows = keys.shape[1]
    in_key = pltpu.make_async_copy(keys_hbm, keys, in_sem.at[0])
    in_value = pltpu.make_async_copy(values_hbm, values, in_sem.at[1])
    in_key.start()
    in_value.start()

    def sent(slot, which, source):
        target = slots.at[slot, pl.ds(which * rows, rows)]
        return pltpu.make_async_copy(source.at[jnp.maximum(asked[slot, 0], 0)], target, out_sem.at[slot, which])

    for which, (arriving, source) in enumerate(((in_key, keys), (in_value, values))):
        arriving.wait()

        @pl.loop(0, slots.shape[0])
        def _(slot, which=which, source=source):
            copy = sent(slot, which, source)
            pl.when(asked[slot, 0] >= 0)(copy.start)

    @pl.loop(0, slots.shape[0])
    def _(slot):
        for which, source in enumerate((keys, values)):
            pl.when(asked[slot, 0] >= 0)(sent(slot, which, source).wait)


def picked_slots(asked, keys, values):
    slot_count = asked.shape[0]
    _, rows, features = keys.shape
    return pl.pallas_call(
        pick_kernel,
        out_shape=pltpu.HBM((slot_count, 2 * rows, features), BF16),
        in_specs=[SMEM, HBM, HBM],
        out_specs=HBM,
        scratch_shapes=[
            pltpu.VMEM(keys.shape, BF16),
            pltpu.VMEM(values.shape, BF16),
            pltpu.SemaphoreType.DMA((2,)),
            pltpu.SemaphoreType.DMA((slot_count, 2)),
        ],
        compiler_params=PARAMS,
        cost_estimate=cost(0, 4 * 2**20),
        name="pick_blocks",
    )(asked, in_hbm(keys), in_hbm(values))


def layer_kernel(
    counts, holder, spot, queries, keys, values, recv, weight_hbm, grad0, grad1, grad2, grad3,
    attended_hbm, grad_query_hbm, own_rows_hbm, slots_hbm,
    weight, held, grads, probs, attended, grad_query, own_rows, slots, weight_sem, held_sem, out_sem, own_sem, slot_sem,
):
    docs, query_count, _ = queries.shape
    mem_count, rows, features = keys.shape
    own = mem_count // docs
    neg = holder.shape[1]
    groups, per, _, block = weight.shape
    heads = features // HD
    scale = HD**-0.5
    total = (own + neg) * rows

    arriving = []
    for j, grad in enumerate((grad0, grad1, grad2, grad3)):
        first = lax.rem(spot[0] + j, groups) * per
        in_weight = pltpu.make_async_copy(weight_hbm.at[pl.ds(first, per)], weight.at[j], weight_sem.at[j])
        in_held = pltpu.make_async_copy(grad, held.at[j], held_sem.at[j])
        in_held.start()
        in_weight.start()
        arriving.append((in_held, in_weight))

    def place(step):
        doc, head = step // heads, lax.rem(step, heads)
        at = pl.ds(pl.multiple_of(head * HD, HD), HD)
        query_rows = pl.ds(pl.multiple_of(doc * query_count, query_count), query_count)
        senders = [holder[doc, m] for m in range(neg)]
        key = jnp.concatenate(
            [keys[doc * own + m, :, at] for m in range(own)] + [recv[e, :rows, at] for e in senders], axis=0
        )
        value = jnp.concatenate(
            [values[doc * own + m, :, at] for m in range(own)] + [recv[e, rows:, at] for e in senders], axis=0
        )
        return doc, at, query_rows, key, value

    position = lax.broadcasted_iota(jnp.int32, (total, 1), 0)

    @pl.loop(0, docs * heads, unroll=4)
    def _(step):
        doc, at, query_rows, key, value = place(step)
        valid = (position < counts[doc] * rows) | (position >= own * rows)
        scores = lax.dot_general(key, queries[doc, :, at], NT, preferred_element_type=F32) * scale
        scores = jnp.where(valid, scores, -jnp.inf)
        expo = jnp.exp(scores - jnp.max(scores, axis=0, keepdims=True))
        prob = expo * (1.0 / jnp.sum(expo, axis=0, keepdims=True))
        probs[step] = prob
        attended[query_rows, at] = lax.dot_general(prob.astype(BF16), value, TN, preferred_element_type=F32).astype(BF16)

    out_attended = pltpu.make_async_copy(attended, attended_hbm, out_sem.at[0])
    out_attended.start()

    for j, copies in enumerate(arriving):
        for copy in copies:
            copy.wait()
        term = None
        for c in range(per):
            part = lax.dot_general(
                held[j, :, c * block : (c + 1) * block], weight[j, c], NT, preferred_element_type=F32
            )
            term = part if term is None else term + part
        grad_rows = term if j == 0 else grad_rows + term
    grads[...] = grad_rows.astype(BF16)

    @pl.loop(0, docs * heads, unroll=8)
    def _(step):
        doc, at, query_rows, key, value = place(step)
        grad = grads[query_rows, at]
        prob = probs[step]
        grad_prob = lax.dot_general(value, grad, NT, preferred_element_type=F32)
        delta = jnp.sum(prob * grad_prob, axis=0, keepdims=True)
        grad_score = (prob * (grad_prob - delta)).astype(BF16)
        grad_value = jnp.dot(prob.astype(BF16), grad, preferred_element_type=F32)
        grad_key = jnp.dot(grad_score, queries[doc, :, at], preferred_element_type=F32) * scale
        grad_query[doc, :, at] = (lax.dot_general(grad_score, key, TN, preferred_element_type=F32) * scale).astype(BF16)
        for m in range(own):
            here = slice(m * rows, (m + 1) * rows)
            own_rows[0, doc * own + m, :, at] = grad_key[here]
            own_rows[1, doc * own + m, :, at] = grad_value[here]
        for m in range(neg):
            here = slice((own + m) * rows, (own + m + 1) * rows)
            slots[doc * neg + m, :rows, at] = grad_key[here].astype(BF16)
            slots[doc * neg + m, rows:, at] = grad_value[here].astype(BF16)

        @pl.when(lax.rem(step, heads) == heads - 1)
        def _():
            for m in range(neg):
                entry = doc * neg + m
                pltpu.make_async_copy(slots.at[entry], slots_hbm.at[holder[doc, m]], slot_sem.at[entry]).start()
            span = pl.ds(doc * own, own)
            pltpu.make_async_copy(own_rows.at[:, span], own_rows_hbm.at[:, span], own_sem.at[doc]).start()

    out_query = pltpu.make_async_copy(grad_query, grad_query_hbm, out_sem.at[1])
    out_query.start()
    for doc in range(docs):
        for m in range(neg):
            entry = doc * neg + m
            pltpu.make_async_copy(slots.at[entry], slots_hbm.at[holder[doc, m]], slot_sem.at[entry]).wait()
        span = pl.ds(doc * own, own)
        pltpu.make_async_copy(own_rows.at[:, span], own_rows_hbm.at[:, span], own_sem.at[doc]).wait()
    out_attended.wait()
    out_query.wait()


def layer(counts, holder, spot, queries, keys, values, recv, weight, held):
    docs, query_count, features = queries.shape
    entries, groups = holder.shape[0] * holder.shape[1], len(held)
    rows, columns = held[0].shape
    dma = pltpu.SemaphoreType.DMA
    return pl.pallas_call(
        layer_kernel,
        out_shape=[
            pltpu.HBM((rows, features), BF16),
            pltpu.HBM(queries.shape, BF16),
            pltpu.HBM((2, *keys.shape), F32),
            pltpu.HBM(recv.shape, BF16),
        ],
        in_specs=[SMEM] * 3 + [VMEM] * 4 + [HBM] * (1 + groups),
        out_specs=[HBM] * 4,
        scratch_shapes=[
            pltpu.VMEM((groups, weight.shape[0] // groups, *weight.shape[1:]), BF16),
            pltpu.VMEM((groups, rows, columns), BF16),
            pltpu.VMEM((rows, features), BF16),
            pltpu.VMEM((docs * features // HD, (keys.shape[0] // docs + holder.shape[1]) * keys.shape[1], query_count), F32),
            pltpu.VMEM((rows, features), BF16),
            pltpu.VMEM(queries.shape, BF16),
            pltpu.VMEM((2, *keys.shape), F32),
            pltpu.VMEM((entries, *recv.shape[1:]), BF16),
            dma((groups,)),
            dma((groups,)),
            dma((2,)),
            dma((docs,)),
            dma((entries,)),
        ],
        compiler_params=PARAMS,
        cost_estimate=cost(5 * 2**30, 16 * 2**20),
        name="layer",
    )(counts, holder, spot, queries, keys, values, recv, in_hbm(weight), *map(in_hbm, held))


def project_kernel(spot, weight_hbm, attended_hbm, out0, out1, out2, out3, weight, attended, sem, in_sem):
    groups, per, _, block = weight.shape
    outs = (out0, out1, out2, out3)
    in_attended = pltpu.make_async_copy(attended_hbm, attended, in_sem)
    in_attended.start()
    copies = []
    for j in range(groups):
        first = lax.rem(spot[0] + j, groups) * per
        copies.append(pltpu.make_async_copy(weight_hbm.at[pl.ds(first, per)], weight.at[j], sem.at[j]))
        copies[j].start()
    in_attended.wait()
    for j, out in enumerate(outs):
        copies[j].wait()
        for c in range(per):
            term = jnp.dot(attended[...], weight[j, c], preferred_element_type=F32)
            out[:, c * block : (c + 1) * block] = term.astype(BF16)


def projected(spot, weight, attended, groups):
    per = weight.shape[0] // groups
    shape = jax.ShapeDtypeStruct((attended.shape[0], per * weight.shape[2]), BF16)
    return pl.pallas_call(
        project_kernel,
        out_shape=[shape] * groups,
        in_specs=[SMEM, HBM, HBM],
        out_specs=[VMEM] * groups,
        scratch_shapes=[
            pltpu.VMEM((groups, per, *weight.shape[1:]), BF16),
            pltpu.VMEM(attended.shape, BF16),
            pltpu.SemaphoreType.DMA((groups,)),
            pltpu.SemaphoreType.DMA,
        ],
        compiler_params=PARAMS,
        cost_estimate=cost(2 * 2**30, 8 * 2**20),
        name="projection",
    )(spot, in_hbm(weight), in_hbm(attended))


def combine_kernel(asked, own_rows_hbm, back, key_grads_hbm, value_grads_hbm, own_rows, total, grads, in_sem, out_sem):
    rows = own_rows.shape[2]
    arriving = [pltpu.make_async_copy(own_rows_hbm.at[i], own_rows.at[i], in_sem.at[i]) for i in range(2)]
    for copy in arriving:
        copy.start()

    @pl.loop(0, total.shape[1])
    def _(block):
        total[:, block] = jnp.zeros_like(total[:, block])

    @pl.loop(0, back.shape[0])
    def _(slot):
        spot = asked[slot, 0]

        @pl.when(spot >= 0)
        def _():
            total[0, spot] += back[slot, :rows, :].astype(F32)
            total[1, spot] += back[slot, rows:, :].astype(F32)

    outgoing = []
    for i, target in enumerate((key_grads_hbm, value_grads_hbm)):
        arriving[i].wait()

        @pl.loop(0, total.shape[1])
        def _(block, i=i):
            grads[i, block] = (own_rows[i, block] + total[i, block]).astype(BF16)

        outgoing.append(pltpu.make_async_copy(grads.at[i], target, out_sem.at[i]))
        outgoing[i].start()
    for copy in outgoing:
        copy.wait()


def combined(asked, own_rows, back):
    shape = pltpu.HBM(own_rows.shape[1:], BF16)
    return pl.pallas_call(
        combine_kernel,
        out_shape=[shape, shape],
        in_specs=[SMEM, HBM, VMEM],
        out_specs=[HBM, HBM],
        scratch_shapes=[
            pltpu.VMEM(own_rows.shape, F32),
            pltpu.VMEM(own_rows.shape, F32),
            pltpu.VMEM(own_rows.shape, BF16),
            pltpu.SemaphoreType.DMA((2,)),
            pltpu.SemaphoreType.DMA((2,)),
        ],
        compiler_params=PARAMS,
        cost_estimate=cost(0, 4 * 2**20),
        name="combine",
    )(asked, in_hbm(own_rows), back)


def on_device(sent_queries, mem_keys, mem_values, out_weight, sent_grads, counts, neg_ids):
    keys, values = mem_keys[0], mem_values[0]
    mem_count = keys.shape[0]
    groups = lax.axis_size("dp")
    tensor = lax.axis_size("tensor")
    tensor_spot = lax.axis_index("tensor").astype(jnp.int32).reshape(1)

    holder = neg_ids // mem_count
    spot = neg_ids - holder * mem_count
    named = holder[None] == jnp.arange(groups, dtype=jnp.int32)[:, None, None]
    request = jnp.sum(jnp.where(named, spot[None] + 1, 0), axis=(1, 2)) - 1
    asked = exchanged(request.reshape(groups, 1))

    queries = passed_along(sent_queries, "section", 1)[0]
    grads = passed_along(sent_grads, "section", -1)[0]
    docs, query_count, features = queries.shape
    weight = lax.all_gather(out_weight[0], "dp")

    recv = exchanged(picked_slots(asked, keys, values))

    grad_rows = grads.reshape(docs * query_count, grads.shape[2])
    held = [grad_rows] + [passed_along(grad_rows, "tensor", -j) for j in range(1, tensor)]
    attended, query_grads, own_rows, slots = layer(
        counts, holder, tensor_spot, queries, keys, values, recv, weight, held
    )
    back = exchanged(slots)
    terms = projected(tensor_spot, weight, attended, tensor)
    arrived = [terms[0]] + [passed_along(terms[j], "tensor", j) for j in range(1, tensor)]
    mixed = sum(term.astype(F32) for term in arrived).astype(BF16).reshape(1, docs, query_count, -1)

    key_grads, value_grads = combined(asked, own_rows, back)
    return mixed, query_grads[None], key_grads[None], value_grads[None]


def solution(mesh):
    rows = P("section", "dp", None, "tensor")
    return jax.shard_map(
        on_device,
        mesh=mesh,
        in_specs=(rows, rows, rows, P("section", "tensor", "dp"), rows, P("dp"), P("dp", None)),
        out_specs=(rows, rows, rows, rows),
        check_vma=False,
    )
```

```python
import jax
import jax.numpy as jnp
from jax import lax
from jax.experimental import pallas as pl
from jax.experimental.pallas import tpu as pltpu
from jax.sharding import PartitionSpec as P

HD = 128
OFFSETS = (0, -1, 1, -2, 2, -3, 3, 4)
F32 = jnp.float32
BF16 = jnp.bfloat16
NT = (((1,), (1,)), ((), ()))
TN = (((0,), (0,)), ((), ()))
VMEM = pl.BlockSpec(memory_space=pltpu.VMEM)
HBM = pl.BlockSpec(memory_space=pltpu.HBM)
ANY = pl.BlockSpec(memory_space=pl.ANY)
SMEM = pl.BlockSpec(memory_space=pltpu.SMEM)
PARAMS = pltpu.CompilerParams(vmem_limit_bytes=20 * 1024 * 1024)


def passed_along(block, axis, distance):
    count = lax.axis_size(axis)
    return lax.ppermute(block, axis, [(i, (i + distance) % count) for i in range(count)])


def exchanged(slots):
    return lax.all_to_all(slots, "dp", split_axis=0, concat_axis=0, tiled=True)


def in_hbm(array):
    return pltpu.with_memory_space_constraint(array, pltpu.HBM)


def cost(flops, nbytes):
    return pl.CostEstimate(flops=int(flops), bytes_accessed=int(nbytes), transcendentals=0)


def pick_kernel(asked, keys_hbm, values_hbm, slots, keys, values, in_sem, out_sem):
    rows = keys.shape[1]
    in_key = pltpu.make_async_copy(keys_hbm, keys, in_sem.at[0])
    in_value = pltpu.make_async_copy(values_hbm, values, in_sem.at[1])
    in_key.start()
    in_value.start()

    def sent(slot, which, source):
        target = slots.at[slot, pl.ds(which * rows, rows)]
        return pltpu.make_async_copy(source.at[jnp.maximum(asked[slot, 0], 0)], target, out_sem.at[slot, which])

    for which, (arriving, source) in enumerate(((in_key, keys), (in_value, values))):
        arriving.wait()

        @pl.loop(0, slots.shape[0])
        def _(slot, which=which, source=source):
            copy = sent(slot, which, source)
            pl.when(asked[slot, 0] >= 0)(copy.start)

    @pl.loop(0, slots.shape[0])
    def _(slot):
        for which, source in enumerate((keys, values)):
            pl.when(asked[slot, 0] >= 0)(sent(slot, which, source).wait)


def picked_slots(asked, keys, values):
    slot_count = asked.shape[0]
    _, rows, features = keys.shape
    return pl.pallas_call(
        pick_kernel,
        out_shape=pltpu.HBM((slot_count, 2 * rows, features), BF16),
        in_specs=[SMEM, HBM, HBM],
        out_specs=HBM,
        scratch_shapes=[
            pltpu.VMEM(keys.shape, BF16),
            pltpu.VMEM(values.shape, BF16),
            pltpu.SemaphoreType.DMA((2,)),
            pltpu.SemaphoreType.DMA((slot_count, 2)),
        ],
        compiler_params=PARAMS,
        cost_estimate=cost(0, 4 * 2**20),
        name="pick_blocks",
    )(asked, in_hbm(keys), in_hbm(values))


def layer_kernel(
    counts, holder, queries, keys, values, recv, grads,
    attended_hbm, grad_query_hbm, own_rows_hbm, slots_hbm,
    attended, grad_query, own_rows, slots, out_sem, own_sem, slot_sem,
):
    docs, query_count, _ = queries.shape
    mem_count, rows, features = keys.shape
    own = mem_count // docs
    neg = holder.shape[1]
    heads = features // HD
    scale = HD**-0.5
    total = (own + neg) * rows

    def place(step):
        doc, head = step // heads, lax.rem(step, heads)
        at = pl.ds(pl.multiple_of(head * HD, HD), HD)
        query_rows = pl.ds(pl.multiple_of(doc * query_count, query_count), query_count)
        senders = [holder[doc, m] for m in range(neg)]
        key = jnp.concatenate(
            [keys[doc * own + m, :, at] for m in range(own)] + [recv[e, :rows, at] for e in senders], axis=0
        )
        value = jnp.concatenate(
            [values[doc * own + m, :, at] for m in range(own)] + [recv[e, rows:, at] for e in senders], axis=0
        )
        return doc, at, query_rows, key, value

    position = lax.broadcasted_iota(jnp.int32, (total, 1), 0)

    @pl.loop(0, docs * heads, unroll=4)
    def _(step):
        doc, at, query_rows, key, value = place(step)
        valid = (position < counts[doc] * rows) | (position >= own * rows)
        scores = lax.dot_general(key, queries[doc, :, at], NT, preferred_element_type=F32) * scale
        scores = jnp.where(valid, scores, -jnp.inf)
        expo = jnp.exp(scores - jnp.max(scores, axis=0, keepdims=True))
        prob = expo * (1.0 / jnp.sum(expo, axis=0, keepdims=True))
        attended[query_rows, at] = lax.dot_general(prob.astype(BF16), value, TN, preferred_element_type=F32).astype(BF16)
        grad = grads[query_rows, at]
        grad_prob = lax.dot_general(value, grad, NT, preferred_element_type=F32)
        delta = jnp.sum(prob * grad_prob, axis=0, keepdims=True)
        grad_score = (prob * (grad_prob - delta)).astype(BF16)
        grad_value = jnp.dot(prob.astype(BF16), grad, preferred_element_type=F32)
        grad_key = jnp.dot(grad_score, queries[doc, :, at], preferred_element_type=F32) * scale
        grad_query[doc, :, at] = (lax.dot_general(grad_score, key, TN, preferred_element_type=F32) * scale).astype(BF16)
        for m in range(own):
            here = slice(m * rows, (m + 1) * rows)
            own_rows[0, doc * own + m, :, at] = grad_key[here]
            own_rows[1, doc * own + m, :, at] = grad_value[here]
        for m in range(neg):
            here = slice((own + m) * rows, (own + m + 1) * rows)
            slots[doc * neg + m, :rows, at] = grad_key[here].astype(BF16)
            slots[doc * neg + m, rows:, at] = grad_value[here].astype(BF16)

        @pl.when(lax.rem(step, heads) == heads - 1)
        def _():
            for m in range(neg):
                entry = doc * neg + m
                pltpu.make_async_copy(slots.at[entry], slots_hbm.at[holder[doc, m]], slot_sem.at[entry]).start()
            span = pl.ds(doc * own, own)
            pltpu.make_async_copy(own_rows.at[:, span], own_rows_hbm.at[:, span], own_sem.at[doc]).start()

    out_attended = pltpu.make_async_copy(attended, attended_hbm, out_sem.at[0])
    out_attended.start()
    out_query = pltpu.make_async_copy(grad_query, grad_query_hbm, out_sem.at[1])
    out_query.start()
    for doc in range(docs):
        for m in range(neg):
            entry = doc * neg + m
            pltpu.make_async_copy(slots.at[entry], slots_hbm.at[holder[doc, m]], slot_sem.at[entry]).wait()
        span = pl.ds(doc * own, own)
        pltpu.make_async_copy(own_rows.at[:, span], own_rows_hbm.at[:, span], own_sem.at[doc]).wait()
    out_attended.wait()
    out_query.wait()


def layer(counts, holder, queries, keys, values, recv, grads):
    docs, _, features = queries.shape
    entries = holder.shape[0] * holder.shape[1]
    rows = grads.shape[0]
    dma = pltpu.SemaphoreType.DMA
    return pl.pallas_call(
        layer_kernel,
        out_shape=[
            pltpu.HBM((rows, features), BF16),
            pltpu.HBM(queries.shape, BF16),
            pltpu.HBM((2, *keys.shape), F32),
            pltpu.HBM(recv.shape, BF16),
        ],
        in_specs=[SMEM] * 2 + [VMEM] * 5,
        out_specs=[HBM] * 4,
        scratch_shapes=[
            pltpu.VMEM((rows, features), BF16),
            pltpu.VMEM(queries.shape, BF16),
            pltpu.VMEM((2, *keys.shape), F32),
            pltpu.VMEM((entries, *recv.shape[1:]), BF16),
            dma((2,)),
            dma((docs,)),
            dma((entries,)),
        ],
        compiler_params=PARAMS,
        cost_estimate=cost(4 * 2**30, 12 * 2**20),
        name="layer",
    )(counts, holder, queries, keys, values, recv, grads)


def copies_in(pairs, sem):
    copies = [pltpu.make_async_copy(source, target, sem.at[i]) for i, (source, target) in enumerate(pairs)]
    for copy in copies:
        copy.start()
    return copies


def placed(spots, step, per, groups):
    chips = len(OFFSETS)
    kind, k = step // chips, lax.rem(step, chips)
    offset = jnp.int32(0)
    for i, value in enumerate(OFFSETS):
        offset = jnp.where(k == i, value, offset)
    own = spots[0] + kind * (1 - 2 * lax.rem(spots[0], 2))
    block = lax.rem(own + 2 * offset + 2 * chips, 2 * chips)
    return lax.rem(block // per + groups - spots[1], groups), lax.rem(block, per)


def back_kernel(spots, own_hbm, other_hbm, grad0, grad1, grad2, grad3, out_hbm, weight, held, total, out, weight_sem, held_sem):
    groups, rows, columns = held.shape
    chips, _, block = own_hbm.shape
    per = columns // block
    waiting = copies_in([(ref, held.at[j]) for j, ref in enumerate((grad0, grad1, grad2, grad3))], held_sem)
    waiting += copies_in([(ref, weight.at[pl.ds(i * chips, chips)]) for i, ref in enumerate((own_hbm, other_hbm))], weight_sem)
    for copy in waiting:
        copy.wait()
    total[...] = jnp.zeros_like(total)

    @pl.loop(0, 2 * chips)
    def _(step):
        group, place = placed(spots, step, per, groups)
        at = pl.ds(pl.multiple_of(place * block, block), block)
        total[...] += lax.dot_general(held[group, :, at], weight[step], NT, preferred_element_type=F32)

    out[...] = total[...].astype(BF16)
    pltpu.sync_copy(out, out_hbm)


def back_projected(spots, own, other, held):
    groups = len(held)
    rows, columns = held[0].shape
    _, features, block = own.shape
    return pl.pallas_call(
        back_kernel,
        out_shape=pltpu.HBM((rows, features), BF16),
        in_specs=[SMEM] + [HBM] * (2 + groups),
        out_specs=HBM,
        scratch_shapes=[
            pltpu.VMEM((2 * own.shape[0], features, block), BF16),
            pltpu.VMEM((groups, rows, columns), BF16),
            pltpu.VMEM((rows, features), F32),
            pltpu.VMEM((rows, features), BF16),
            pltpu.SemaphoreType.DMA((2,)),
            pltpu.SemaphoreType.DMA((groups,)),
        ],
        compiler_params=PARAMS,
        cost_estimate=cost(2 * 2**30, 8 * 2**20),
        name="back_projection",
    )(spots, in_hbm(own), in_hbm(other), *map(in_hbm, held))


def project_kernel(spots, own_hbm, other_hbm, attended_hbm, out0, out1, out2, out3, weight, attended, terms, weight_sem, in_sem):
    groups, _, columns = terms.shape
    chips, _, block = own_hbm.shape
    per = columns // block
    waiting = copies_in([(attended_hbm, attended)], in_sem)
    waiting += copies_in([(ref, weight.at[pl.ds(i * chips, chips)]) for i, ref in enumerate((own_hbm, other_hbm))], weight_sem)
    for copy in waiting:
        copy.wait()

    @pl.loop(0, 2 * chips)
    def _(step):
        group, place = placed(spots, step, per, groups)
        at = pl.ds(pl.multiple_of(place * block, block), block)
        terms[group, :, at] = jnp.dot(attended[...], weight[step], preferred_element_type=F32).astype(BF16)

    for j, out in enumerate((out0, out1, out2, out3)):
        out[...] = terms[j]


def projected(spots, own, other, attended, groups):
    chips, features, block = own.shape
    rows, columns = attended.shape[0], 2 * chips * block // groups
    shape = jax.ShapeDtypeStruct((rows, columns), BF16)
    return pl.pallas_call(
        project_kernel,
        out_shape=[shape] * groups,
        in_specs=[SMEM] + [HBM] * 3,
        out_specs=[VMEM] * groups,
        scratch_shapes=[
            pltpu.VMEM((2 * chips, features, block), BF16),
            pltpu.VMEM(attended.shape, BF16),
            pltpu.VMEM((groups, rows, columns), BF16),
            pltpu.SemaphoreType.DMA((2,)),
            pltpu.SemaphoreType.DMA((1,)),
        ],
        compiler_params=PARAMS,
        cost_estimate=cost(2 * 2**30, 8 * 2**20),
        name="projection",
    )(spots, in_hbm(own), in_hbm(other), in_hbm(attended))


def combine_kernel(asked, own_rows_hbm, back, key_grads_hbm, value_grads_hbm, own_rows, total, grads, in_sem, out_sem):
    rows = own_rows.shape[2]
    arriving = [pltpu.make_async_copy(own_rows_hbm.at[i], own_rows.at[i], in_sem.at[i]) for i in range(2)]
    for copy in arriving:
        copy.start()

    @pl.loop(0, total.shape[1])
    def _(block):
        total[:, block] = jnp.zeros_like(total[:, block])

    @pl.loop(0, back.shape[0])
    def _(slot):
        spot = asked[slot, 0]

        @pl.when(spot >= 0)
        def _():
            total[0, spot] += back[slot, :rows, :].astype(F32)
            total[1, spot] += back[slot, rows:, :].astype(F32)

    outgoing = []
    for i, target in enumerate((key_grads_hbm, value_grads_hbm)):
        arriving[i].wait()

        @pl.loop(0, total.shape[1])
        def _(block, i=i):
            grads[i, block] = (own_rows[i, block] + total[i, block]).astype(BF16)

        outgoing.append(pltpu.make_async_copy(grads.at[i], target, out_sem.at[i]))
        outgoing[i].start()
    for copy in outgoing:
        copy.wait()


def combined(asked, own_rows, back):
    shape = pltpu.HBM(own_rows.shape[1:], BF16)
    return pl.pallas_call(
        combine_kernel,
        out_shape=[shape, shape],
        in_specs=[SMEM, HBM, VMEM],
        out_specs=[HBM, HBM],
        scratch_shapes=[
            pltpu.VMEM(own_rows.shape, F32),
            pltpu.VMEM(own_rows.shape, F32),
            pltpu.VMEM(own_rows.shape, BF16),
            pltpu.SemaphoreType.DMA((2,)),
            pltpu.SemaphoreType.DMA((2,)),
        ],
        compiler_params=PARAMS,
        cost_estimate=cost(0, 4 * 2**20),
        name="combine",
    )(asked, in_hbm(own_rows), back)


def on_device(sent_queries, mem_keys, mem_values, out_weight, sent_grads, counts, neg_ids):
    keys, values = mem_keys[0], mem_values[0]
    mem_count = keys.shape[0]
    groups = lax.axis_size("dp")
    tensor = lax.axis_size("tensor")
    spots = jnp.stack([lax.axis_index("dp"), lax.axis_index("tensor")]).astype(jnp.int32)

    holder = neg_ids // mem_count
    spot = neg_ids - holder * mem_count
    named = holder[None] == jnp.arange(groups, dtype=jnp.int32)[:, None, None]
    request = jnp.sum(jnp.where(named, spot[None] + 1, 0), axis=(1, 2)) - 1
    asked = exchanged(request.reshape(groups, 1))

    weight = out_weight[0]
    half = weight.shape[0] // 2
    below, above = passed_along(weight, "dp", 2), passed_along(weight, "dp", -2)
    below2, above2 = passed_along(weight, "dp", 4), passed_along(weight, "dp", -4)
    below2, above2, asked = lax.optimization_barrier((below2, above2, asked))
    below3, above3 = passed_along(below2, "dp", 2), passed_along(above2, "dp", -2)
    far_low, far_high = passed_along(below2[:half], "dp", 4), passed_along(above2[half:], "dp", -4)
    slots = picked_slots(asked, keys, values)
    slots, below3, above3, far_low, far_high = lax.optimization_barrier((slots, below3, above3, far_low, far_high))
    recv = exchanged(slots)

    own_kind = jnp.stack([weight, below, above, below2, above2, below3, above3, jnp.concatenate([far_low, far_high])])
    other_kind = lax.ppermute(own_kind, "dp", [(i, i ^ 1) for i in range(groups)])

    queries = passed_along(sent_queries, "section", 1)[0]
    grads = passed_along(sent_grads, "section", -1)[0]
    docs, query_count, features = queries.shape
    grad_rows = grads.reshape(docs * query_count, grads.shape[2])
    held = [grad_rows] + [passed_along(grad_rows, "tensor", -j) for j in range(1, tensor)]
    grad_attended = back_projected(spots, own_kind, other_kind, held)

    attended, query_grads, own_rows, slots = layer(counts, holder, queries, keys, values, recv, grad_attended)
    back = exchanged(slots)
    terms = projected(spots, own_kind, other_kind, attended, tensor)
    arrived = [terms[0]] + [passed_along(terms[j], "tensor", j) for j in range(1, tensor)]
    mixed = sum(term.astype(F32) for term in arrived).astype(BF16).reshape(1, docs, query_count, -1)

    key_grads, value_grads = combined(asked, own_rows, back)
    return mixed, query_grads[None], key_grads[None], value_grads[None]


def solution(mesh):
    rows = P("section", "dp", None, "tensor")
    return jax.shard_map(
        on_device,
        mesh=mesh,
        in_specs=(rows, rows, rows, P("section", "tensor", "dp"), rows, P("dp"), P("dp", None)),
        out_specs=(rows, rows, rows, rows),
        check_vma=False,
    )
```

```python
import jax
import jax.numpy as jnp
from jax import lax
from jax.experimental import pallas as pl
from jax.experimental.pallas import tpu as pltpu
from jax.sharding import PartitionSpec as P

HD = 128
DELTAS = (0, 1, -2, -1, -4, -3, -6, -5, -8, 3, 2, 5, 4, 7, 6, 9)
F32 = jnp.float32
BF16 = jnp.bfloat16
NT = (((1,), (1,)), ((), ()))
TN = (((0,), (0,)), ((), ()))
VMEM = pl.BlockSpec(memory_space=pltpu.VMEM)
HBM = pl.BlockSpec(memory_space=pltpu.HBM)
ANY = pl.BlockSpec(memory_space=pl.ANY)
SMEM = pl.BlockSpec(memory_space=pltpu.SMEM)
PARAMS = pltpu.CompilerParams(vmem_limit_bytes=20 * 1024 * 1024)


def passed_along(block, axis, distance):
    count = lax.axis_size(axis)
    return lax.ppermute(block, axis, [(i, (i + distance) % count) for i in range(count)])


def swapped(block):
    return lax.ppermute(block, "dp", [(i, i ^ 1) for i in range(lax.axis_size("dp"))])


def along_ring(block, chips):
    count = lax.axis_size("dp")
    return lax.ppermute(block, "dp", [(i, (i + (1 - i % 2 * 2) * 2 * chips) % count) for i in range(count)])


def exchanged(slots):
    return lax.all_to_all(slots, "dp", split_axis=0, concat_axis=0, tiled=True)


def in_hbm(array):
    return pltpu.with_memory_space_constraint(array, pltpu.HBM)


def cost(flops, nbytes):
    return pl.CostEstimate(flops=int(flops), bytes_accessed=int(nbytes), transcendentals=0)


def pick_kernel(asked, keys_hbm, values_hbm, slots, keys, values, in_sem, out_sem):
    rows = keys.shape[1]
    in_key = pltpu.make_async_copy(keys_hbm, keys, in_sem.at[0])
    in_value = pltpu.make_async_copy(values_hbm, values, in_sem.at[1])
    in_key.start()
    in_value.start()

    def sent(slot, which, source):
        target = slots.at[slot, pl.ds(which * rows, rows)]
        return pltpu.make_async_copy(source.at[jnp.maximum(asked[slot, 0], 0)], target, out_sem.at[slot, which])

    for which, (arriving, source) in enumerate(((in_key, keys), (in_value, values))):
        arriving.wait()

        @pl.loop(0, slots.shape[0])
        def _(slot, which=which, source=source):
            copy = sent(slot, which, source)
            pl.when(asked[slot, 0] >= 0)(copy.start)

    @pl.loop(0, slots.shape[0])
    def _(slot):
        for which, source in enumerate((keys, values)):
            pl.when(asked[slot, 0] >= 0)(sent(slot, which, source).wait)


def picked_slots(asked, keys, values):
    slot_count = asked.shape[0]
    _, rows, features = keys.shape
    return pl.pallas_call(
        pick_kernel,
        out_shape=pltpu.HBM((slot_count, 2 * rows, features), BF16),
        in_specs=[SMEM, HBM, HBM],
        out_specs=HBM,
        scratch_shapes=[
            pltpu.VMEM(keys.shape, BF16),
            pltpu.VMEM(values.shape, BF16),
            pltpu.SemaphoreType.DMA((2,)),
            pltpu.SemaphoreType.DMA((slot_count, 2)),
        ],
        compiler_params=PARAMS,
        cost_estimate=cost(0, 4 * 2**20),
        name="pick_blocks",
    )(asked, in_hbm(keys), in_hbm(values))


def layer_kernel(
    counts, holder, queries, keys, values, recv, grads,
    attended_hbm, grad_query_hbm, own_rows_hbm, slots_hbm,
    attended, grad_query, own_rows, slots, out_sem, own_sem, slot_sem,
):
    docs, query_count, _ = queries.shape
    mem_count, rows, features = keys.shape
    own = mem_count // docs
    neg = holder.shape[1]
    heads = features // HD
    scale = HD**-0.5
    total = (own + neg) * rows

    def place(step):
        doc, head = step // heads, lax.rem(step, heads)
        at = pl.ds(pl.multiple_of(head * HD, HD), HD)
        query_rows = pl.ds(pl.multiple_of(doc * query_count, query_count), query_count)
        senders = [holder[doc, m] for m in range(neg)]
        key = jnp.concatenate(
            [keys[doc * own + m, :, at] for m in range(own)] + [recv[e, :rows, at] for e in senders], axis=0
        )
        value = jnp.concatenate(
            [values[doc * own + m, :, at] for m in range(own)] + [recv[e, rows:, at] for e in senders], axis=0
        )
        return doc, at, query_rows, key, value

    position = lax.broadcasted_iota(jnp.int32, (total, 1), 0)

    @pl.loop(0, docs * heads, unroll=4)
    def _(step):
        doc, at, query_rows, key, value = place(step)
        valid = (position < counts[doc] * rows) | (position >= own * rows)
        scores = lax.dot_general(key, queries[doc, :, at], NT, preferred_element_type=F32) * scale
        scores = jnp.where(valid, scores, -jnp.inf)
        expo = jnp.exp(scores - jnp.max(scores, axis=0, keepdims=True))
        prob = expo * (1.0 / jnp.sum(expo, axis=0, keepdims=True))
        attended[query_rows, at] = lax.dot_general(prob.astype(BF16), value, TN, preferred_element_type=F32).astype(BF16)
        grad = grads[query_rows, at]
        grad_prob = lax.dot_general(value, grad, NT, preferred_element_type=F32)
        delta = jnp.sum(prob * grad_prob, axis=0, keepdims=True)
        grad_score = (prob * (grad_prob - delta)).astype(BF16)
        grad_value = jnp.dot(prob.astype(BF16), grad, preferred_element_type=F32)
        grad_key = jnp.dot(grad_score, queries[doc, :, at], preferred_element_type=F32) * scale
        grad_query[doc, :, at] = (lax.dot_general(grad_score, key, TN, preferred_element_type=F32) * scale).astype(BF16)
        for m in range(own):
            here = slice(m * rows, (m + 1) * rows)
            own_rows[0, doc * own + m, :, at] = grad_key[here]
            own_rows[1, doc * own + m, :, at] = grad_value[here]
        for m in range(neg):
            here = slice((own + m) * rows, (own + m + 1) * rows)
            slots[doc * neg + m, :rows, at] = grad_key[here].astype(BF16)
            slots[doc * neg + m, rows:, at] = grad_value[here].astype(BF16)

        @pl.when(lax.rem(step, heads) == heads - 1)
        def _():
            for m in range(neg):
                entry = doc * neg + m
                pltpu.make_async_copy(slots.at[entry], slots_hbm.at[holder[doc, m]], slot_sem.at[entry]).start()
            span = pl.ds(doc * own, own)
            pltpu.make_async_copy(own_rows.at[:, span], own_rows_hbm.at[:, span], own_sem.at[doc]).start()

    out_attended = pltpu.make_async_copy(attended, attended_hbm, out_sem.at[0])
    out_attended.start()
    out_query = pltpu.make_async_copy(grad_query, grad_query_hbm, out_sem.at[1])
    out_query.start()
    for doc in range(docs):
        for m in range(neg):
            entry = doc * neg + m
            pltpu.make_async_copy(slots.at[entry], slots_hbm.at[holder[doc, m]], slot_sem.at[entry]).wait()
        span = pl.ds(doc * own, own)
        pltpu.make_async_copy(own_rows.at[:, span], own_rows_hbm.at[:, span], own_sem.at[doc]).wait()
    out_attended.wait()
    out_query.wait()


def layer(counts, holder, queries, keys, values, recv, grads):
    docs, _, features = queries.shape
    entries = holder.shape[0] * holder.shape[1]
    rows = grads.shape[0]
    dma = pltpu.SemaphoreType.DMA
    return pl.pallas_call(
        layer_kernel,
        out_shape=[
            pltpu.HBM((rows, features), BF16),
            pltpu.HBM(queries.shape, BF16),
            pltpu.HBM((2, *keys.shape), F32),
            pltpu.HBM(recv.shape, BF16),
        ],
        in_specs=[SMEM] * 2 + [VMEM] * 5,
        out_specs=[HBM] * 4,
        scratch_shapes=[
            pltpu.VMEM((rows, features), BF16),
            pltpu.VMEM(queries.shape, BF16),
            pltpu.VMEM((2, *keys.shape), F32),
            pltpu.VMEM((entries, *recv.shape[1:]), BF16),
            dma((2,)),
            dma((docs,)),
            dma((entries,)),
        ],
        compiler_params=PARAMS,
        cost_estimate=cost(4 * 2**30, 12 * 2**20),
        name="layer",
    )(counts, holder, queries, keys, values, recv, grads)


def copies_in(pairs, sem):
    copies = [pltpu.make_async_copy(source, target, sem.at[i]) for i, (source, target) in enumerate(pairs)]
    for copy in copies:
        copy.start()
    return copies


def weight_copies(refs, weight, sem):
    first, pairs = 0, []
    for ref in refs:
        count = ref.shape[0] // weight.shape[1]
        for i in range(count):
            pairs.append((ref.at[pl.ds(i * weight.shape[1], weight.shape[1])], weight.at[first + i]))
        first += count
    return copies_in(pairs, sem)


def back_kernel(table, grad0, grad1, grad2, grad3, *refs):
    *blocks, out_hbm, weight, held, total, out, weight_sem, held_sem = refs
    block = weight.shape[2]
    waiting = copies_in([(ref, held.at[j]) for j, ref in enumerate((grad0, grad1, grad2, grad3))], held_sem)
    waiting += weight_copies(blocks, weight, weight_sem)
    for copy in waiting:
        copy.wait()
    total[...] = jnp.zeros_like(total)

    @pl.loop(0, weight.shape[0], unroll=4)
    def _(step):
        at = pl.ds(pl.multiple_of(table[1, step] * block, block), block)
        total[...] += lax.dot_general(held[table[0, step], :, at], weight[step], NT, preferred_element_type=F32)

    out[...] = total[...].astype(BF16)
    pltpu.sync_copy(out, out_hbm)


def back_projected(table, held, blocks):
    groups = len(held)
    rows, columns = held[0].shape
    features, block = blocks[0].shape
    count = table.shape[1]
    return pl.pallas_call(
        back_kernel,
        out_shape=pltpu.HBM((rows, features), BF16),
        in_specs=[SMEM] + [HBM] * (len(blocks) + groups),
        out_specs=HBM,
        scratch_shapes=[
            pltpu.VMEM((count, features, block), BF16),
            pltpu.VMEM((groups, rows, columns), BF16),
            pltpu.VMEM((rows, features), F32),
            pltpu.VMEM((rows, features), BF16),
            pltpu.SemaphoreType.DMA((count,)),
            pltpu.SemaphoreType.DMA((groups,)),
        ],
        compiler_params=PARAMS,
        cost_estimate=cost(2 * 2**30, 8 * 2**20),
        name="back_projection",
    )(table, *map(in_hbm, held), *map(in_hbm, blocks))


def project_kernel(table, attended_hbm, *refs):
    *blocks, out0, out1, out2, out3, weight, attended, terms, weight_sem, in_sem = refs
    block = weight.shape[2]
    waiting = copies_in([(attended_hbm, attended)], in_sem) + weight_copies(blocks, weight, weight_sem)
    for copy in waiting:
        copy.wait()

    @pl.loop(0, weight.shape[0], unroll=4)
    def _(step):
        at = pl.ds(pl.multiple_of(table[1, step] * block, block), block)
        terms[table[0, step], :, at] = jnp.dot(attended[...], weight[step], preferred_element_type=F32).astype(BF16)

    for j, out in enumerate((out0, out1, out2, out3)):
        out[...] = terms[j]


def projected(table, attended, blocks, groups):
    features, block = blocks[0].shape
    rows, count = attended.shape[0], table.shape[1]
    columns = count * block // groups
    return pl.pallas_call(
        project_kernel,
        out_shape=[jax.ShapeDtypeStruct((rows, columns), BF16)] * groups,
        in_specs=[SMEM] + [HBM] * (1 + len(blocks)),
        out_specs=[VMEM] * groups,
        scratch_shapes=[
            pltpu.VMEM((count, features, block), BF16),
            pltpu.VMEM(attended.shape, BF16),
            pltpu.VMEM((groups, rows, columns), BF16),
            pltpu.SemaphoreType.DMA((count,)),
            pltpu.SemaphoreType.DMA((1,)),
        ],
        compiler_params=PARAMS,
        cost_estimate=cost(2 * 2**30, 8 * 2**20),
        name="projection",
    )(table, in_hbm(attended), *map(in_hbm, blocks))


def combine_kernel(asked, own_rows_hbm, back, key_grads_hbm, value_grads_hbm, own_rows, total, grads, in_sem, out_sem):
    rows = own_rows.shape[2]
    arriving = [pltpu.make_async_copy(own_rows_hbm.at[i], own_rows.at[i], in_sem.at[i]) for i in range(2)]
    for copy in arriving:
        copy.start()

    @pl.loop(0, total.shape[1])
    def _(block):
        total[:, block] = jnp.zeros_like(total[:, block])

    @pl.loop(0, back.shape[0])
    def _(slot):
        spot = asked[slot, 0]

        @pl.when(spot >= 0)
        def _():
            total[0, spot] += back[slot, :rows, :].astype(F32)
            total[1, spot] += back[slot, rows:, :].astype(F32)

    outgoing = []
    for i, target in enumerate((key_grads_hbm, value_grads_hbm)):
        arriving[i].wait()

        @pl.loop(0, total.shape[1])
        def _(block, i=i):
            grads[i, block] = (own_rows[i, block] + total[i, block]).astype(BF16)

        outgoing.append(pltpu.make_async_copy(grads.at[i], target, out_sem.at[i]))
        outgoing[i].start()
    for copy in outgoing:
        copy.wait()


def combined(asked, own_rows, back):
    shape = pltpu.HBM(own_rows.shape[1:], BF16)
    return pl.pallas_call(
        combine_kernel,
        out_shape=[shape, shape],
        in_specs=[SMEM, HBM, VMEM],
        out_specs=[HBM, HBM],
        scratch_shapes=[
            pltpu.VMEM(own_rows.shape, F32),
            pltpu.VMEM(own_rows.shape, F32),
            pltpu.VMEM(own_rows.shape, BF16),
            pltpu.SemaphoreType.DMA((2,)),
            pltpu.SemaphoreType.DMA((2,)),
        ],
        compiler_params=PARAMS,
        cost_estimate=cost(0, 4 * 2**20),
        name="combine",
    )(asked, in_hbm(own_rows), back)


def on_device(sent_queries, mem_keys, mem_values, out_weight, sent_grads, counts, neg_ids):
    keys, values = mem_keys[0], mem_values[0]
    mem_count = keys.shape[0]
    groups = lax.axis_size("dp")
    tensor = lax.axis_size("tensor")
    me = lax.axis_index("dp")
    sign = 1 - 2 * lax.rem(me, 2)
    block_of = (me + sign * jnp.array(DELTAS, jnp.int32) + 2 * groups) % groups
    per = groups // tensor
    table = jnp.stack([(block_of // per + tensor - lax.axis_index("tensor")) % tensor, block_of % per]).astype(jnp.int32)

    holder = neg_ids // mem_count
    spot = neg_ids - holder * mem_count
    named = holder[None] == jnp.arange(groups, dtype=jnp.int32)[:, None, None]
    request = jnp.sum(jnp.where(named, spot[None] + 1, 0), axis=(1, 2)) - 1
    asked = exchanged(request.reshape(groups, 1))

    weight = out_weight[0]
    other = swapped(weight)
    pair = jnp.concatenate([weight, other])
    near, next_near = along_ring(pair, 1), along_ring(pair, 2)
    grads = passed_along(sent_grads, "section", -1)[0]
    next_near, asked, grads = lax.optimization_barrier((next_near, asked, grads))
    third, far = along_ring(next_near, 1), along_ring(next_near[: weight.shape[0]], 2)
    slots = picked_slots(asked, keys, values)
    slots, near, third, far = lax.optimization_barrier((slots, near, third, far))
    recv = exchanged(slots)
    blocks = [weight, other, near, next_near, third, far]
    blocks += [swapped(block) for block in blocks[2:]]

    queries = passed_along(sent_queries, "section", 1)[0]
    docs, query_count, features = queries.shape
    grad_rows = grads.reshape(docs * query_count, grads.shape[2])
    held = [grad_rows] + [passed_along(grad_rows, "tensor", -j) for j in range(1, tensor)]
    grad_attended = back_projected(table, held, blocks)

    attended, query_grads, own_rows, slots = layer(counts, holder, queries, keys, values, recv, grad_attended)
    back = exchanged(slots)
    terms = projected(table, attended, blocks, tensor)
    arrived = [terms[0]] + [passed_along(terms[j], "tensor", j) for j in range(1, tensor)]
    mixed = sum(term.astype(F32) for term in arrived).astype(BF16).reshape(1, docs, query_count, -1)

    key_grads, value_grads = combined(asked, own_rows, back)
    return mixed, query_grads[None], key_grads[None], value_grads[None]


def solution(mesh):
    rows = P("section", "dp", None, "tensor")
    return jax.shard_map(
        on_device,
        mesh=mesh,
        in_specs=(rows, rows, rows, P("section", "tensor", "dp"), rows, P("dp"), P("dp", None)),
        out_specs=(rows, rows, rows, rows),
        check_vma=False,
    )
```

```python
import jax
import jax.numpy as jnp
from jax import lax
from jax.experimental import pallas as pl
from jax.experimental.pallas import tpu as pltpu
from jax.sharding import PartitionSpec as P

HD = 128
DELTAS = (0, 1, -2, -1, -4, -3, -6, -5, -8, 3, 2, 5, 4, 7, 6, 9)
F32 = jnp.float32
BF16 = jnp.bfloat16
NT = (((1,), (1,)), ((), ()))
TN = (((0,), (0,)), ((), ()))
VMEM = pl.BlockSpec(memory_space=pltpu.VMEM)
HBM = pl.BlockSpec(memory_space=pltpu.HBM)
ANY = pl.BlockSpec(memory_space=pl.ANY)
SMEM = pl.BlockSpec(memory_space=pltpu.SMEM)
PARAMS = pltpu.CompilerParams(vmem_limit_bytes=20 * 1024 * 1024)


def passed_along(block, axis, distance):
    count = lax.axis_size(axis)
    return lax.ppermute(block, axis, [(i, (i + distance) % count) for i in range(count)])


def swapped(block):
    return lax.ppermute(block, "dp", [(i, i ^ 1) for i in range(lax.axis_size("dp"))])


def along_ring(block, chips):
    count = lax.axis_size("dp")
    return lax.ppermute(block, "dp", [(i, (i + (1 - i % 2 * 2) * 2 * chips) % count) for i in range(count)])


def exchanged(slots):
    return lax.all_to_all(slots, "dp", split_axis=0, concat_axis=0, tiled=True)


def in_hbm(array):
    return pltpu.with_memory_space_constraint(array, pltpu.HBM)


def cost(flops, nbytes):
    return pl.CostEstimate(flops=int(flops), bytes_accessed=int(nbytes), transcendentals=0)


def pick_kernel(asked, keys_hbm, values_hbm, slots, keys, values, in_sem, out_sem):
    rows = keys.shape[1]
    in_key = pltpu.make_async_copy(keys_hbm, keys, in_sem.at[0])
    in_value = pltpu.make_async_copy(values_hbm, values, in_sem.at[1])
    in_key.start()
    in_value.start()

    def sent(slot, which, source):
        target = slots.at[slot, pl.ds(which * rows, rows)]
        return pltpu.make_async_copy(source.at[jnp.maximum(asked[slot, 0], 0)], target, out_sem.at[slot, which])

    for which, (arriving, source) in enumerate(((in_key, keys), (in_value, values))):
        arriving.wait()

        @pl.loop(0, slots.shape[0])
        def _(slot, which=which, source=source):
            copy = sent(slot, which, source)
            pl.when(asked[slot, 0] >= 0)(copy.start)

    @pl.loop(0, slots.shape[0])
    def _(slot):
        for which, source in enumerate((keys, values)):
            pl.when(asked[slot, 0] >= 0)(sent(slot, which, source).wait)


def picked_slots(asked, keys, values):
    slot_count = asked.shape[0]
    _, rows, features = keys.shape
    return pl.pallas_call(
        pick_kernel,
        out_shape=pltpu.HBM((slot_count, 2 * rows, features), BF16),
        in_specs=[SMEM, HBM, HBM],
        out_specs=HBM,
        scratch_shapes=[
            pltpu.VMEM(keys.shape, BF16),
            pltpu.VMEM(values.shape, BF16),
            pltpu.SemaphoreType.DMA((2,)),
            pltpu.SemaphoreType.DMA((slot_count, 2)),
        ],
        compiler_params=PARAMS,
        cost_estimate=cost(0, 4 * 2**20),
        name="pick_blocks",
    )(asked, in_hbm(keys), in_hbm(values))


def layer_kernel(
    counts, holder, queries, keys, values, recv, grads,
    attended_hbm, grad_query_hbm, own_rows_hbm, slots_hbm,
    attended, grad_query, own_rows, slots, out_sem, own_sem, slot_sem,
):
    docs, query_count, _ = queries.shape
    mem_count, rows, features = keys.shape
    own = mem_count // docs
    neg = holder.shape[1]
    heads = features // HD
    scale = HD**-0.5
    total = (own + neg) * rows

    def place(step):
        doc, head = step // heads, lax.rem(step, heads)
        at = pl.ds(pl.multiple_of(head * HD, HD), HD)
        query_rows = pl.ds(pl.multiple_of(doc * query_count, query_count), query_count)
        senders = [holder[doc, m] for m in range(neg)]
        key = jnp.concatenate(
            [keys[doc * own + m, :, at] for m in range(own)] + [recv[e, :rows, at] for e in senders], axis=0
        )
        value = jnp.concatenate(
            [values[doc * own + m, :, at] for m in range(own)] + [recv[e, rows:, at] for e in senders], axis=0
        )
        return doc, at, query_rows, key, value

    position = lax.broadcasted_iota(jnp.int32, (total, 1), 0)

    @pl.loop(0, docs * heads, unroll=4)
    def _(step):
        doc, at, query_rows, key, value = place(step)
        valid = (position < counts[doc] * rows) | (position >= own * rows)
        scores = lax.dot_general(key, queries[doc, :, at], NT, preferred_element_type=F32) * scale
        scores = jnp.where(valid, scores, -jnp.inf)
        expo = jnp.exp(scores - jnp.max(scores, axis=0, keepdims=True))
        prob = expo * (1.0 / jnp.sum(expo, axis=0, keepdims=True))
        attended[query_rows, at] = lax.dot_general(prob.astype(BF16), value, TN, preferred_element_type=F32).astype(BF16)
        grad = grads[query_rows, at]
        grad_prob = lax.dot_general(value, grad, NT, preferred_element_type=F32)
        delta = jnp.sum(prob * grad_prob, axis=0, keepdims=True)
        grad_score = (prob * (grad_prob - delta)).astype(BF16)
        grad_value = jnp.dot(prob.astype(BF16), grad, preferred_element_type=F32)
        grad_key = jnp.dot(grad_score, queries[doc, :, at], preferred_element_type=F32) * scale
        grad_query[doc, :, at] = (lax.dot_general(grad_score, key, TN, preferred_element_type=F32) * scale).astype(BF16)
        for m in range(own):
            here = slice(m * rows, (m + 1) * rows)
            own_rows[0, doc * own + m, :, at] = grad_key[here]
            own_rows[1, doc * own + m, :, at] = grad_value[here]
        for m in range(neg):
            here = slice((own + m) * rows, (own + m + 1) * rows)
            slots[doc * neg + m, :rows, at] = grad_key[here].astype(BF16)
            slots[doc * neg + m, rows:, at] = grad_value[here].astype(BF16)

        @pl.when(lax.rem(step, heads) == heads - 1)
        def _():
            for m in range(neg):
                entry = doc * neg + m
                pltpu.make_async_copy(slots.at[entry], slots_hbm.at[holder[doc, m]], slot_sem.at[entry]).start()
            span = pl.ds(doc * own, own)
            pltpu.make_async_copy(own_rows.at[:, span], own_rows_hbm.at[:, span], own_sem.at[doc]).start()

    out_attended = pltpu.make_async_copy(attended, attended_hbm, out_sem.at[0])
    out_attended.start()
    out_query = pltpu.make_async_copy(grad_query, grad_query_hbm, out_sem.at[1])
    out_query.start()
    for doc in range(docs):
        for m in range(neg):
            entry = doc * neg + m
            pltpu.make_async_copy(slots.at[entry], slots_hbm.at[holder[doc, m]], slot_sem.at[entry]).wait()
        span = pl.ds(doc * own, own)
        pltpu.make_async_copy(own_rows.at[:, span], own_rows_hbm.at[:, span], own_sem.at[doc]).wait()
    out_attended.wait()
    out_query.wait()


def layer(counts, holder, queries, keys, values, recv, grads):
    docs, _, features = queries.shape
    entries = holder.shape[0] * holder.shape[1]
    rows = grads.shape[0]
    dma = pltpu.SemaphoreType.DMA
    return pl.pallas_call(
        layer_kernel,
        out_shape=[
            pltpu.HBM((rows, features), BF16),
            pltpu.HBM(queries.shape, BF16),
            pltpu.HBM((2, *keys.shape), F32),
            pltpu.HBM(recv.shape, BF16),
        ],
        in_specs=[SMEM] * 2 + [VMEM] * 5,
        out_specs=[HBM] * 4,
        scratch_shapes=[
            pltpu.VMEM((rows, features), BF16),
            pltpu.VMEM(queries.shape, BF16),
            pltpu.VMEM((2, *keys.shape), F32),
            pltpu.VMEM((entries, *recv.shape[1:]), BF16),
            dma((2,)),
            dma((docs,)),
            dma((entries,)),
        ],
        compiler_params=PARAMS,
        cost_estimate=cost(4 * 2**30, 12 * 2**20),
        name="layer",
    )(counts, holder, queries, keys, values, recv, grads)


def copies_in(pairs, sem):
    copies = [pltpu.make_async_copy(source, target, sem.at[i]) for i, (source, target) in enumerate(pairs)]
    for copy in copies:
        copy.start()
    return copies


def weight_copies(refs, weight, sem):
    first, pairs = 0, []
    for ref in refs:
        count = ref.shape[0] // weight.shape[1]
        for i in range(count):
            pairs.append((ref.at[pl.ds(i * weight.shape[1], weight.shape[1])], weight.at[first + i]))
        first += count
    return copies_in(pairs, sem)


def back_kernel(table, grad0, grad1, grad2, grad3, *refs):
    *blocks, out_hbm, weight, held, total, out, weight_sem, held_sem = refs
    block = weight.shape[2]
    waiting = copies_in([(ref, held.at[j]) for j, ref in enumerate((grad0, grad1, grad2, grad3))], held_sem)
    waiting += weight_copies(blocks, weight, weight_sem)
    for copy in waiting:
        copy.wait()
    total[...] = jnp.zeros_like(total)

    @pl.loop(0, weight.shape[0], unroll=4)
    def _(step):
        at = pl.ds(pl.multiple_of(table[1, step] * block, block), block)
        total[...] += lax.dot_general(held[table[0, step], :, at], weight[step], NT, preferred_element_type=F32)

    out[...] = total[...].astype(BF16)
    pltpu.sync_copy(out, out_hbm)


def back_projected(table, held, blocks):
    groups = len(held)
    rows, columns = held[0].shape
    features, block = blocks[0].shape
    count = table.shape[1]
    return pl.pallas_call(
        back_kernel,
        out_shape=pltpu.HBM((rows, features), BF16),
        in_specs=[SMEM] + [HBM] * (len(blocks) + groups),
        out_specs=HBM,
        scratch_shapes=[
            pltpu.VMEM((count, features, block), BF16),
            pltpu.VMEM((groups, rows, columns), BF16),
            pltpu.VMEM((rows, features), F32),
            pltpu.VMEM((rows, features), BF16),
            pltpu.SemaphoreType.DMA((count,)),
            pltpu.SemaphoreType.DMA((groups,)),
        ],
        compiler_params=PARAMS,
        cost_estimate=cost(2 * 2**30, 8 * 2**20),
        name="back_projection",
    )(table, *map(in_hbm, held), *map(in_hbm, blocks))


def project_kernel(table, attended_hbm, *refs):
    *blocks, out0, out1, out2, out3, weight, attended, terms, weight_sem, in_sem = refs
    block = weight.shape[2]
    waiting = copies_in([(attended_hbm, attended)], in_sem) + weight_copies(blocks, weight, weight_sem)
    for copy in waiting:
        copy.wait()

    @pl.loop(0, weight.shape[0], unroll=4)
    def _(step):
        at = pl.ds(pl.multiple_of(table[1, step] * block, block), block)
        terms[table[0, step], :, at] = jnp.dot(attended[...], weight[step], preferred_element_type=F32).astype(BF16)

    for j, out in enumerate((out0, out1, out2, out3)):
        out[...] = terms[j]


def projected(table, attended, blocks, groups):
    features, block = blocks[0].shape
    rows, count = attended.shape[0], table.shape[1]
    columns = count * block // groups
    return pl.pallas_call(
        project_kernel,
        out_shape=[jax.ShapeDtypeStruct((rows, columns), BF16)] * groups,
        in_specs=[SMEM] + [HBM] * (1 + len(blocks)),
        out_specs=[VMEM] * groups,
        scratch_shapes=[
            pltpu.VMEM((count, features, block), BF16),
            pltpu.VMEM(attended.shape, BF16),
            pltpu.VMEM((groups, rows, columns), BF16),
            pltpu.SemaphoreType.DMA((count,)),
            pltpu.SemaphoreType.DMA((1,)),
        ],
        compiler_params=PARAMS,
        cost_estimate=cost(2 * 2**30, 8 * 2**20),
        name="projection",
    )(table, in_hbm(attended), *map(in_hbm, blocks))


def combine_kernel(asked, own_rows_hbm, back, key_grads_hbm, value_grads_hbm, own_rows, total, grads, in_sem, out_sem):
    rows = own_rows.shape[2]
    arriving = [pltpu.make_async_copy(own_rows_hbm.at[i], own_rows.at[i], in_sem.at[i]) for i in range(2)]
    for copy in arriving:
        copy.start()

    @pl.loop(0, total.shape[1])
    def _(block):
        total[:, block] = jnp.zeros_like(total[:, block])

    @pl.loop(0, back.shape[0])
    def _(slot):
        spot = asked[slot, 0]

        @pl.when(spot >= 0)
        def _():
            total[0, spot] += back[slot, :rows, :].astype(F32)
            total[1, spot] += back[slot, rows:, :].astype(F32)

    outgoing = []
    for i, target in enumerate((key_grads_hbm, value_grads_hbm)):
        arriving[i].wait()

        @pl.loop(0, total.shape[1])
        def _(block, i=i):
            grads[i, block] = (own_rows[i, block] + total[i, block]).astype(BF16)

        outgoing.append(pltpu.make_async_copy(grads.at[i], target, out_sem.at[i]))
        outgoing[i].start()
    for copy in outgoing:
        copy.wait()


def combined(asked, own_rows, back):
    shape = pltpu.HBM(own_rows.shape[1:], BF16)
    return pl.pallas_call(
        combine_kernel,
        out_shape=[shape, shape],
        in_specs=[SMEM, HBM, VMEM],
        out_specs=[HBM, HBM],
        scratch_shapes=[
            pltpu.VMEM(own_rows.shape, F32),
            pltpu.VMEM(own_rows.shape, F32),
            pltpu.VMEM(own_rows.shape, BF16),
            pltpu.SemaphoreType.DMA((2,)),
            pltpu.SemaphoreType.DMA((2,)),
        ],
        compiler_params=PARAMS,
        cost_estimate=cost(0, 4 * 2**20),
        name="combine",
    )(asked, in_hbm(own_rows), back)


def on_device(sent_queries, mem_keys, mem_values, out_weight, sent_grads, counts, neg_ids):
    keys, values = mem_keys[0], mem_values[0]
    mem_count = keys.shape[0]
    groups = lax.axis_size("dp")
    tensor = lax.axis_size("tensor")
    me = lax.axis_index("dp")
    sign = 1 - 2 * lax.rem(me, 2)
    block_of = (me + sign * jnp.array(DELTAS, jnp.int32) + 2 * groups) % groups
    per = groups // tensor
    table = jnp.stack([(block_of // per + tensor - lax.axis_index("tensor")) % tensor, block_of % per]).astype(jnp.int32)

    holder = neg_ids // mem_count
    spot = neg_ids - holder * mem_count
    named = holder[None] == jnp.arange(groups, dtype=jnp.int32)[:, None, None]
    request = jnp.sum(jnp.where(named, spot[None] + 1, 0), axis=(1, 2)) - 1
    asked = exchanged(request.reshape(groups, 1))

    weight = out_weight[0]
    other = swapped(weight)
    pair, asked = lax.optimization_barrier((jnp.concatenate([weight, other]), asked))
    near, next_near = along_ring(pair, 1), along_ring(pair, 2)
    grads = passed_along(sent_grads, "section", -1)[0]
    next_near, grads = lax.optimization_barrier((next_near, grads))
    third, far = along_ring(next_near, 1), along_ring(next_near[: weight.shape[0]], 2)
    slots = picked_slots(asked, keys, values)
    slots, near, third, far = lax.optimization_barrier((slots, near, third, far))
    recv = exchanged(slots)
    blocks = [weight, other, near, next_near, third, far]
    blocks += [swapped(block) for block in blocks[2:]]

    queries = passed_along(sent_queries, "section", 1)[0]
    docs, query_count, features = queries.shape
    grad_rows = grads.reshape(docs * query_count, grads.shape[2])
    held = [grad_rows] + [passed_along(grad_rows, "tensor", -j) for j in range(1, tensor)]
    grad_attended = back_projected(table, held, blocks)

    attended, query_grads, own_rows, slots = layer(counts, holder, queries, keys, values, recv, grad_attended)
    back = exchanged(slots)
    terms = projected(table, attended, blocks, tensor)
    arrived = [terms[0]] + [passed_along(terms[j], "tensor", j) for j in range(1, tensor)]
    mixed = sum(term.astype(F32) for term in arrived).astype(BF16).reshape(1, docs, query_count, -1)

    key_grads, value_grads = combined(asked, own_rows, back)
    return mixed, query_grads[None], key_grads[None], value_grads[None]


def solution(mesh):
    rows = P("section", "dp", None, "tensor")
    return jax.shard_map(
        on_device,
        mesh=mesh,
        in_specs=(rows, rows, rows, P("section", "tensor", "dp"), rows, P("dp"), P("dp", None)),
        out_specs=(rows, rows, rows, rows),
        check_vma=False,
    )
```

```python
import jax
import jax.numpy as jnp
from jax import lax
from jax.experimental import pallas as pl
from jax.experimental.pallas import tpu as pltpu
from jax.sharding import PartitionSpec as P

HD = 128
DELTAS = (0, 1, -2, -1, -4, -3, -6, -5, -8, 3, 2, 5, 4, 7, 6, 9)
F32 = jnp.float32
BF16 = jnp.bfloat16
NT = (((1,), (1,)), ((), ()))
TN = (((0,), (0,)), ((), ()))
VMEM = pl.BlockSpec(memory_space=pltpu.VMEM)
HBM = pl.BlockSpec(memory_space=pltpu.HBM)
ANY = pl.BlockSpec(memory_space=pl.ANY)
SMEM = pl.BlockSpec(memory_space=pltpu.SMEM)
PARAMS = pltpu.CompilerParams(vmem_limit_bytes=20 * 1024 * 1024)


def passed_along(block, axis, distance):
    count = lax.axis_size(axis)
    return lax.ppermute(block, axis, [(i, (i + distance) % count) for i in range(count)])


def swapped(block):
    return lax.ppermute(block, "dp", [(i, i ^ 1) for i in range(lax.axis_size("dp"))])


def along_ring(block, chips):
    count = lax.axis_size("dp")
    return lax.ppermute(block, "dp", [(i, (i + (1 - i % 2 * 2) * 2 * chips) % count) for i in range(count)])


def exchanged(slots):
    return lax.all_to_all(slots, "dp", split_axis=0, concat_axis=0, tiled=True)


def in_hbm(array):
    return pltpu.with_memory_space_constraint(array, pltpu.HBM)


def cost(flops, nbytes):
    return pl.CostEstimate(flops=int(flops), bytes_accessed=int(nbytes), transcendentals=0)


def pick_kernel(asked, keys_hbm, values_hbm, key_slots, value_slots, keys, values, in_sem, out_sem):
    in_key = pltpu.make_async_copy(keys_hbm, keys, in_sem.at[0])
    in_value = pltpu.make_async_copy(values_hbm, values, in_sem.at[1])
    in_key.start()
    in_value.start()
    outgoing = []
    for which, (arriving, source, slots) in enumerate(((in_key, keys, key_slots), (in_value, values, value_slots))):
        arriving.wait()
        for slot in range(slots.shape[0]):
            spot = asked[slot, 0]
            copy = pltpu.make_async_copy(source.at[jnp.maximum(spot, 0)], slots.at[slot], out_sem.at[slot, which])
            pl.when(spot >= 0)(copy.start)
            outgoing.append((spot, copy))
    for spot, copy in outgoing:
        pl.when(spot >= 0)(copy.wait)


def picked_slots(asked, keys, values):
    slot_count = asked.shape[0]
    shape = pltpu.HBM((slot_count, *keys.shape[1:]), BF16)
    return pl.pallas_call(
        pick_kernel,
        out_shape=[shape, shape],
        in_specs=[SMEM, HBM, HBM],
        out_specs=[HBM, HBM],
        scratch_shapes=[
            pltpu.VMEM(keys.shape, BF16),
            pltpu.VMEM(values.shape, BF16),
            pltpu.SemaphoreType.DMA((2,)),
            pltpu.SemaphoreType.DMA((slot_count, 2)),
        ],
        compiler_params=PARAMS,
        cost_estimate=cost(0, 4 * 2**20),
        name="pick_blocks",
    )(asked, in_hbm(keys), in_hbm(values))


def layer_kernel(
    counts, holder, queries, keys, values, recv_keys, recv_values, grads,
    attended_hbm, grad_query_hbm, own_rows_hbm, slots_hbm,
    attended, grad_query, own_rows, slots, out_sem, own_sem, slot_sem,
):
    docs, query_count, _ = queries.shape
    mem_count, rows, features = keys.shape
    own = mem_count // docs
    neg = holder.shape[1]
    heads = features // HD
    scale = HD**-0.5
    total = (own + neg) * rows

    def place(step):
        doc, head = step // heads, lax.rem(step, heads)
        at = pl.ds(pl.multiple_of(head * HD, HD), HD)
        query_rows = pl.ds(pl.multiple_of(doc * query_count, query_count), query_count)
        senders = [holder[doc, m] for m in range(neg)]
        key = jnp.concatenate(
            [keys[doc * own + m, :, at] for m in range(own)] + [recv_keys[e, :, at] for e in senders], axis=0
        )
        value = jnp.concatenate(
            [values[doc * own + m, :, at] for m in range(own)] + [recv_values[e, :, at] for e in senders], axis=0
        )
        return doc, at, query_rows, key, value

    position = lax.broadcasted_iota(jnp.int32, (total, 1), 0)

    @pl.loop(0, docs * heads, unroll=4)
    def _(step):
        doc, at, query_rows, key, value = place(step)
        valid = (position < counts[doc] * rows) | (position >= own * rows)
        scores = lax.dot_general(key, queries[doc, :, at], NT, preferred_element_type=F32) * scale
        scores = jnp.where(valid, scores, -jnp.inf)
        expo = jnp.exp(scores - jnp.max(scores, axis=0, keepdims=True))
        prob = expo * (1.0 / jnp.sum(expo, axis=0, keepdims=True))
        attended[query_rows, at] = lax.dot_general(prob.astype(BF16), value, TN, preferred_element_type=F32).astype(BF16)
        grad = grads[query_rows, at]
        grad_prob = lax.dot_general(value, grad, NT, preferred_element_type=F32)
        delta = jnp.sum(prob * grad_prob, axis=0, keepdims=True)
        grad_score = (prob * (grad_prob - delta)).astype(BF16)
        grad_value = jnp.dot(prob.astype(BF16), grad, preferred_element_type=F32)
        grad_key = jnp.dot(grad_score, queries[doc, :, at], preferred_element_type=F32) * scale
        grad_query[doc, :, at] = (lax.dot_general(grad_score, key, TN, preferred_element_type=F32) * scale).astype(BF16)
        for m in range(own):
            here = slice(m * rows, (m + 1) * rows)
            own_rows[0, doc * own + m, :, at] = grad_key[here]
            own_rows[1, doc * own + m, :, at] = grad_value[here]
        for m in range(neg):
            here = slice((own + m) * rows, (own + m + 1) * rows)
            slots[doc * neg + m, :rows, at] = grad_key[here].astype(BF16)
            slots[doc * neg + m, rows:, at] = grad_value[here].astype(BF16)

        @pl.when(lax.rem(step, heads) == heads - 1)
        def _():
            for m in range(neg):
                entry = doc * neg + m
                pltpu.make_async_copy(slots.at[entry], slots_hbm.at[holder[doc, m]], slot_sem.at[entry]).start()
            span = pl.ds(doc * own, own)
            pltpu.make_async_copy(own_rows.at[:, span], own_rows_hbm.at[:, span], own_sem.at[doc]).start()

    out_attended = pltpu.make_async_copy(attended, attended_hbm, out_sem.at[0])
    out_attended.start()
    out_query = pltpu.make_async_copy(grad_query, grad_query_hbm, out_sem.at[1])
    out_query.start()
    for doc in range(docs):
        for m in range(neg):
            entry = doc * neg + m
            pltpu.make_async_copy(slots.at[entry], slots_hbm.at[holder[doc, m]], slot_sem.at[entry]).wait()
        span = pl.ds(doc * own, own)
        pltpu.make_async_copy(own_rows.at[:, span], own_rows_hbm.at[:, span], own_sem.at[doc]).wait()
    out_attended.wait()
    out_query.wait()


def layer(counts, holder, queries, keys, values, recv_keys, recv_values, grads):
    docs, _, features = queries.shape
    entries = holder.shape[0] * holder.shape[1]
    rows = grads.shape[0]
    slot_count, block_rows, _ = recv_keys.shape
    slot_shape = (2 * block_rows, features)
    dma = pltpu.SemaphoreType.DMA
    return pl.pallas_call(
        layer_kernel,
        out_shape=[
            pltpu.HBM((rows, features), BF16),
            pltpu.HBM(queries.shape, BF16),
            pltpu.HBM((2, *keys.shape), F32),
            pltpu.HBM((slot_count, *slot_shape), BF16),
        ],
        in_specs=[SMEM] * 2 + [VMEM] * 6,
        out_specs=[HBM] * 4,
        scratch_shapes=[
            pltpu.VMEM((rows, features), BF16),
            pltpu.VMEM(queries.shape, BF16),
            pltpu.VMEM((2, *keys.shape), F32),
            pltpu.VMEM((entries, *slot_shape), BF16),
            dma((2,)),
            dma((docs,)),
            dma((entries,)),
        ],
        compiler_params=PARAMS,
        cost_estimate=cost(4 * 2**30, 12 * 2**20),
        name="layer",
    )(counts, holder, queries, keys, values, recv_keys, recv_values, grads)


def copies_in(pairs, sem):
    copies = [pltpu.make_async_copy(source, target, sem.at[i]) for i, (source, target) in enumerate(pairs)]
    for copy in copies:
        copy.start()
    return copies


def weight_copies(refs, weight, sem):
    first, pairs = 0, []
    for ref in refs:
        count = ref.shape[0] // weight.shape[1]
        for i in range(count):
            pairs.append((ref.at[pl.ds(i * weight.shape[1], weight.shape[1])], weight.at[first + i]))
        first += count
    return copies_in(pairs, sem)


def back_kernel(table, grad0, grad1, grad2, grad3, *refs):
    *blocks, out_hbm, weight, held, total, out, weight_sem, held_sem = refs
    block = weight.shape[2]
    waiting = copies_in([(ref, held.at[j]) for j, ref in enumerate((grad0, grad1, grad2, grad3))], held_sem)
    waiting += weight_copies(blocks, weight, weight_sem)
    for copy in waiting:
        copy.wait()
    total[...] = jnp.zeros_like(total)

    @pl.loop(0, weight.shape[0], unroll=4)
    def _(step):
        at = pl.ds(pl.multiple_of(table[1, step] * block, block), block)
        total[...] += lax.dot_general(held[table[0, step], :, at], weight[step], NT, preferred_element_type=F32)

    out[...] = total[...].astype(BF16)
    pltpu.sync_copy(out, out_hbm)


def back_projected(table, held, blocks):
    groups = len(held)
    rows, columns = held[0].shape
    features, block = blocks[0].shape
    count = table.shape[1]
    return pl.pallas_call(
        back_kernel,
        out_shape=pltpu.HBM((rows, features), BF16),
        in_specs=[SMEM] + [HBM] * (len(blocks) + groups),
        out_specs=HBM,
        scratch_shapes=[
            pltpu.VMEM((count, features, block), BF16),
            pltpu.VMEM((groups, rows, columns), BF16),
            pltpu.VMEM((rows, features), F32),
            pltpu.VMEM((rows, features), BF16),
            pltpu.SemaphoreType.DMA((count,)),
            pltpu.SemaphoreType.DMA((groups,)),
        ],
        compiler_params=PARAMS,
        cost_estimate=cost(2 * 2**30, 8 * 2**20),
        name="back_projection",
    )(table, *map(in_hbm, held), *map(in_hbm, blocks))


def project_kernel(table, attended_hbm, *refs):
    *blocks, out0, out1, out2, out3, weight, attended, terms, weight_sem, in_sem = refs
    block = weight.shape[2]
    waiting = copies_in([(attended_hbm, attended)], in_sem) + weight_copies(blocks, weight, weight_sem)
    for copy in waiting:
        copy.wait()

    @pl.loop(0, weight.shape[0], unroll=4)
    def _(step):
        at = pl.ds(pl.multiple_of(table[1, step] * block, block), block)
        terms[table[0, step], :, at] = jnp.dot(attended[...], weight[step], preferred_element_type=F32).astype(BF16)

    for j, out in enumerate((out0, out1, out2, out3)):
        out[...] = terms[j]


def projected(table, attended, blocks, groups):
    features, block = blocks[0].shape
    rows, count = attended.shape[0], table.shape[1]
    columns = count * block // groups
    return pl.pallas_call(
        project_kernel,
        out_shape=[jax.ShapeDtypeStruct((rows, columns), BF16)] * groups,
        in_specs=[SMEM] + [HBM] * (1 + len(blocks)),
        out_specs=[VMEM] * groups,
        scratch_shapes=[
            pltpu.VMEM((count, features, block), BF16),
            pltpu.VMEM(attended.shape, BF16),
            pltpu.VMEM((groups, rows, columns), BF16),
            pltpu.SemaphoreType.DMA((count,)),
            pltpu.SemaphoreType.DMA((1,)),
        ],
        compiler_params=PARAMS,
        cost_estimate=cost(2 * 2**30, 8 * 2**20),
        name="projection",
    )(table, in_hbm(attended), *map(in_hbm, blocks))


def combine_kernel(asked, own_rows_hbm, back, key_grads_hbm, value_grads_hbm, own_rows, total, grads, in_sem, out_sem):
    rows = own_rows.shape[2]
    arriving = [pltpu.make_async_copy(own_rows_hbm.at[i], own_rows.at[i], in_sem.at[i]) for i in range(2)]
    for copy in arriving:
        copy.start()

    @pl.loop(0, total.shape[1])
    def _(block):
        total[:, block] = jnp.zeros_like(total[:, block])

    @pl.loop(0, back.shape[0])
    def _(slot):
        spot = asked[slot, 0]

        @pl.when(spot >= 0)
        def _():
            total[0, spot] += back[slot, :rows, :].astype(F32)
            total[1, spot] += back[slot, rows:, :].astype(F32)

    outgoing = []
    for i, target in enumerate((key_grads_hbm, value_grads_hbm)):
        arriving[i].wait()

        @pl.loop(0, total.shape[1])
        def _(block, i=i):
            grads[i, block] = (own_rows[i, block] + total[i, block]).astype(BF16)

        outgoing.append(pltpu.make_async_copy(grads.at[i], target, out_sem.at[i]))
        outgoing[i].start()
    for copy in outgoing:
        copy.wait()


def combined(asked, own_rows, back):
    shape = pltpu.HBM(own_rows.shape[1:], BF16)
    return pl.pallas_call(
        combine_kernel,
        out_shape=[shape, shape],
        in_specs=[SMEM, HBM, VMEM],
        out_specs=[HBM, HBM],
        scratch_shapes=[
            pltpu.VMEM(own_rows.shape, F32),
            pltpu.VMEM(own_rows.shape, F32),
            pltpu.VMEM(own_rows.shape, BF16),
            pltpu.SemaphoreType.DMA((2,)),
            pltpu.SemaphoreType.DMA((2,)),
        ],
        compiler_params=PARAMS,
        cost_estimate=cost(0, 4 * 2**20),
        name="combine",
    )(asked, in_hbm(own_rows), back)


def on_device(sent_queries, mem_keys, mem_values, out_weight, sent_grads, counts, neg_ids):
    keys, values = mem_keys[0], mem_values[0]
    mem_count = keys.shape[0]
    groups = lax.axis_size("dp")
    tensor = lax.axis_size("tensor")
    me = lax.axis_index("dp")
    sign = 1 - 2 * lax.rem(me, 2)
    block_of = (me + sign * jnp.array(DELTAS, jnp.int32) + 2 * groups) % groups
    per = groups // tensor
    table = jnp.stack([(block_of // per + tensor - lax.axis_index("tensor")) % tensor, block_of % per]).astype(jnp.int32)

    holder = neg_ids // mem_count
    spot = neg_ids - holder * mem_count
    named = holder[None] == jnp.arange(groups, dtype=jnp.int32)[:, None, None]
    request = jnp.sum(jnp.where(named, spot[None] + 1, 0), axis=(1, 2)) - 1
    asked = exchanged(request.reshape(groups, 1))

    weight = out_weight[0]
    other = swapped(weight)
    pair, asked = lax.optimization_barrier((jnp.concatenate([weight, other]), asked))
    near, next_near = along_ring(pair, 1), along_ring(pair, 2)
    grads = passed_along(sent_grads, "section", -1)[0]
    key_slots, value_slots = picked_slots(asked, keys, values)
    key_slots, near, next_near, grads = lax.optimization_barrier((key_slots, near, next_near, grads))
    recv_keys = exchanged(key_slots)
    third, far = along_ring(next_near, 1), along_ring(next_near[: weight.shape[0]], 2)
    docs, query_count = sent_queries.shape[1:3]
    grad_rows = grads.reshape(docs * query_count, grads.shape[2])
    held = [grad_rows] + [passed_along(grad_rows, "tensor", -j) for j in range(1, tensor)]
    value_slots, third, far, *held = lax.optimization_barrier((value_slots, third, far, *held))
    recv_values = exchanged(value_slots)
    blocks = [weight, other, near, next_near, third, far]
    blocks += [swapped(block) for block in blocks[2:]]

    queries = passed_along(sent_queries, "section", 1)[0]
    grad_attended = back_projected(table, held, blocks)

    attended, query_grads, own_rows, slots = layer(
        counts, holder, queries, keys, values, recv_keys, recv_values, grad_attended
    )
    back = exchanged(slots)
    terms = projected(table, attended, blocks, tensor)
    arrived = [terms[0]] + [passed_along(terms[j], "tensor", j) for j in range(1, tensor)]
    mixed = sum(term.astype(F32) for term in arrived).astype(BF16).reshape(1, docs, query_count, -1)

    key_grads, value_grads = combined(asked, own_rows, back)
    return mixed, query_grads[None], key_grads[None], value_grads[None]


def solution(mesh):
    rows = P("section", "dp", None, "tensor")
    return jax.shard_map(
        on_device,
        mesh=mesh,
        in_specs=(rows, rows, rows, P("section", "tensor", "dp"), rows, P("dp"), P("dp", None)),
        out_specs=(rows, rows, rows, rows),
        check_vma=False,
    )
```

```python
import jax
import jax.numpy as jnp
from jax import lax
from jax.experimental import pallas as pl
from jax.experimental.pallas import tpu as pltpu
from jax.sharding import PartitionSpec as P

HD = 128
F32 = jnp.float32
BF16 = jnp.bfloat16
NT = (((1,), (1,)), ((), ()))
TN = (((0,), (0,)), ((), ()))
VMEM = pl.BlockSpec(memory_space=pltpu.VMEM)
HBM = pl.BlockSpec(memory_space=pltpu.HBM)
ANY = pl.BlockSpec(memory_space=pl.ANY)
SMEM = pl.BlockSpec(memory_space=pltpu.SMEM)
PARAMS = pltpu.CompilerParams(vmem_limit_bytes=16 * 1024 * 1024)


def passed_along(block, axis, distance):
    count = lax.axis_size(axis)
    return lax.ppermute(block, axis, [(i, (i + distance) % count) for i in range(count)])


def exchanged(slots):
    return lax.all_to_all(slots, "dp", split_axis=0, concat_axis=0, tiled=True)


def in_hbm(array):
    return pltpu.with_memory_space_constraint(array, pltpu.HBM)


def cost(flops, nbytes):
    return pl.CostEstimate(flops=int(flops), bytes_accessed=int(nbytes), transcendentals=0)


def pick_kernel(asked, keys_hbm, values_hbm, slots, keys, values, in_sem, out_sem):
    rows = keys.shape[1]
    in_key = pltpu.make_async_copy(keys_hbm, keys, in_sem.at[0])
    in_value = pltpu.make_async_copy(values_hbm, values, in_sem.at[1])
    in_key.start()
    in_value.start()

    def sent(slot, which, source):
        target = slots.at[slot, pl.ds(which * rows, rows)]
        return pltpu.make_async_copy(source.at[jnp.maximum(asked[slot, 0], 0)], target, out_sem.at[slot, which])

    for which, (arriving, source) in enumerate(((in_key, keys), (in_value, values))):
        arriving.wait()

        @pl.loop(0, slots.shape[0])
        def _(slot, which=which, source=source):
            copy = sent(slot, which, source)
            pl.when(asked[slot, 0] >= 0)(copy.start)

    @pl.loop(0, slots.shape[0])
    def _(slot):
        for which, source in enumerate((keys, values)):
            pl.when(asked[slot, 0] >= 0)(sent(slot, which, source).wait)


def picked_slots(asked, keys, values):
    slot_count = asked.shape[0]
    _, rows, features = keys.shape
    return pl.pallas_call(
        pick_kernel,
        out_shape=pltpu.HBM((slot_count, 2 * rows, features), BF16),
        in_specs=[SMEM, HBM, HBM],
        out_specs=HBM,
        scratch_shapes=[
            pltpu.VMEM(keys.shape, BF16),
            pltpu.VMEM(values.shape, BF16),
            pltpu.SemaphoreType.DMA((2,)),
            pltpu.SemaphoreType.DMA((slot_count, 2)),
        ],
        compiler_params=PARAMS,
        cost_estimate=cost(0, 4 * 2**20),
        name="pick_blocks",
    )(asked, in_hbm(keys), in_hbm(values))


def layer_kernel(
    counts, holder, spot, queries, keys, values, recv, weight_hbm, grad0, grad1, grad2, grad3,
    attended_hbm, grad_query_hbm, own_rows_hbm, slots_hbm,
    weight, held, grads, probs, attended, grad_query, own_rows, slots, weight_sem, held_sem, out_sem, own_sem, slot_sem,
):
    docs, query_count, _ = queries.shape
    mem_count, rows, features = keys.shape
    own = mem_count // docs
    neg = holder.shape[1]
    groups, per, _, block = weight.shape
    heads = features // HD
    scale = HD**-0.5

    arriving = []
    for j, grad in enumerate((grad0, grad1, grad2, grad3)):
        first = lax.rem(spot[0] + j, groups) * per
        in_weight = pltpu.make_async_copy(weight_hbm.at[pl.ds(first, per)], weight.at[j], weight_sem.at[j])
        in_held = pltpu.make_async_copy(grad, held.at[j], held_sem.at[j])
        in_held.start()
        in_weight.start()
        arriving.append((in_held, in_weight))

    def place(step):
        doc, head = step // heads, lax.rem(step, heads)
        at = pl.ds(pl.multiple_of(head * HD, HD), HD)
        query_rows = pl.ds(pl.multiple_of(doc * query_count, query_count), query_count)
        senders = [holder[doc, m] for m in range(neg)]
        key = jnp.concatenate(
            [keys[doc * own + m, :, at] for m in range(own)] + [recv[e, :rows, at] for e in senders], axis=0
        )
        value = jnp.concatenate(
            [values[doc * own + m, :, at] for m in range(own)] + [recv[e, rows:, at] for e in senders], axis=0
        )
        return doc, at, query_rows, key, value

    position = lax.broadcasted_iota(jnp.int32, (own * rows, 1), 0)

    @pl.loop(0, docs * heads, unroll=4)
    def _(step):
        doc, at, query_rows, key, value = place(step)
        valid = position < counts[doc] * rows
        scores = lax.dot_general(key, queries[doc, :, at], NT, preferred_element_type=F32) * scale
        scores = jnp.concatenate([jnp.where(valid, scores[: own * rows], -jnp.inf), scores[own * rows :]], axis=0)
        expo = jnp.exp(scores - jnp.max(scores, axis=0, keepdims=True))
        prob = expo * (1.0 / jnp.sum(expo, axis=0, keepdims=True))
        probs[step] = prob
        attended[query_rows, at] = lax.dot_general(prob.astype(BF16), value, TN, preferred_element_type=F32).astype(BF16)

    out_attended = pltpu.make_async_copy(attended, attended_hbm, out_sem.at[0])
    out_attended.start()

    for j, copies in enumerate(arriving):
        for copy in copies:
            copy.wait()
        term = None
        for c in range(per):
            part = lax.dot_general(
                held[j, :, c * block : (c + 1) * block], weight[j, c], NT, preferred_element_type=F32
            )
            term = part if term is None else term + part
        grad_rows = term if j == 0 else grad_rows + term
    grads[...] = grad_rows.astype(BF16)

    @pl.loop(0, docs * heads, unroll=8)
    def _(step):
        doc, at, query_rows, key, value = place(step)
        grad = grads[query_rows, at]
        prob = probs[step]
        grad_prob = lax.dot_general(value, grad, NT, preferred_element_type=F32)
        delta = jnp.sum(prob * grad_prob, axis=0, keepdims=True)
        grad_score = (prob * (grad_prob - delta)).astype(BF16)
        grad_value = jnp.dot(prob.astype(BF16), grad, preferred_element_type=F32)
        grad_key = jnp.dot(grad_score, queries[doc, :, at], preferred_element_type=F32) * scale
        grad_query[doc, :, at] = (lax.dot_general(grad_score, key, TN, preferred_element_type=F32) * scale).astype(BF16)
        for m in range(own):
            here = slice(m * rows, (m + 1) * rows)
            own_rows[0, doc * own + m, :, at] = grad_key[here].astype(BF16)
            own_rows[1, doc * own + m, :, at] = grad_value[here].astype(BF16)
        for m in range(neg):
            here = slice((own + m) * rows, (own + m + 1) * rows)
            slots[doc * neg + m, :rows, at] = grad_key[here].astype(BF16)
            slots[doc * neg + m, rows:, at] = grad_value[here].astype(BF16)

        @pl.when(lax.rem(step, heads) == heads - 1)
        def _():
            for m in range(neg):
                entry = doc * neg + m
                pltpu.make_async_copy(slots.at[entry], slots_hbm.at[holder[doc, m]], slot_sem.at[entry]).start()
            span = pl.ds(doc * own, own)
            pltpu.make_async_copy(own_rows.at[:, span], own_rows_hbm.at[:, span], own_sem.at[doc]).start()

    out_query = pltpu.make_async_copy(grad_query, grad_query_hbm, out_sem.at[1])
    out_query.start()
    for doc in range(docs):
        for m in range(neg):
            entry = doc * neg + m
            pltpu.make_async_copy(slots.at[entry], slots_hbm.at[holder[doc, m]], slot_sem.at[entry]).wait()
        span = pl.ds(doc * own, own)
        pltpu.make_async_copy(own_rows.at[:, span], own_rows_hbm.at[:, span], own_sem.at[doc]).wait()
    out_attended.wait()
    out_query.wait()


def layer(counts, holder, spot, queries, keys, values, recv, weight, held):
    docs, query_count, features = queries.shape
    entries, groups = holder.shape[0] * holder.shape[1], len(held)
    rows, columns = held[0].shape
    dma = pltpu.SemaphoreType.DMA
    return pl.pallas_call(
        layer_kernel,
        out_shape=[
            pltpu.HBM((rows, features), BF16),
            pltpu.HBM(queries.shape, BF16),
            pltpu.HBM((2, *keys.shape), BF16),
            pltpu.HBM(recv.shape, BF16),
        ],
        in_specs=[SMEM] * 3 + [VMEM] * 4 + [HBM] * (1 + groups),
        out_specs=[HBM] * 4,
        scratch_shapes=[
            pltpu.VMEM((groups, weight.shape[0] // groups, *weight.shape[1:]), BF16),
            pltpu.VMEM((groups, rows, columns), BF16),
            pltpu.VMEM((rows, features), BF16),
            pltpu.VMEM((docs * features // HD, (keys.shape[0] // docs + holder.shape[1]) * keys.shape[1], query_count), F32),
            pltpu.VMEM((rows, features), BF16),
            pltpu.VMEM(queries.shape, BF16),
            pltpu.VMEM((2, *keys.shape), BF16),
            pltpu.VMEM((entries, *recv.shape[1:]), BF16),
            dma((groups,)),
            dma((groups,)),
            dma((2,)),
            dma((docs,)),
            dma((entries,)),
        ],
        compiler_params=PARAMS,
        cost_estimate=cost(5 * 2**30, 16 * 2**20),
        name="layer",
    )(counts, holder, spot, queries, keys, values, recv, in_hbm(weight), *map(in_hbm, held))


def project_kernel(spot, weight_hbm, attended_hbm, out0, out1, out2, out3, weight, attended, sem, in_sem):
    groups, per, _, block = weight.shape
    outs = (out0, out1, out2, out3)
    in_attended = pltpu.make_async_copy(attended_hbm, attended, in_sem)
    in_attended.start()
    copies = []
    for j in range(groups):
        first = lax.rem(spot[0] + j, groups) * per
        copies.append(pltpu.make_async_copy(weight_hbm.at[pl.ds(first, per)], weight.at[j], sem.at[j]))
        copies[j].start()
    in_attended.wait()
    for j, out in enumerate(outs):
        copies[j].wait()
        for c in range(per):
            term = jnp.dot(attended[...], weight[j, c], preferred_element_type=F32)
            out[:, c * block : (c + 1) * block] = term.astype(BF16)


def projected(spot, weight, attended, groups):
    per = weight.shape[0] // groups
    shape = jax.ShapeDtypeStruct((attended.shape[0], per * weight.shape[2]), BF16)
    return pl.pallas_call(
        project_kernel,
        out_shape=[shape] * groups,
        in_specs=[SMEM, HBM, HBM],
        out_specs=[VMEM] * groups,
        scratch_shapes=[
            pltpu.VMEM((groups, per, *weight.shape[1:]), BF16),
            pltpu.VMEM(attended.shape, BF16),
            pltpu.SemaphoreType.DMA((groups,)),
            pltpu.SemaphoreType.DMA,
        ],
        compiler_params=PARAMS,
        cost_estimate=cost(2 * 2**30, 8 * 2**20),
        name="projection",
    )(spot, in_hbm(weight), in_hbm(attended))


def combine_kernel(asked, own_rows_hbm, back, key_grads_hbm, value_grads_hbm, own_rows, total, grads, in_sem, out_sem):
    rows = own_rows.shape[2]
    arriving = [pltpu.make_async_copy(own_rows_hbm.at[i], own_rows.at[i], in_sem.at[i]) for i in range(2)]
    for copy in arriving:
        copy.start()

    @pl.loop(0, total.shape[1])
    def _(block):
        total[:, block] = jnp.zeros_like(total[:, block])

    @pl.loop(0, back.shape[0])
    def _(slot):
        spot = asked[slot, 0]

        @pl.when(spot >= 0)
        def _():
            total[0, spot] += back[slot, :rows, :].astype(F32)
            total[1, spot] += back[slot, rows:, :].astype(F32)

    outgoing = []
    for i, target in enumerate((key_grads_hbm, value_grads_hbm)):
        arriving[i].wait()

        @pl.loop(0, total.shape[1])
        def _(block, i=i):
            grads[i, block] = (own_rows[i, block] + total[i, block]).astype(BF16)

        outgoing.append(pltpu.make_async_copy(grads.at[i], target, out_sem.at[i]))
        outgoing[i].start()
    for copy in outgoing:
        copy.wait()


def combined(asked, own_rows, back):
    shape = pltpu.HBM(own_rows.shape[1:], BF16)
    return pl.pallas_call(
        combine_kernel,
        out_shape=[shape, shape],
        in_specs=[SMEM, HBM, VMEM],
        out_specs=[HBM, HBM],
        scratch_shapes=[
            pltpu.VMEM(own_rows.shape, BF16),
            pltpu.VMEM(own_rows.shape, F32),
            pltpu.VMEM(own_rows.shape, BF16),
            pltpu.SemaphoreType.DMA((2,)),
            pltpu.SemaphoreType.DMA((2,)),
        ],
        compiler_params=PARAMS,
        cost_estimate=cost(0, 4 * 2**20),
        name="combine",
    )(asked, in_hbm(own_rows), back)


def on_device(sent_queries, mem_keys, mem_values, out_weight, sent_grads, counts, neg_ids):
    keys, values = mem_keys[0], mem_values[0]
    mem_count = keys.shape[0]
    groups = lax.axis_size("dp")
    tensor = lax.axis_size("tensor")
    tensor_spot = lax.axis_index("tensor").astype(jnp.int32).reshape(1)

    holder = neg_ids // mem_count
    spot = neg_ids[None] - mem_count * jnp.arange(groups, dtype=jnp.int32)[:, None, None]
    request = jnp.max(jnp.where((spot >= 0) & (spot < mem_count), spot, -1), axis=(1, 2))
    asked = exchanged(request.reshape(groups, 1))

    queries = passed_along(sent_queries, "section", 1)[0]
    grads = passed_along(sent_grads, "section", -1)[0]
    docs, query_count, features = queries.shape
    weight = lax.all_gather(out_weight[0], "dp")

    recv = exchanged(picked_slots(asked, keys, values))

    grad_rows = grads.reshape(docs * query_count, grads.shape[2])
    held = [grad_rows] + [passed_along(grad_rows, "tensor", -j) for j in range(1, tensor)]
    attended, query_grads, own_rows, slots = layer(
        counts, holder, tensor_spot, queries, keys, values, recv, weight, held
    )
    back = exchanged(slots)
    terms = projected(tensor_spot, weight, attended, tensor)
    arrived = [terms[0]] + [passed_along(terms[j], "tensor", j) for j in range(1, tensor)]
    mixed = sum(term.astype(F32) for term in arrived).astype(BF16).reshape(1, docs, query_count, -1)

    key_grads, value_grads = combined(asked, own_rows, back)
    return mixed, query_grads[None], key_grads[None], value_grads[None]


def solution(mesh):
    rows = P("section", "dp", None, "tensor")
    return jax.shard_map(
        on_device,
        mesh=mesh,
        in_specs=(rows, rows, rows, P("section", "tensor", "dp"), rows, P("dp"), P("dp", None)),
        out_specs=(rows, rows, rows, rows),
        check_vma=False,
    )
```

```python
import jax
import jax.numpy as jnp
from jax import lax
from jax.experimental import pallas as pl
from jax.experimental.pallas import tpu as pltpu
from jax.sharding import PartitionSpec as P

HD = 128
F32 = jnp.float32
BF16 = jnp.bfloat16
NT = (((1,), (1,)), ((), ()))
TN = (((0,), (0,)), ((), ()))
VMEM = pl.BlockSpec(memory_space=pltpu.VMEM)
HBM = pl.BlockSpec(memory_space=pltpu.HBM)
ANY = pl.BlockSpec(memory_space=pl.ANY)
SMEM = pl.BlockSpec(memory_space=pltpu.SMEM)
PARAMS = pltpu.CompilerParams(vmem_limit_bytes=16 * 1024 * 1024)


def passed_along(block, axis, distance):
    count = lax.axis_size(axis)
    return lax.ppermute(block, axis, [(i, (i + distance) % count) for i in range(count)])


def exchanged(slots):
    return lax.all_to_all(slots, "dp", split_axis=0, concat_axis=0, tiled=True)


def in_hbm(array):
    return pltpu.with_memory_space_constraint(array, pltpu.HBM)


def cost(flops, nbytes):
    return pl.CostEstimate(flops=int(flops), bytes_accessed=int(nbytes), transcendentals=0)


def pick_kernel(asked, keys_hbm, values_hbm, slots, sem):
    rows = keys_hbm.shape[1]
    copies = []
    for slot in range(slots.shape[0]):
        spot = asked[slot, 0]
        for which, source in enumerate((keys_hbm, values_hbm)):
            target = slots.at[slot, pl.ds(which * rows, rows)]
            copy = pltpu.make_async_copy(source.at[jnp.maximum(spot, 0)], target, sem.at[slot, which])
            pl.when(spot >= 0)(copy.start)
            copies.append((spot, copy))
    for spot, copy in copies:
        pl.when(spot >= 0)(copy.wait)


def picked_slots(asked, keys, values):
    slot_count = asked.shape[0]
    _, rows, features = keys.shape
    return pl.pallas_call(
        pick_kernel,
        out_shape=pltpu.VMEM((slot_count, 2 * rows, features), BF16),
        in_specs=[SMEM, HBM, HBM],
        out_specs=VMEM,
        scratch_shapes=[pltpu.SemaphoreType.DMA((slot_count, 2))],
        compiler_params=PARAMS,
        cost_estimate=cost(0, 2 * 2**20),
        name="pick_blocks",
    )(asked, in_hbm(keys), in_hbm(values))


def layer_kernel(
    counts, holder, spot, queries, keys, values, recv, weight_hbm, grad0, grad1, grad2, grad3,
    attended_hbm, grad_query_hbm, own_rows_hbm, slots_hbm,
    weight, held, grads, probs, attended, grad_query, own_rows, slots, weight_sem, held_sem, out_sem, own_sem, slot_sem,
):
    docs, query_count, _ = queries.shape
    mem_count, rows, features = keys.shape
    own = mem_count // docs
    neg = holder.shape[1]
    groups, per, _, block = weight.shape
    heads = features // HD
    scale = HD**-0.5

    arriving = []
    for j, grad in enumerate((grad0, grad1, grad2, grad3)):
        first = lax.rem(spot[0] + j, groups) * per
        in_weight = pltpu.make_async_copy(weight_hbm.at[pl.ds(first, per)], weight.at[j], weight_sem.at[j])
        in_held = pltpu.make_async_copy(grad, held.at[j], held_sem.at[j])
        in_held.start()
        in_weight.start()
        arriving.append((in_held, in_weight))

    def place(step):
        doc, head = step // heads, lax.rem(step, heads)
        at = pl.ds(pl.multiple_of(head * HD, HD), HD)
        query_rows = pl.ds(pl.multiple_of(doc * query_count, query_count), query_count)
        senders = [holder[doc, m] for m in range(neg)]
        key = jnp.concatenate(
            [keys[doc * own + m, :, at] for m in range(own)] + [recv[e, :rows, at] for e in senders], axis=0
        )
        value = jnp.concatenate(
            [values[doc * own + m, :, at] for m in range(own)] + [recv[e, rows:, at] for e in senders], axis=0
        )
        return doc, at, query_rows, key, value

    position = lax.broadcasted_iota(jnp.int32, (own * rows, 1), 0)

    @pl.loop(0, docs * heads, unroll=4)
    def _(step):
        doc, at, query_rows, key, value = place(step)
        valid = position < counts[doc] * rows
        scores = lax.dot_general(key, queries[doc, :, at], NT, preferred_element_type=F32) * scale
        scores = jnp.concatenate([jnp.where(valid, scores[: own * rows], -jnp.inf), scores[own * rows :]], axis=0)
        expo = jnp.exp(scores - jnp.max(scores, axis=0, keepdims=True))
        prob = expo * (1.0 / jnp.sum(expo, axis=0, keepdims=True))
        probs[step] = prob
        attended[query_rows, at] = lax.dot_general(prob.astype(BF16), value, TN, preferred_element_type=F32).astype(BF16)

    out_attended = pltpu.make_async_copy(attended, attended_hbm, out_sem.at[0])
    out_attended.start()

    for j, copies in enumerate(arriving):
        for copy in copies:
            copy.wait()
        term = None
        for c in range(per):
            part = lax.dot_general(
                held[j, :, c * block : (c + 1) * block], weight[j, c], NT, preferred_element_type=F32
            )
            term = part if term is None else term + part
        grad_rows = term if j == 0 else grad_rows + term
    grads[...] = grad_rows.astype(BF16)

    @pl.loop(0, docs * heads, unroll=8)
    def _(step):
        doc, at, query_rows, key, value = place(step)
        grad = grads[query_rows, at]
        prob = probs[step]
        grad_prob = lax.dot_general(value, grad, NT, preferred_element_type=F32)
        delta = jnp.sum(prob * grad_prob, axis=0, keepdims=True)
        grad_score = (prob * (grad_prob - delta)).astype(BF16)
        grad_value = jnp.dot(prob.astype(BF16), grad, preferred_element_type=F32)
        grad_key = jnp.dot(grad_score, queries[doc, :, at], preferred_element_type=F32) * scale
        grad_query[doc, :, at] = (lax.dot_general(grad_score, key, TN, preferred_element_type=F32) * scale).astype(BF16)
        for m in range(own):
            here = slice(m * rows, (m + 1) * rows)
            own_rows[0, doc * own + m, :, at] = grad_key[here].astype(BF16)
            own_rows[1, doc * own + m, :, at] = grad_value[here].astype(BF16)
        for m in range(neg):
            here = slice((own + m) * rows, (own + m + 1) * rows)
            slots[doc * neg + m, :rows, at] = grad_key[here].astype(BF16)
            slots[doc * neg + m, rows:, at] = grad_value[here].astype(BF16)

        @pl.when(lax.rem(step, heads) == heads - 1)
        def _():
            for m in range(neg):
                entry = doc * neg + m
                pltpu.make_async_copy(slots.at[entry], slots_hbm.at[holder[doc, m]], slot_sem.at[entry]).start()
            span = pl.ds(doc * own, own)
            pltpu.make_async_copy(own_rows.at[:, span], own_rows_hbm.at[:, span], own_sem.at[doc]).start()

    out_query = pltpu.make_async_copy(grad_query, grad_query_hbm, out_sem.at[1])
    out_query.start()
    for doc in range(docs):
        for m in range(neg):
            entry = doc * neg + m
            pltpu.make_async_copy(slots.at[entry], slots_hbm.at[holder[doc, m]], slot_sem.at[entry]).wait()
        span = pl.ds(doc * own, own)
        pltpu.make_async_copy(own_rows.at[:, span], own_rows_hbm.at[:, span], own_sem.at[doc]).wait()
    out_attended.wait()
    out_query.wait()


def layer(counts, holder, spot, queries, keys, values, recv, weight, held):
    docs, query_count, features = queries.shape
    entries, groups = holder.shape[0] * holder.shape[1], len(held)
    rows, columns = held[0].shape
    dma = pltpu.SemaphoreType.DMA
    return pl.pallas_call(
        layer_kernel,
        out_shape=[
            pltpu.HBM((rows, features), BF16),
            pltpu.HBM(queries.shape, BF16),
            pltpu.HBM((2, *keys.shape), BF16),
            pltpu.HBM(recv.shape, BF16),
        ],
        in_specs=[SMEM] * 3 + [VMEM] * 4 + [HBM] * (1 + groups),
        out_specs=[HBM] * 4,
        scratch_shapes=[
            pltpu.VMEM((groups, weight.shape[0] // groups, *weight.shape[1:]), BF16),
            pltpu.VMEM((groups, rows, columns), BF16),
            pltpu.VMEM((rows, features), BF16),
            pltpu.VMEM((docs * features // HD, (keys.shape[0] // docs + holder.shape[1]) * keys.shape[1], query_count), F32),
            pltpu.VMEM((rows, features), BF16),
            pltpu.VMEM(queries.shape, BF16),
            pltpu.VMEM((2, *keys.shape), BF16),
            pltpu.VMEM((entries, *recv.shape[1:]), BF16),
            dma((groups,)),
            dma((groups,)),
            dma((2,)),
            dma((docs,)),
            dma((entries,)),
        ],
        compiler_params=PARAMS,
        cost_estimate=cost(5 * 2**30, 16 * 2**20),
        name="layer",
    )(counts, holder, spot, queries, keys, values, recv, in_hbm(weight), *map(in_hbm, held))


def project_kernel(spot, weight_hbm, attended_hbm, out0, out1, out2, out3, weight, attended, sem, in_sem):
    groups, per, _, block = weight.shape
    outs = (out0, out1, out2, out3)
    in_attended = pltpu.make_async_copy(attended_hbm, attended, in_sem)
    in_attended.start()
    copies = []
    for j in range(groups):
        first = lax.rem(spot[0] + j, groups) * per
        copies.append(pltpu.make_async_copy(weight_hbm.at[pl.ds(first, per)], weight.at[j], sem.at[j]))
        copies[j].start()
    in_attended.wait()
    for j, out in enumerate(outs):
        copies[j].wait()
        for c in range(per):
            term = jnp.dot(attended[...], weight[j, c], preferred_element_type=F32)
            out[:, c * block : (c + 1) * block] = term.astype(BF16)


def projected(spot, weight, attended, groups):
    per = weight.shape[0] // groups
    shape = jax.ShapeDtypeStruct((attended.shape[0], per * weight.shape[2]), BF16)
    return pl.pallas_call(
        project_kernel,
        out_shape=[shape] * groups,
        in_specs=[SMEM, HBM, HBM],
        out_specs=[VMEM] * groups,
        scratch_shapes=[
            pltpu.VMEM((groups, per, *weight.shape[1:]), BF16),
            pltpu.VMEM(attended.shape, BF16),
            pltpu.SemaphoreType.DMA((groups,)),
            pltpu.SemaphoreType.DMA,
        ],
        compiler_params=PARAMS,
        cost_estimate=cost(2 * 2**30, 8 * 2**20),
        name="projection",
    )(spot, in_hbm(weight), in_hbm(attended))


def combine_kernel(asked, own_rows, back, key_grads_hbm, value_grads_hbm, total, grads, out_sem):
    rows = own_rows.shape[2]

    @pl.loop(0, total.shape[1])
    def _(block):
        total[:, block] = jnp.zeros_like(total[:, block])

    @pl.loop(0, back.shape[0])
    def _(slot):
        spot = asked[slot, 0]

        @pl.when(spot >= 0)
        def _():
            total[0, spot] += back[slot, :rows, :].astype(F32)
            total[1, spot] += back[slot, rows:, :].astype(F32)

    outgoing = []
    for i, target in enumerate((key_grads_hbm, value_grads_hbm)):

        @pl.loop(0, total.shape[1])
        def _(block, i=i):
            grads[i, block] = (own_rows[i, block] + total[i, block]).astype(BF16)

        outgoing.append(pltpu.make_async_copy(grads.at[i], target, out_sem.at[i]))
        outgoing[i].start()
    for copy in outgoing:
        copy.wait()


def combined(asked, own_rows, back):
    shape = pltpu.HBM(own_rows.shape[1:], BF16)
    return pl.pallas_call(
        combine_kernel,
        out_shape=[shape, shape],
        in_specs=[SMEM, VMEM, VMEM],
        out_specs=[HBM, HBM],
        scratch_shapes=[
            pltpu.VMEM(own_rows.shape, F32),
            pltpu.VMEM(own_rows.shape, BF16),
            pltpu.SemaphoreType.DMA((2,)),
        ],
        compiler_params=PARAMS,
        cost_estimate=cost(0, 4 * 2**20),
        name="combine",
    )(asked, own_rows, back)


def on_device(sent_queries, mem_keys, mem_values, out_weight, sent_grads, counts, neg_ids):
    keys, values = mem_keys[0], mem_values[0]
    mem_count = keys.shape[0]
    groups = lax.axis_size("dp")
    tensor = lax.axis_size("tensor")
    tensor_spot = lax.axis_index("tensor").astype(jnp.int32).reshape(1)

    holder = neg_ids // mem_count
    spot = neg_ids[None] - mem_count * jnp.arange(groups, dtype=jnp.int32)[:, None, None]
    request = jnp.max(jnp.where((spot >= 0) & (spot < mem_count), spot, -1), axis=(1, 2))
    asked = exchanged(request.reshape(groups, 1))

    queries = passed_along(sent_queries, "section", 1)[0]
    grads = passed_along(sent_grads, "section", -1)[0]
    docs, query_count, features = queries.shape
    weight = lax.all_gather(out_weight[0], "dp")

    recv = exchanged(picked_slots(asked, keys, values))

    grad_rows = grads.reshape(docs * query_count, grads.shape[2])
    held = [grad_rows] + [passed_along(grad_rows, "tensor", -j) for j in range(1, tensor)]
    attended, query_grads, own_rows, slots = layer(
        counts, holder, tensor_spot, queries, keys, values, recv, weight, held
    )
    back = exchanged(slots)
    terms = projected(tensor_spot, weight, attended, tensor)
    arrived = [terms[0]] + [passed_along(terms[j], "tensor", j) for j in range(1, tensor)]
    mixed = sum(term.astype(F32) for term in arrived).astype(BF16).reshape(1, docs, query_count, -1)

    key_grads, value_grads = combined(asked, own_rows, back)
    return mixed, query_grads[None], key_grads[None], value_grads[None]


def solution(mesh):
    rows = P("section", "dp", None, "tensor")
    return jax.shard_map(
        on_device,
        mesh=mesh,
        in_specs=(rows, rows, rows, P("section", "tensor", "dp"), rows, P("dp"), P("dp", None)),
        out_specs=(rows, rows, rows, rows),
        check_vma=False,
    )
```

```python
import jax
import jax.numpy as jnp
from jax import lax
from jax.experimental import pallas as pl
from jax.experimental.pallas import tpu as pltpu
from jax.sharding import PartitionSpec as P

HD = 128
F32 = jnp.float32
BF16 = jnp.bfloat16
NT = (((1,), (1,)), ((), ()))
TN = (((0,), (0,)), ((), ()))
VMEM = pl.BlockSpec(memory_space=pltpu.VMEM)
HBM = pl.BlockSpec(memory_space=pltpu.HBM)
ANY = pl.BlockSpec(memory_space=pl.ANY)
SMEM = pl.BlockSpec(memory_space=pltpu.SMEM)
PARAMS = pltpu.CompilerParams(vmem_limit_bytes=16 * 1024 * 1024)


def passed_along(block, axis, distance):
    count = lax.axis_size(axis)
    return lax.ppermute(block, axis, [(i, (i + distance) % count) for i in range(count)])


def exchanged(slots):
    return lax.all_to_all(slots, "dp", split_axis=0, concat_axis=0, tiled=True)


def in_hbm(array):
    return pltpu.with_memory_space_constraint(array, pltpu.HBM)


def cost(flops, nbytes):
    return pl.CostEstimate(flops=int(flops), bytes_accessed=int(nbytes), transcendentals=0)


def pick_kernel(asked, keys_hbm, values_hbm, slots, keys, values, in_sem, out_sem):
    rows = keys.shape[1]
    in_key = pltpu.make_async_copy(keys_hbm, keys, in_sem.at[0])
    in_value = pltpu.make_async_copy(values_hbm, values, in_sem.at[1])
    in_key.start()
    in_value.start()

    def sent(slot, which, source):
        target = slots.at[slot, pl.ds(which * rows, rows)]
        return pltpu.make_async_copy(source.at[jnp.maximum(asked[slot, 0], 0)], target, out_sem.at[slot, which])

    for which, (arriving, source) in enumerate(((in_key, keys), (in_value, values))):
        arriving.wait()

        @pl.loop(0, slots.shape[0])
        def _(slot, which=which, source=source):
            copy = sent(slot, which, source)
            pl.when(asked[slot, 0] >= 0)(copy.start)

    @pl.loop(0, slots.shape[0])
    def _(slot):
        for which, source in enumerate((keys, values)):
            pl.when(asked[slot, 0] >= 0)(sent(slot, which, source).wait)


def picked_slots(asked, keys, values):
    slot_count = asked.shape[0]
    _, rows, features = keys.shape
    return pl.pallas_call(
        pick_kernel,
        out_shape=pltpu.HBM((slot_count, 2 * rows, features), BF16),
        in_specs=[SMEM, HBM, HBM],
        out_specs=HBM,
        scratch_shapes=[
            pltpu.VMEM(keys.shape, BF16),
            pltpu.VMEM(values.shape, BF16),
            pltpu.SemaphoreType.DMA((2,)),
            pltpu.SemaphoreType.DMA((slot_count, 2)),
        ],
        compiler_params=PARAMS,
        cost_estimate=cost(0, 4 * 2**20),
        name="pick_blocks",
    )(asked, in_hbm(keys), in_hbm(values))


def layer_kernel(
    counts, holder, spot, queries, keys, values, recv, weight_hbm, grad0, grad1, grad2, grad3,
    attended_hbm, grad_query_hbm, own_rows_hbm, slots_hbm,
    weight, held, grads, probs, attended, grad_query, own_rows, slots, weight_sem, held_sem, out_sem, own_sem, slot_sem,
):
    docs, query_count, _ = queries.shape
    mem_count, rows, features = keys.shape
    own = mem_count // docs
    neg = holder.shape[1]
    groups, per, _, block = weight.shape
    heads = features // HD
    scale = HD**-0.5

    arriving = []
    for j, grad in enumerate((grad0, grad1, grad2, grad3)):
        first = lax.rem(spot[0] + j, groups) * per
        in_weight = pltpu.make_async_copy(weight_hbm.at[pl.ds(first, per)], weight.at[j], weight_sem.at[j])
        in_held = pltpu.make_async_copy(grad, held.at[j], held_sem.at[j])
        in_held.start()
        in_weight.start()
        arriving.append((in_held, in_weight))

    def place(step):
        doc, head = step // heads, lax.rem(step, heads)
        at = pl.ds(pl.multiple_of(head * HD, HD), HD)
        query_rows = pl.ds(pl.multiple_of(doc * query_count, query_count), query_count)
        senders = [holder[doc, m] for m in range(neg)]
        key = jnp.concatenate(
            [keys[doc * own + m, :, at] for m in range(own)] + [recv[e, :rows, at] for e in senders], axis=0
        )
        value = jnp.concatenate(
            [values[doc * own + m, :, at] for m in range(own)] + [recv[e, rows:, at] for e in senders], axis=0
        )
        return doc, at, query_rows, key, value

    position = lax.broadcasted_iota(jnp.int32, (own * rows, 1), 0)

    @pl.loop(0, docs * heads, unroll=4)
    def _(step):
        doc, at, query_rows, key, value = place(step)
        valid = position < counts[doc] * rows
        scores = lax.dot_general(key, queries[doc, :, at], NT, preferred_element_type=F32) * scale
        scores = jnp.concatenate([jnp.where(valid, scores[: own * rows], -jnp.inf), scores[own * rows :]], axis=0)
        expo = jnp.exp(scores - jnp.max(scores, axis=0, keepdims=True))
        prob = expo * (1.0 / jnp.sum(expo, axis=0, keepdims=True))
        probs[step] = prob
        attended[query_rows, at] = lax.dot_general(prob.astype(BF16), value, TN, preferred_element_type=F32).astype(BF16)

    out_attended = pltpu.make_async_copy(attended, attended_hbm, out_sem.at[0])
    out_attended.start()

    for j, copies in enumerate(arriving):
        for copy in copies:
            copy.wait()
        term = None
        for c in range(per):
            part = lax.dot_general(
                held[j, :, c * block : (c + 1) * block], weight[j, c], NT, preferred_element_type=F32
            )
            term = part if term is None else term + part
        grad_rows = term if j == 0 else grad_rows + term
    grads[...] = grad_rows.astype(BF16)

    @pl.loop(0, docs * heads, unroll=8)
    def _(step):
        doc, at, query_rows, key, value = place(step)
        grad = grads[query_rows, at]
        prob = probs[step]
        grad_prob = lax.dot_general(value, grad, NT, preferred_element_type=F32)
        delta = jnp.sum(prob * grad_prob, axis=0, keepdims=True)
        grad_score = (prob * (grad_prob - delta)).astype(BF16)
        grad_value = jnp.dot(prob.astype(BF16), grad, preferred_element_type=F32)
        grad_key = jnp.dot(grad_score, queries[doc, :, at], preferred_element_type=F32) * scale
        grad_query[doc, :, at] = (lax.dot_general(grad_score, key, TN, preferred_element_type=F32) * scale).astype(BF16)
        for m in range(own):
            here = slice(m * rows, (m + 1) * rows)
            own_rows[0, doc * own + m, :, at] = grad_key[here].astype(BF16)
            own_rows[1, doc * own + m, :, at] = grad_value[here].astype(BF16)
        for m in range(neg):
            here = slice((own + m) * rows, (own + m + 1) * rows)
            slots[doc * neg + m, :rows, at] = grad_key[here].astype(BF16)
            slots[doc * neg + m, rows:, at] = grad_value[here].astype(BF16)

        @pl.when(lax.rem(step, heads) == heads - 1)
        def _():
            for m in range(neg):
                entry = doc * neg + m
                pltpu.make_async_copy(slots.at[entry], slots_hbm.at[holder[doc, m]], slot_sem.at[entry]).start()
            span = pl.ds(doc * own, own)
            pltpu.make_async_copy(own_rows.at[:, span], own_rows_hbm.at[:, span], own_sem.at[doc]).start()

    out_query = pltpu.make_async_copy(grad_query, grad_query_hbm, out_sem.at[1])
    out_query.start()
    for doc in range(docs):
        for m in range(neg):
            entry = doc * neg + m
            pltpu.make_async_copy(slots.at[entry], slots_hbm.at[holder[doc, m]], slot_sem.at[entry]).wait()
        span = pl.ds(doc * own, own)
        pltpu.make_async_copy(own_rows.at[:, span], own_rows_hbm.at[:, span], own_sem.at[doc]).wait()
    out_attended.wait()
    out_query.wait()


def layer(counts, holder, spot, queries, keys, values, recv, weight, held):
    docs, query_count, features = queries.shape
    entries, groups = holder.shape[0] * holder.shape[1], len(held)
    rows, columns = held[0].shape
    dma = pltpu.SemaphoreType.DMA
    return pl.pallas_call(
        layer_kernel,
        out_shape=[
            pltpu.HBM((rows, features), BF16),
            pltpu.HBM(queries.shape, BF16),
            pltpu.HBM((2, *keys.shape), BF16),
            pltpu.HBM(recv.shape, BF16),
        ],
        in_specs=[SMEM] * 3 + [VMEM] * 4 + [HBM] * (1 + groups),
        out_specs=[HBM] * 4,
        scratch_shapes=[
            pltpu.VMEM((groups, weight.shape[0] // groups, *weight.shape[1:]), BF16),
            pltpu.VMEM((groups, rows, columns), BF16),
            pltpu.VMEM((rows, features), BF16),
            pltpu.VMEM((docs * features // HD, (keys.shape[0] // docs + holder.shape[1]) * keys.shape[1], query_count), F32),
            pltpu.VMEM((rows, features), BF16),
            pltpu.VMEM(queries.shape, BF16),
            pltpu.VMEM((2, *keys.shape), BF16),
            pltpu.VMEM((entries, *recv.shape[1:]), BF16),
            dma((groups,)),
            dma((groups,)),
            dma((2,)),
            dma((docs,)),
            dma((entries,)),
        ],
        compiler_params=PARAMS,
        cost_estimate=cost(5 * 2**30, 16 * 2**20),
        name="layer",
    )(counts, holder, spot, queries, keys, values, recv, in_hbm(weight), *map(in_hbm, held))


def project_kernel(spot, weight_hbm, attended_hbm, out0, out1, out2, out3, weight, attended, sem, in_sem):
    groups, per, _, block = weight.shape
    outs = (out0, out1, out2, out3)
    in_attended = pltpu.make_async_copy(attended_hbm, attended, in_sem)
    in_attended.start()
    copies = []
    for j in range(groups):
        first = lax.rem(spot[0] + j, groups) * per
        copies.append(pltpu.make_async_copy(weight_hbm.at[pl.ds(first, per)], weight.at[j], sem.at[j]))
        copies[j].start()
    in_attended.wait()
    for j, out in enumerate(outs):
        copies[j].wait()
        for c in range(per):
            term = jnp.dot(attended[...], weight[j, c], preferred_element_type=F32)
            out[:, c * block : (c + 1) * block] = term.astype(BF16)


def projected(spot, weight, attended, groups):
    per = weight.shape[0] // groups
    shape = jax.ShapeDtypeStruct((attended.shape[0], per * weight.shape[2]), BF16)
    return pl.pallas_call(
        project_kernel,
        out_shape=[shape] * groups,
        in_specs=[SMEM, HBM, HBM],
        out_specs=[VMEM] * groups,
        scratch_shapes=[
            pltpu.VMEM((groups, per, *weight.shape[1:]), BF16),
            pltpu.VMEM(attended.shape, BF16),
            pltpu.SemaphoreType.DMA((groups,)),
            pltpu.SemaphoreType.DMA,
        ],
        compiler_params=PARAMS,
        cost_estimate=cost(2 * 2**30, 8 * 2**20),
        name="projection",
    )(spot, in_hbm(weight), in_hbm(attended))


def combine_kernel(asked, own_rows, back, key_grads_hbm, value_grads_hbm, total, grads, out_sem):
    rows = own_rows.shape[2]

    @pl.loop(0, total.shape[1])
    def _(block):
        total[:, block] = jnp.zeros_like(total[:, block])

    @pl.loop(0, back.shape[0])
    def _(slot):
        spot = asked[slot, 0]

        @pl.when(spot >= 0)
        def _():
            total[0, spot] += back[slot, :rows, :].astype(F32)
            total[1, spot] += back[slot, rows:, :].astype(F32)

    outgoing = []
    for i, target in enumerate((key_grads_hbm, value_grads_hbm)):

        @pl.loop(0, total.shape[1])
        def _(block, i=i):
            grads[i, block] = (own_rows[i, block] + total[i, block]).astype(BF16)

        outgoing.append(pltpu.make_async_copy(grads.at[i], target, out_sem.at[i]))
        outgoing[i].start()
    for copy in outgoing:
        copy.wait()


def combined(asked, own_rows, back):
    shape = pltpu.HBM(own_rows.shape[1:], BF16)
    return pl.pallas_call(
        combine_kernel,
        out_shape=[shape, shape],
        in_specs=[SMEM, VMEM, VMEM],
        out_specs=[HBM, HBM],
        scratch_shapes=[
            pltpu.VMEM(own_rows.shape, F32),
            pltpu.VMEM(own_rows.shape, BF16),
            pltpu.SemaphoreType.DMA((2,)),
        ],
        compiler_params=PARAMS,
        cost_estimate=cost(0, 4 * 2**20),
        name="combine",
    )(asked, own_rows, back)


def on_device(sent_queries, mem_keys, mem_values, out_weight, sent_grads, counts, neg_ids):
    keys, values = mem_keys[0], mem_values[0]
    mem_count = keys.shape[0]
    groups = lax.axis_size("dp")
    tensor = lax.axis_size("tensor")
    tensor_spot = lax.axis_index("tensor").astype(jnp.int32).reshape(1)

    holder = neg_ids // mem_count
    spot = neg_ids[None] - mem_count * jnp.arange(groups, dtype=jnp.int32)[:, None, None]
    request = jnp.max(jnp.where((spot >= 0) & (spot < mem_count), spot, -1), axis=(1, 2))
    asked = exchanged(request.reshape(groups, 1))

    queries = passed_along(sent_queries, "section", 1)[0]
    grads = passed_along(sent_grads, "section", -1)[0]
    docs, query_count, features = queries.shape
    weight = lax.all_gather(out_weight[0], "dp")

    recv = exchanged(picked_slots(asked, keys, values))

    grad_rows = grads.reshape(docs * query_count, grads.shape[2])
    held = [grad_rows] + [passed_along(grad_rows, "tensor", -j) for j in range(1, tensor)]
    attended, query_grads, own_rows, slots = layer(
        counts, holder, tensor_spot, queries, keys, values, recv, weight, held
    )
    back = exchanged(slots)
    terms = projected(tensor_spot, weight, attended, tensor)
    arrived = [terms[0]] + [passed_along(terms[j], "tensor", j) for j in range(1, tensor)]
    mixed = sum(term.astype(F32) for term in arrived).astype(BF16).reshape(1, docs, query_count, -1)

    key_grads, value_grads = combined(asked, own_rows, back)
    return mixed, query_grads[None], key_grads[None], value_grads[None]


def solution(mesh):
    rows = P("section", "dp", None, "tensor")
    return jax.shard_map(
        on_device,
        mesh=mesh,
        in_specs=(rows, rows, rows, P("section", "tensor", "dp"), rows, P("dp"), P("dp", None)),
        out_specs=(rows, rows, rows, rows),
        check_vma=False,
    )
```
